256 devices in a mesh: section: 16 (over z, core), tensor: 8 (over y, x_lo), dp: 2 (over x_hi).
Axes of the slice: x: 4 (x_hi: 2, x_lo: 2; x = x_hi * 2 + x_lo), y: 4, z: 8, core: 2. Of those that a mesh axis runs over, the one named last changes fastest.
Arguments:
- old_master: float32 [12288, 8192], P('section', ('tensor', 'dp')), may hold values from -0.0546875 to 0.0546875
- old_first: float32 [12288, 8192], P('section', ('tensor', 'dp')), may hold values from -0.3 to 0.3
- old_second: float32 [12288, 8192], P('section', ('tensor', 'dp')), may hold values from 0.001 to 0.01
- dest_section: int32 [96], replicated, may hold values from 0 to 15, as said below
- dest_offset: int32 [96], replicated, may hold values from 0 to 7, as said below
- hidden_acts: bfloat16 [2, 1024, 16384], P('dp', None, 'section'), may hold values from -6 to 6
- out_grad: bfloat16 [2, 1024, 8192], P('dp', None, 'tensor'), may hold values from -6 to 6
Outputs:
- proj_out: bfloat16 [2, 1024, 8192], P('dp', 'section', 'tensor')
- hidden_grad: bfloat16 [2, 1024, 16384], P('dp', None, ('section', 'tensor'))
- adam_step: float32 [16384, 8192], P('section', ('tensor', 'dp'))
The draws below stay inside these ranges and needn't reach their ends.
Inputs may be any that keep to these rules, and one draw needn't show every extreme that they name: `dest_section`: no new owner receives more than 8 blocks and some receive exactly 8; one old owner sends at most 1 block to any one new owner; every new owner receives some block. `dest_offset`: the blocks that go to one new owner have distinct slots.
All inputs are finite; a program needn't handle non-finite values.
Results may differ from the reference program's by a relative error of at most 0.0049.
Values may be sent and summed in bfloat16 or wider, within the bound.
A program may use at most 128 MiB of HBM per device.

```python
import math
import jax
import jax.numpy as jnp
from jax import lax

D = 8192
ROWS = 128
BLOCKS = 6
CAP = 1
RCAP = 8
TOK_DEV = 1024
N_SECTION = 16
N_DP = 2


def route_table(key):
    heavy = N_SECTION // 4
    light = N_SECTION - heavy
    order = jax.random.permutation(jax.random.fold_in(key, 11), N_SECTION).astype(jnp.int32)
    start = jax.random.randint(jax.random.fold_in(key, 12), (), 0, light)
    sender = jnp.arange(N_SECTION, dtype=jnp.int32)
    first = jnp.repeat(order[sender % heavy][:, None], CAP, axis=1)
    second = jnp.repeat(order[(sender + 1) % heavy][:, None], CAP, axis=1)
    singles = BLOCKS - 2 * CAP
    picks = (singles * sender[:, None] + jnp.arange(singles, dtype=jnp.int32)[None, :] + start) % light
    others = order[heavy + picks]
    table = jnp.concatenate([first, second, others], axis=1)
    keys = jax.random.split(jax.random.fold_in(key, 13), N_SECTION)
    table = jax.vmap(jax.random.permutation)(keys, table)
    dest = table.reshape(-1).astype(jnp.int32)
    score = jax.random.permutation(jax.random.fold_in(key, 14), N_SECTION * BLOCKS)
    same = dest[:, None] == dest[None, :]
    before = score[None, :] < score[:, None]
    offset = jnp.sum(same & before, axis=1).astype(jnp.int32)
    return (dest, offset)


def draw_dest_section(key, part):
    return route_table(key)[0]


def draw_dest_offset(key, part):
    return route_table(key)[1]


def level_of(rng, dims, cuts, smallest, top_value):
    gain, own = 1.0, jax.random.fold_in(rng, 6)
    for dim, blocks in cuts:
        draws = jnp.exp(jax.random.uniform(jax.random.fold_in(own, dim), (blocks,), jnp.float32, smallest / len(cuts), top_value / len(cuts)))
        gain = gain * jnp.repeat(draws, dims[dim] // blocks).reshape([-1 if axis == dim else 1 for axis in range(len(dims))])
    return gain


def scatter_about(rng, extent, width, most, cuts=(), kind=jnp.bfloat16):
    array = width * jax.random.normal(rng, extent, jnp.float32)
    if cuts:
        array = array * level_of(rng, extent, cuts, -0.22, 0.18)
    return jnp.clip(array, -most, most).astype(kind)


def setup_inputs(seed: int = 0) -> dict:
    streams_of = jax.random.split(jax.random.key(seed), 8)
    old_master = scatter_about(streams_of[0], (N_SECTION * BLOCKS * ROWS, D), (N_SECTION * BLOCKS * ROWS) ** -0.5, 0.0546875, ((0, 16), (1, 16)), jnp.float32)
    old_first = scatter_about(streams_of[1], (N_SECTION * BLOCKS * ROWS, D), 0.05, 0.3, ((0, 16), (1, 16)), jnp.float32)
    old_second = jnp.clip(jnp.exp(math.log(0.01) - 2.30258502 * jax.random.uniform(streams_of[2], (N_SECTION * BLOCKS * ROWS, D), jnp.float32) ** level_of(streams_of[2], (N_SECTION * BLOCKS * ROWS, D), ((0, 16), (1, 16)), -0.2, 0.2)), 0.001, 0.01)
    dest_section = draw_dest_section(jax.random.fold_in(streams_of[7], 71), 0)
    dest_offset = draw_dest_offset(jax.random.fold_in(streams_of[7], 71), 0)
    hidden_acts = scatter_about(streams_of[5], (N_DP, TOK_DEV, N_SECTION * RCAP * ROWS), 1.0, 6.0, ((0, 2), (2, 16)))
    out_grad = scatter_about(streams_of[6], (N_DP, TOK_DEV, D), 1.0, 6.0, ((0, 2), (2, 8)))
    return {"old_master": old_master, "old_first": old_first, "old_second": old_second, "dest_section": dest_section, "dest_offset": dest_offset, "hidden_acts": hidden_acts, "out_grad": out_grad}


CORR_FIRST = 1.0
CORR_SECOND = 0.6323045752

def place_blocks(old, slot):
    count = slot.shape[0]
    cols = old.shape[1]
    pieces = old.reshape(count, ROWS * cols)
    placed = jnp.zeros((N_SECTION * RCAP, ROWS * cols), jnp.float32).at[slot].set(pieces)
    return placed.reshape(N_SECTION, RCAP * ROWS, cols)

def reference(old_master, old_first, old_second, dest_section, dest_offset, hidden_acts, out_grad):
    slot = (dest_section * RCAP + dest_offset).astype(jnp.int32)
    master = place_blocks(old_master, slot)
    first_old = place_blocks(old_first, slot)
    second_old = place_blocks(old_second, slot)
    used = jnp.zeros((N_SECTION * RCAP,), jnp.float32).at[slot].set(1.0)
    used = jnp.repeat(used, ROWS).reshape(N_SECTION, RCAP * ROWS, 1)
    weight = master.reshape(N_SECTION * RCAP * ROWS, D).astype(jnp.bfloat16)
    tokens_all = N_DP * TOK_DEV
    acts = hidden_acts.reshape(tokens_all, N_SECTION * RCAP * ROWS)
    grads_out = out_grad.reshape(tokens_all, D)
    proj_out = jnp.dot(acts, weight, preferred_element_type=jnp.float32).astype(jnp.bfloat16)
    hidden_grad = jnp.dot(grads_out, weight.T, preferred_element_type=jnp.float32).astype(jnp.bfloat16)
    acts_split = acts.reshape(tokens_all, N_SECTION, RCAP * ROWS).transpose(1, 0, 2)

    def section_step(items):
        first_r, second_r, used_r, acts_r = items
        grad = jnp.dot(acts_r.T, grads_out, preferred_element_type=jnp.float32) / float(tokens_all)
        first = 0.9 * first_r + 0.1 * grad
        second = 0.999 * second_r + 0.001 * grad * grad
        return used_r * (first / CORR_FIRST) / (jnp.sqrt(second / CORR_SECOND) + 1e-08)
    step = lax.map(section_step, (first_old, second_old, used, acts_split))
    return (proj_out.reshape(N_DP, TOK_DEV, D), hidden_grad.reshape(N_DP, TOK_DEV, N_SECTION * RCAP * ROWS), step.reshape(N_SECTION * RCAP * ROWS, D))
```

```python
import jax
import jax.numpy as jnp
from jax import lax
from jax.experimental import pallas as pl
from jax.experimental.pallas import tpu as pltpu
from jax.sharding import PartitionSpec as P

ROWS = 128
BLOCKS = 6
RCAP = 8
CORR_SECOND = 0.6323045752
MESH = pl.DeviceIdType.MESH
BF = jnp.bfloat16
F32 = jnp.float32


def plan(dest_ref, off_ref, tab):
    s = lax.axis_index("section")
    for i in range(64):
        tab[i] = 0

    def owner(o, _):
        for b in range(BLOCKS):
            g = o * BLOCKS + b

            @pl.when(dest_ref[g] == s)
            def _():
                k = off_ref[g]
                tab[o] = k
                tab[32 + k] = o
                tab[40 + k] = 1

        return 0

    lax.fori_loop(0, 16, owner, 0)
    for b in range(BLOCKS):
        p = dest_ref[s * BLOCKS + b]
        tab[16 + p] = b
        tab[48 + b] = p


def kernel(
    tab, master, first, second, acts, grads,
    proj_out, hidden_out, step_out,
    strip, blk, mv, gv, fv, sv,
    send1, recv1, aold, wf, gsend, grecv, gown, pk, pown, cp, q, rq,
    hgs, hgr, hb, send3, recv3, send5, hgf, ab, send4, recv4,
    lsem, ss1, rs1, ss2, rs2, xss, xrs, ssq, rsq, ssh, rsh, ss3, rs3, ss5, rs5, ss4, rs4,
):
    ns, nt = 16, 8
    s = lax.axis_index("section")
    t = lax.axis_index("tensor")
    d = lax.axis_index("dp")
    z, c = s // 2, s % 2
    od = 1 - d
    core_peer = (z * 2 + (1 - c), t, d)
    dp_peer = (s, t, od)

    def sec(k):
        return lax.rem(s + k, ns)

    def ten(k):
        return lax.rem(t + k, nt)

    trow = pl.multiple_of(t * 128, 128)
    locals_ = [
        pltpu.make_async_copy(acts.at[pl.ds(trow, 128)], strip, lsem.at[0]),
        pltpu.make_async_copy(master, mv, lsem.at[1]),
        pltpu.make_async_copy(grads, gv, lsem.at[2]),
        pltpu.make_async_copy(first, fv, lsem.at[3]),
        pltpu.make_async_copy(second, sv, lsem.at[4]),
    ]
    for cpy in locals_:
        cpy.start()

    bar = pltpu.get_barrier_semaphore()
    for k in range(1, ns):
        pl.semaphore_signal(bar, inc=1, device_id=(sec(k), t, d), device_id_type=MESH)
    for k in range(1, nt):
        pl.semaphore_signal(bar, inc=1, device_id=(s, ten(k), d), device_id_type=MESH)
    pl.semaphore_signal(bar, inc=1, device_id=dp_peer, device_id_type=MESH)

    slot_of = [tab[o] for o in range(ns)]
    block_for = [tab[16 + p] for p in range(ns)]
    owner_of = [tab[32 + k] for k in range(RCAP)]
    used = [tab[40 + k].astype(F32) for k in range(RCAP)]
    mine = [tab[48 + b] for b in range(BLOCKS)]

    locals_[0].wait()
    for k in range(RCAP):
        blk[k] = strip[:, pl.ds(k * 128, 128)]
    for o in range(ns):
        send1[o] = blk[slot_of[o]]
    locals_[1].wait()
    for b in range(BLOCKS):
        wf[d, pl.ds(b * 128, 128)] = mv[pl.ds(b * 128, 128)].astype(BF)

    pl.semaphore_wait(bar, ns - 1 + nt - 1 + 1)

    def to_sections(src, dst, sends, recvs):
        def copy(p):
            return pltpu.make_async_remote_copy(
                src_ref=src.at[p], dst_ref=dst.at[s],
                send_sem=sends.at[p], recv_sem=recvs.at[s],
                device_id=(p, t, d), device_id_type=MESH)

        def go(k, _):
            copy(sec(k)).start()
            return 0

        def wait_send(k, _):
            copy(sec(k)).wait_send()
            return 0

        def wait_recv(k, _):
            p = sec(k)
            pltpu.make_async_remote_copy(
                src_ref=src.at[p], dst_ref=dst.at[p],
                send_sem=sends.at[p], recv_sem=recvs.at[p],
                device_id=(p, t, d), device_id_type=MESH).wait_recv()
            return 0

        return (
            lambda: lax.fori_loop(1, ns, go, 0),
            lambda: lax.fori_loop(1, ns, wait_send, 0),
            lambda: lax.fori_loop(1, ns, wait_recv, 0),
        )

    go1, ws1, wr1 = to_sections(send1, recv1, ss1, rs1)
    go1()
    wcopy = pltpu.make_async_remote_copy(
        src_ref=wf.at[d], dst_ref=wf.at[d], send_sem=xss.at[0], recv_sem=xrs.at[0],
        device_id=dp_peer, device_id_type=MESH)
    wcopy.start()
    recv1[s] = send1[s]
    wr1()
    for b in range(BLOCKS):
        aold[pl.ds(trow, 128), pl.ds(b * 128, 128)] = recv1[mine[b]]

    def gather(p, q_):
        row = pl.multiple_of(q_ * 128, 128)
        return pltpu.make_async_remote_copy(
            src_ref=aold.at[pl.ds(row, 128)], dst_ref=aold.at[pl.ds(row, 128)],
            send_sem=ss2.at[p], recv_sem=rs2.at[q_],
            device_id=(s, p, d), device_id_type=MESH)

    def go2(k, _):
        gather(ten(k), t).start()
        return 0

    def wr2(k, _):
        p = ten(k)
        gather(p, p).wait_recv()
        return 0

    lax.fori_loop(1, nt, go2, 0)
    locals_[2].wait()
    lax.fori_loop(1, nt, wr2, 0)

    tn = (((0,), (0,)), ((), ()))
    nt_dims = (((1,), (1,)), ((), ()))

    def grad_tile(r, half):
        cols = pl.ds(pl.multiple_of(half * 512, 512), 512)
        return lax.dot_general(
            aold[:, pl.ds(r * 256, 256)], gv[:, cols], tn, preferred_element_type=F32
        ) * (1.0 / 2048.0)

    for r in range(3):
        gsend[pl.ds(r * 256, 256)] = grad_tile(r, od).astype(BF)
    gcopy = pltpu.make_async_remote_copy(
        src_ref=gsend, dst_ref=grecv, send_sem=xss.at[1], recv_sem=xrs.at[1],
        device_id=dp_peer, device_id_type=MESH)
    gcopy.start()

    wcopy.wait_recv()

    def proj_tile(i, _):
        row = pl.multiple_of(i * 128, 128)
        a = aold[pl.ds(row, 128)]
        for h in range(2):
            r = jnp.dot(a, wf[h], preferred_element_type=F32)
            cols = pl.ds(h * 512, 512)
            lo, hi = r[:64], r[64:]
            pk[i, :, cols] = jnp.where(c == 0, hi, lo).astype(BF)
            pown[i, :, cols] = jnp.where(c == 0, lo, hi)
        return 0

    lax.fori_loop(0, nt, proj_tile, 0)
    ccopy = pltpu.make_async_remote_copy(
        src_ref=pk, dst_ref=cp, send_sem=xss.at[2], recv_sem=xrs.at[2],
        device_id=core_peer, device_id_type=MESH)
    ccopy.start()

    def hid(i):
        row = pl.multiple_of(i * 128, 128)
        r = lax.dot_general(gv[pl.ds(row, 128), pl.ds(0, 512)], wf[0], nt_dims, preferred_element_type=F32)
        return r + lax.dot_general(gv[pl.ds(row, 128), pl.ds(512, 512)], wf[1], nt_dims, preferred_element_type=F32)

    def hcopy(p, q_):
        return pltpu.make_async_remote_copy(
            src_ref=hgs.at[p], dst_ref=hgr.at[q_], send_sem=ssh.at[p], recv_sem=rsh.at[q_],
            device_id=(s, p, d), device_id_type=MESH)

    def go_h(k, _):
        p = ten(k)
        hgs[p] = hid(p).astype(BF)
        hcopy(p, t).start()
        return 0

    lax.fori_loop(1, nt, go_h, 0)
    hown = hid(t)
    for b in range(BLOCKS):
        hgr[t, :, pl.ds(b * 128, 128)] = hown[:, b * 128:(b + 1) * 128].astype(BF)

    for r in range(3):
        gown[pl.ds(r * 256, 256)] = grad_tile(r, d)

    ccopy.wait_recv()

    def qcopy(p, q_):
        return pltpu.make_async_remote_copy(
            src_ref=q.at[p], dst_ref=rq.at[q_], send_sem=ssq.at[p], recv_sem=rsq.at[q_],
            device_id=(p * 2 + c, t, d), device_id_type=MESH)

    def go_q(k, _):
        p = lax.rem(z + k, 8)
        q[p] = (pown[p] + cp[p].astype(F32)).astype(BF)
        qcopy(p, z).start()
        return 0

    lax.fori_loop(1, 8, go_q, 0)
    rq[z] = (pown[z] + cp[z].astype(F32)).astype(BF)

    locals_[3].wait()
    locals_[4].wait()
    gcopy.wait_recv()
    for b in range(BLOCKS):
        rows = pl.ds(b * 128, 128)
        g = gown[rows] + grecv[rows].astype(F32)
        f1 = 0.9 * fv[rows] + 0.1 * g
        s1 = 0.999 * sv[rows] + 0.001 * g * g
        ab[b] = (f1 / (jnp.sqrt(s1 / CORR_SECOND) + 1e-08)).astype(BF)
    go4, ws4, wr4 = to_sections(send4, recv4, ss4, rs4)
    for p in range(ns):
        send4[p] = ab[block_for[p]]
    go4()
    recv4[s] = send4[s]

    def wr_h(k, _):
        p = ten(k)
        hcopy(p, p).wait_recv()
        return 0

    lax.fori_loop(1, nt, wr_h, 0)
    for b in range(BLOCKS):
        acc = hgr[0, :, pl.ds(b * 128, 128)].astype(F32)
        for p in range(1, nt):
            acc = acc + hgr[p, :, pl.ds(b * 128, 128)].astype(F32)
        hb[b] = acc.astype(BF)
    for p in range(ns):
        send3[p] = hb[block_for[p]]
    go3, ws3, wr3 = to_sections(send3, recv3, ss3, rs3)
    go3()
    recv3[s] = send3[s]
    wr3()
    for k in range(RCAP):
        send5[k] = (recv3[owner_of[k]].astype(F32) * used[k]).astype(BF)

    def fcopy(p, q_):
        row = pl.multiple_of(q_ * 128, 128)
        return pltpu.make_async_remote_copy(
            src_ref=send5.at[p], dst_ref=hgf.at[pl.ds(row, 128)], send_sem=ss5.at[p], recv_sem=rs5.at[q_],
            device_id=(s, p, d), device_id_type=MESH)

    def go5(k, _):
        fcopy(ten(k), t).start()
        return 0

    def wr5(k, _):
        p = ten(k)
        fcopy(p, p).wait_recv()
        return 0

    lax.fori_loop(1, nt, go5, 0)
    hgf[pl.ds(trow, 128)] = send5[t]

    def wr_q(k, _):
        p = lax.rem(z + k, 8)
        qcopy(p, p).wait_recv()
        return 0

    lax.fori_loop(1, 8, wr_q, 0)
    acc = rq[0].astype(F32)
    for p in range(1, 8):
        acc = acc + rq[p].astype(F32)
    proj_out[...] = acc.astype(BF)

    lax.fori_loop(1, nt, wr5, 0)
    hidden_out[...] = hgf[...]

    wr4()
    for k in range(RCAP):
        step_out[pl.ds(k * 128, 128)] = recv4[owner_of[k]].astype(F32) * used[k]

    ws1()
    ws3()
    ws4()
    wcopy.wait_send()
    gcopy.wait_send()
    ccopy.wait_send()

    def ws_t(k, _):
        p = ten(k)
        gather(p, t).wait_send()
        hcopy(p, t).wait_send()
        fcopy(p, t).wait_send()
        return 0

    lax.fori_loop(1, nt, ws_t, 0)

    def ws_q(k, _):
        qcopy(lax.rem(z + k, 8), z).wait_send()
        return 0

    lax.fori_loop(1, 8, ws_q, 0)


def shards(old_master, old_first, old_second, dest_section, dest_offset, hidden_acts, out_grad):
    any_ = pl.BlockSpec(memory_space=pl.ANY)
    smem = pl.BlockSpec(memory_space=pltpu.SMEM)
    vmem = pl.BlockSpec(memory_space=pltpu.VMEM)
    V = pltpu.VMEM
    dma = pltpu.SemaphoreType.DMA
    tab = pl.pallas_call(
        plan,
        out_shape=jax.ShapeDtypeStruct((64,), jnp.int32),
        in_specs=[smem, smem],
        out_specs=smem,
        name="plan",
    )(dest_section, dest_offset)
    proj, hidden, step = pl.pallas_call(
        kernel,
        out_shape=(
            jax.ShapeDtypeStruct((64, 1024), BF),
            jax.ShapeDtypeStruct((1024, 128), BF),
            jax.ShapeDtypeStruct((1024, 512), F32),
        ),
        in_specs=[smem, any_, any_, any_, any_, any_],
        out_specs=(vmem, vmem, vmem),
        scratch_shapes=[
            V((128, 1024), BF), V((8, 128, 128), BF), V((768, 512), F32), V((1024, 1024), BF), V((768, 512), F32), V((768, 512), F32),
            V((16, 128, 128), BF), V((16, 128, 128), BF), V((1024, 768), BF), V((2, 768, 512), BF),
            V((768, 512), BF), V((768, 512), BF), V((768, 512), F32),
            V((8, 64, 1024), BF), V((8, 64, 1024), F32), V((8, 64, 1024), BF), V((8, 64, 1024), BF), V((8, 64, 1024), BF),
            V((8, 128, 768), BF), V((8, 128, 768), BF), V((6, 128, 128), BF), V((16, 128, 128), BF), V((16, 128, 128), BF),
            V((8, 128, 128), BF), V((1024, 128), BF), V((6, 128, 512), BF), V((16, 128, 512), BF), V((16, 128, 512), BF),
            dma((5,)), dma((16,)), dma((16,)), dma((8,)), dma((8,)), dma((3,)), dma((3,)), dma((8,)), dma((8,)),
            dma((8,)), dma((8,)), dma((16,)), dma((16,)), dma((8,)), dma((8,)), dma((16,)), dma((16,)),
        ],
        compiler_params=pltpu.CompilerParams(
            collective_id=0, has_side_effects=True, vmem_limit_bytes=56 * 2**20),
        name="layer",
    )(tab, old_master, old_first, old_second, hidden_acts[0], out_grad[0])
    return proj[None], hidden[None], step


def solution(mesh):
    placed = (
        P("section", ("tensor", "dp")),
        P("section", ("tensor", "dp")),
        P("section", ("tensor", "dp")),
        P(),
        P(),
        P("dp", None, "section"),
        P("dp", None, "tensor"),
    )
    return jax.shard_map(
        shards,
        mesh=mesh,
        in_specs=placed,
        out_specs=(
            P("dp", "section", "tensor"),
            P("dp", None, ("section", "tensor")),
            P("section", ("tensor", "dp")),
        ),
        check_vma=False,
    )
```

```python
import jax
import jax.numpy as jnp
from jax import lax
from jax.experimental import pallas as pl
from jax.experimental.pallas import tpu as pltpu
from jax.sharding import PartitionSpec as P

ROWS = 128
BLOCKS = 6
RCAP = 8
CORR_SECOND = 0.6323045752
MESH = pl.DeviceIdType.MESH
BF = jnp.bfloat16
F32 = jnp.float32


def plan(dest, off, tab, route):
    s = lax.axis_index("section")
    z = s // 2
    for i in range(128):
        tab[i] = 30 if 80 <= i < 96 else (8 if 64 <= i < 74 else (1 if i == 96 else 0))

    def clear(i, _):
        for j in range(8):
            route[i * 8 + j] = -1
        return 0

    lax.fori_loop(0, 32, clear, 0)

    def owner(o, _):
        for b in range(BLOCKS):
            g = o * BLOCKS + b

            @pl.when(dest[g] == s)
            def _():
                k = off[g]
                tab[o] = k
                tab[32 + k] = o
                tab[40 + k] = 1

        return 0

    lax.fori_loop(0, 16, owner, 0)
    for b in range(BLOCKS):
        p = dest[s * BLOCKS + b]
        tab[16 + p] = b
        tab[48 + b] = p

    def rank(a, _):
        count = jnp.int32(0)
        for i in range(12):
            g = a * 12 + i
            p = dest[g] // 2
            r = jnp.bitwise_and(lax.shift_right_logical(count, p * 4), 15)
            count = count + lax.shift_left(jnp.int32(1), p * 4)
            route[r * 64 + a * 8 + p] = g
        return 0

    lax.fori_loop(0, 8, rank, 0)

    def near(a, p):
        k = jnp.bitwise_and(p - a, 7)
        return (k == 1) | (k == 7)

    def detour(a, p, g):
        best = jnp.int32(-1)
        for k in (4, 3, 5, 2, 6, 1, 7):
            m = jnp.bitwise_and(p + k, 7)
            am, mp = a * 8 + m, m * 8 + p
            last = jnp.where(route[64 + mp] < 0, 1, jnp.where((k == 1 or k == 7) & (route[128 + mp] < 0), 2, 0))
            held = route[am]
            direct = dest[jnp.maximum(held, 0)] // 2 == m
            second = jnp.where(route[64 + am] < 0, 1, jnp.where(near(a, m) & (route[128 + am] < 0), 2, 3))
            move = jnp.where(held < 0, 0, jnp.where(direct, second, 3))
            good = (last > 0) & (move < 3) & (m != a)
            best = jnp.where(good, m * 16 + last * 4 + move, best)

        @pl.when(best >= 0)
        def _():
            m = best // 16
            am = a * 8 + m
            move = jnp.bitwise_and(best, 3)
            last = jnp.bitwise_and(best // 4, 3)

            @pl.when(move > 0)
            def _():
                route[move * 64 + am] = route[am]

            route[am] = g
            route[last * 64 + m * 8 + p] = g

        @pl.when(best < 0)
        def _():
            tab[96] = 0

    def spill(pair, _):
        a, p = pair // 8, jnp.bitwise_and(pair, 7)
        g2, g3 = route[128 + pair], route[192 + pair]

        @pl.when((a != p) & (g2 >= 0) & jnp.logical_not(near(a, p)))
        def _():
            route[128 + pair] = -1
            detour(a, p, g2)

        @pl.when((a != p) & (g3 >= 0))
        def _():
            detour(a, p, g3)

        return 0

    lax.fori_loop(0, 64, spill, 0)

    for m in range(8):
        g = route[z * 8 + m]
        tab[56 + m] = jnp.where((g >= 0) & (z != m), g - 12 * z, 0)
    for j in range(10):
        if j < 8:
            g = route[64 + z * 8 + j]
        else:
            g = route[128 + z * 8 + jnp.bitwise_and(z + (1 if j == 8 else 7), 7)]
        a = jnp.maximum(g, 0) // 12
        from_pool = 8 + g - 12 * z
        tab[64 + j] = jnp.where(g < 0, 8, jnp.where(a == z, from_pool, a))

    def final(g, source, wanted):
        h = jnp.maximum(g, 0)
        p = dest[h]

        @pl.when(wanted & (g >= 0) & (p // 2 == z))
        def _():
            tab[80 + jnp.bitwise_and(p, 1) * 8 + off[h]] = source

    for a in range(8):
        final(route[a * 8 + z], 8 + a, a != z)
        final(route[64 + a * 8 + z], a, a != z)
    final(route[128 + jnp.bitwise_and(z + 7, 7) * 8 + z], 28, True)
    final(route[128 + jnp.bitwise_and(z + 1, 7) * 8 + z], 29, True)
    for l in range(12):
        final(12 * z + l, 16 + l, True)


def padded_kernel(
    tab, master, first, second, acts, grads,
    proj_out, hidden_out, step_out,
    strip, blk, mv, gv, fv, sv,
    send1, recv1, aold, wf, gsend, grecv, gown, pk, pown, cp, q, rq,
    hgs, hgr, hb, send3, recv3, send5, hgf, ab, send4, recv4,
    lsem, ss1, rs1, ss2, rs2, xss, xrs, ssq, rsq, ssh, rsh, ss3, rs3, ss5, rs5, ss4, rs4,
):
    ns, nt = 16, 8
    s = lax.axis_index("section")
    t = lax.axis_index("tensor")
    d = lax.axis_index("dp")
    z, c = s // 2, s % 2
    od = 1 - d
    core_peer = (z * 2 + (1 - c), t, d)
    dp_peer = (s, t, od)

    def sec(k):
        return lax.rem(s + k, ns)

    def ten(k):
        return lax.rem(t + k, nt)

    trow = pl.multiple_of(t * 128, 128)
    locals_ = [
        pltpu.make_async_copy(acts.at[pl.ds(trow, 128)], strip, lsem.at[0]),
        pltpu.make_async_copy(master, mv, lsem.at[1]),
        pltpu.make_async_copy(grads, gv, lsem.at[2]),
        pltpu.make_async_copy(first, fv, lsem.at[3]),
        pltpu.make_async_copy(second, sv, lsem.at[4]),
    ]
    for cpy in locals_:
        cpy.start()

    bar = pltpu.get_barrier_semaphore()
    for k in range(1, ns):
        pl.semaphore_signal(bar, inc=1, device_id=(sec(k), t, d), device_id_type=MESH)
    for k in range(1, nt):
        pl.semaphore_signal(bar, inc=1, device_id=(s, ten(k), d), device_id_type=MESH)
    pl.semaphore_signal(bar, inc=1, device_id=dp_peer, device_id_type=MESH)

    slot_of = [tab[o] for o in range(ns)]
    block_for = [tab[16 + p] for p in range(ns)]
    owner_of = [tab[32 + k] for k in range(RCAP)]
    used = [tab[40 + k].astype(F32) for k in range(RCAP)]
    mine = [tab[48 + b] for b in range(BLOCKS)]

    locals_[0].wait()
    for k in range(RCAP):
        blk[k] = strip[:, pl.ds(k * 128, 128)]
    for o in range(ns):
        send1[o] = blk[slot_of[o]]
    locals_[1].wait()
    for b in range(BLOCKS):
        wf[d, pl.ds(b * 128, 128)] = mv[pl.ds(b * 128, 128)].astype(BF)

    pl.semaphore_wait(bar, ns - 1 + nt - 1 + 1)

    def to_sections(src, dst, sends, recvs):
        def copy(p):
            return pltpu.make_async_remote_copy(
                src_ref=src.at[p], dst_ref=dst.at[s],
                send_sem=sends.at[p], recv_sem=recvs.at[s],
                device_id=(p, t, d), device_id_type=MESH)

        def go(k, _):
            copy(sec(k)).start()
            return 0

        def wait_send(k, _):
            copy(sec(k)).wait_send()
            return 0

        def wait_recv(k, _):
            p = sec(k)
            pltpu.make_async_remote_copy(
                src_ref=src.at[p], dst_ref=dst.at[p],
                send_sem=sends.at[p], recv_sem=recvs.at[p],
                device_id=(p, t, d), device_id_type=MESH).wait_recv()
            return 0

        return (
            lambda: lax.fori_loop(1, ns, go, 0),
            lambda: lax.fori_loop(1, ns, wait_send, 0),
            lambda: lax.fori_loop(1, ns, wait_recv, 0),
        )

    go1, ws1, wr1 = to_sections(send1, recv1, ss1, rs1)
    go1()
    wcopy = pltpu.make_async_remote_copy(
        src_ref=wf.at[d], dst_ref=wf.at[d], send_sem=xss.at[0], recv_sem=xrs.at[0],
        device_id=dp_peer, device_id_type=MESH)
    wcopy.start()
    recv1[s] = send1[s]
    wr1()
    for b in range(BLOCKS):
        aold[pl.ds(trow, 128), pl.ds(b * 128, 128)] = recv1[mine[b]]

    def gather(p, q_):
        row = pl.multiple_of(q_ * 128, 128)
        return pltpu.make_async_remote_copy(
            src_ref=aold.at[pl.ds(row, 128)], dst_ref=aold.at[pl.ds(row, 128)],
            send_sem=ss2.at[p], recv_sem=rs2.at[q_],
            device_id=(s, p, d), device_id_type=MESH)

    def go2(k, _):
        gather(ten(k), t).start()
        return 0

    def wr2(k, _):
        p = ten(k)
        gather(p, p).wait_recv()
        return 0

    lax.fori_loop(1, nt, go2, 0)
    locals_[2].wait()
    lax.fori_loop(1, nt, wr2, 0)

    tn = (((0,), (0,)), ((), ()))
    nt_dims = (((1,), (1,)), ((), ()))

    def grad_tile(r, half):
        cols = pl.ds(pl.multiple_of(half * 512, 512), 512)
        return lax.dot_general(
            aold[:, pl.ds(r * 256, 256)], gv[:, cols], tn, preferred_element_type=F32
        ) * (1.0 / 2048.0)

    for r in range(3):
        gsend[pl.ds(r * 256, 256)] = grad_tile(r, od).astype(BF)
    gcopy = pltpu.make_async_remote_copy(
        src_ref=gsend, dst_ref=grecv, send_sem=xss.at[1], recv_sem=xrs.at[1],
        device_id=dp_peer, device_id_type=MESH)
    gcopy.start()

    wcopy.wait_recv()

    def proj_tile(i, _):
        row = pl.multiple_of(i * 128, 128)
        a = aold[pl.ds(row, 128)]
        for h in range(2):
            r = jnp.dot(a, wf[h], preferred_element_type=F32)
            cols = pl.ds(h * 512, 512)
            lo, hi = r[:64], r[64:]
            pk[i, :, cols] = jnp.where(c == 0, hi, lo).astype(BF)
            pown[i, :, cols] = jnp.where(c == 0, lo, hi)
        return 0

    lax.fori_loop(0, nt, proj_tile, 0)
    ccopy = pltpu.make_async_remote_copy(
        src_ref=pk, dst_ref=cp, send_sem=xss.at[2], recv_sem=xrs.at[2],
        device_id=core_peer, device_id_type=MESH)
    ccopy.start()

    def hid(i):
        row = pl.multiple_of(i * 128, 128)
        r = lax.dot_general(gv[pl.ds(row, 128), pl.ds(0, 512)], wf[0], nt_dims, preferred_element_type=F32)
        return r + lax.dot_general(gv[pl.ds(row, 128), pl.ds(512, 512)], wf[1], nt_dims, preferred_element_type=F32)

    def hcopy(p, q_):
        return pltpu.make_async_remote_copy(
            src_ref=hgs.at[p], dst_ref=hgr.at[q_], send_sem=ssh.at[p], recv_sem=rsh.at[q_],
            device_id=(s, p, d), device_id_type=MESH)

    def go_h(k, _):
        p = ten(k)
        hgs[p] = hid(p).astype(BF)
        hcopy(p, t).start()
        return 0

    lax.fori_loop(1, nt, go_h, 0)
    hown = hid(t)
    for b in range(BLOCKS):
        hgr[t, :, pl.ds(b * 128, 128)] = hown[:, b * 128:(b + 1) * 128].astype(BF)

    for r in range(3):
        gown[pl.ds(r * 256, 256)] = grad_tile(r, d)

    ccopy.wait_recv()

    def qcopy(p, q_):
        return pltpu.make_async_remote_copy(
            src_ref=q.at[p], dst_ref=rq.at[q_], send_sem=ssq.at[p], recv_sem=rsq.at[q_],
            device_id=(p * 2 + c, t, d), device_id_type=MESH)

    def go_q(k, _):
        p = lax.rem(z + k, 8)
        q[p] = (pown[p] + cp[p].astype(F32)).astype(BF)
        qcopy(p, z).start()
        return 0

    lax.fori_loop(1, 8, go_q, 0)
    rq[z] = (pown[z] + cp[z].astype(F32)).astype(BF)

    locals_[3].wait()
    locals_[4].wait()
    gcopy.wait_recv()
    for b in range(BLOCKS):
        rows = pl.ds(b * 128, 128)
        g = gown[rows] + grecv[rows].astype(F32)
        f1 = 0.9 * fv[rows] + 0.1 * g
        s1 = 0.999 * sv[rows] + 0.001 * g * g
        ab[b] = (f1 / (jnp.sqrt(s1 / CORR_SECOND) + 1e-08)).astype(BF)
    go4, ws4, wr4 = to_sections(send4, recv4, ss4, rs4)
    for p in range(ns):
        send4[p] = ab[block_for[p]]
    go4()
    recv4[s] = send4[s]

    def wr_h(k, _):
        p = ten(k)
        hcopy(p, p).wait_recv()
        return 0

    lax.fori_loop(1, nt, wr_h, 0)
    for b in range(BLOCKS):
        acc = hgr[0, :, pl.ds(b * 128, 128)].astype(F32)
        for p in range(1, nt):
            acc = acc + hgr[p, :, pl.ds(b * 128, 128)].astype(F32)
        hb[b] = acc.astype(BF)
    for p in range(ns):
        send3[p] = hb[block_for[p]]
    go3, ws3, wr3 = to_sections(send3, recv3, ss3, rs3)
    go3()
    recv3[s] = send3[s]
    wr3()
    for k in range(RCAP):
        send5[k] = (recv3[owner_of[k]].astype(F32) * used[k]).astype(BF)

    def fcopy(p, q_):
        row = pl.multiple_of(q_ * 128, 128)
        return pltpu.make_async_remote_copy(
            src_ref=send5.at[p], dst_ref=hgf.at[pl.ds(row, 128)], send_sem=ss5.at[p], recv_sem=rs5.at[q_],
            device_id=(s, p, d), device_id_type=MESH)

    def go5(k, _):
        fcopy(ten(k), t).start()
        return 0

    def wr5(k, _):
        p = ten(k)
        fcopy(p, p).wait_recv()
        return 0

    lax.fori_loop(1, nt, go5, 0)
    hgf[pl.ds(trow, 128)] = send5[t]

    def wr_q(k, _):
        p = lax.rem(z + k, 8)
        qcopy(p, p).wait_recv()
        return 0

    lax.fori_loop(1, 8, wr_q, 0)
    acc = rq[0].astype(F32)
    for p in range(1, 8):
        acc = acc + rq[p].astype(F32)
    proj_out[...] = acc.astype(BF)

    lax.fori_loop(1, nt, wr5, 0)
    hidden_out[...] = hgf[...]

    wr4()
    for k in range(RCAP):
        step_out[k] = (recv4[owner_of[k]].astype(F32) * used[k]).astype(BF)

    ws1()
    ws3()
    ws4()
    wcopy.wait_send()
    gcopy.wait_send()
    ccopy.wait_send()

    def ws_t(k, _):
        p = ten(k)
        gather(p, t).wait_send()
        hcopy(p, t).wait_send()
        fcopy(p, t).wait_send()
        return 0

    lax.fori_loop(1, nt, ws_t, 0)

    def ws_q(k, _):
        qcopy(lax.rem(z + k, 8), z).wait_send()
        return 0

    lax.fori_loop(1, 8, ws_q, 0)


def routed_kernel(
    tab, master, first, second, acts, grads,
    proj_out, hidden_out, step_out,
    strip, blk, mv, gv, fv, sv,
    send1, recv1, aold, wf, gq, gsend, grecv, gown, pk, pown, cp, q, rq,
    hgs, hgr, hxs, hxr, hown, send5, hgf,
    ab0, pool0, xa0, fa0, sa0, sb0, xs0, xr0,
    ab1, pool1, xa1, fa1, sa1, sb1, xs1, xr1,
    ab2, pool2, xa2, fa2, sa2, sb2, xs2, xr2,
    lsem, ss1, rs1, ss2, rs2, xss, xrs, ssq, rsq, ssh, rsh, ss5, rs5, rss, rsr,
):
    ns, nt = 16, 8
    s = lax.axis_index("section")
    t = lax.axis_index("tensor")
    d = lax.axis_index("dp")
    z, c = s // 2, s % 2
    y, xl = t // 2, t % 2
    od, oc, tx = 1 - d, 1 - c, y * 2 + (1 - xl)
    core_peer = (z * 2 + oc, t, d)
    dp_peer = (s, t, od)
    x_peer = (s, tx, d)

    def sec(k):
        return lax.rem(s + k, ns)

    def ten(k):
        return lax.rem(t + k, nt)

    def ypeer(k):
        return lax.rem(y + k, 4)

    def chip(k):
        return lax.rem(z + k, 8)

    def remote(src, dst, sends, recvs, device):
        return pltpu.make_async_remote_copy(
            src_ref=src, dst_ref=dst, send_sem=sends, recv_sem=recvs,
            device_id=device, device_id_type=MESH)

    trow = pl.multiple_of(t * 128, 128)
    xrow = pl.multiple_of(tx * 128, 128)
    locals_ = [
        pltpu.make_async_copy(acts.at[pl.ds(trow, 128)], strip, lsem.at[0]),
        pltpu.make_async_copy(master, mv, lsem.at[1]),
        pltpu.make_async_copy(grads, gv, lsem.at[2]),
        pltpu.make_async_copy(first, fv, lsem.at[3]),
        pltpu.make_async_copy(second, sv, lsem.at[4]),
    ]
    for cpy in locals_:
        cpy.start()

    bar = pltpu.get_barrier_semaphore()
    for k in range(1, ns):
        pl.semaphore_signal(bar, inc=1, device_id=(sec(k), t, d), device_id_type=MESH)
    for k in range(1, nt):
        pl.semaphore_signal(bar, inc=1, device_id=(s, ten(k), d), device_id_type=MESH)
    pl.semaphore_signal(bar, inc=1, device_id=dp_peer, device_id_type=MESH)

    locals_[0].wait()
    for k in range(RCAP):
        blk[k] = strip[:, pl.ds(k * 128, 128)]
    for o in range(ns):
        send1[o] = blk[tab[o]]
    locals_[1].wait()
    for b in range(BLOCKS):
        wf[d, pl.ds(b * 128, 128)] = mv[pl.ds(b * 128, 128)].astype(BF)

    pl.semaphore_wait(bar, ns - 1 + nt - 1 + 1)

    def acopy(p, o):
        return remote(send1.at[p], recv1.at[o], ss1.at[p], rs1.at[o], (p, t, d))

    def go1(k, _):
        acopy(sec(k), s).start()
        return 0

    lax.fori_loop(1, ns, go1, 0)
    wcopy = remote(wf.at[d], wf.at[d], xss.at[0], xrs.at[0], dp_peer)
    wcopy.start()
    recv1[s] = send1[s]

    locals_[2].wait()
    for u in range(2):
        for j in range(2):
            src = j * 256 + u * 128
            for h in range(2):
                gq[h, u, :, pl.ds(j * 128, 128)] = gv[:, pl.ds(h * 512 + src, 128)]

    def wr1(k, _):
        p = sec(k)
        acopy(p, p).wait_recv()
        return 0

    lax.fori_loop(1, ns, wr1, 0)
    for b in range(BLOCKS):
        aold[pl.ds(trow, 128), pl.ds(b * 128, 128)] = recv1[tab[48 + b]]

    def piece(i, sends, owner, device):
        rows = aold.at[pl.ds(pl.multiple_of(owner * 128, 128), 128)]
        return remote(rows, rows, ss2.at[sends], rs2.at[owner], device)

    gx = piece(0, 0, t, x_peer)
    gx.start()
    for k in range(1, 4):
        piece(0, k, t, (s, ypeer(k) * 2 + xl, d)).start()
    piece(0, 0, tx, x_peer).wait_recv()
    for k in range(1, 4):
        piece(0, 3 + k, tx, (s, ypeer(k) * 2 + xl, d)).start()

    nt_dims = (((1,), (1,)), ((), ()))
    tn = (((0,), (0,)), ((), ()))
    wcopy.wait_recv()

    def hid(i):
        row = pl.multiple_of(i * 128, 128)
        r = lax.dot_general(gv[pl.ds(row, 128), pl.ds(0, 512)], wf[0], nt_dims, preferred_element_type=F32)
        return r + lax.dot_general(gv[pl.ds(row, 128), pl.ds(512, 512)], wf[1], nt_dims, preferred_element_type=F32)

    def hid_y(k, _):
        i = ypeer(k)
        for x in range(2):
            hgs[i, x] = hid(i * 2 + x).astype(BF)
        return 0

    lax.fori_loop(1, 4, hid_y, 0)
    for x in range(2):
        hown[x] = hid(y * 2 + x)

    for k in range(1, 4):
        piece(0, 0, ypeer(k) * 2 + xl, x_peer).wait_recv()
        piece(0, 0, ypeer(k) * 2 + (1 - xl), x_peer).wait_recv()

    def grad_tile(r, h, u):
        return lax.dot_general(
            aold[:, pl.ds(r * 256, 256)], gq[h, u], tn, preferred_element_type=F32) * (1.0 / 2048.0)

    gcopies = []
    for u in range(2):
        for r in range(3):
            gsend[u, pl.ds(r * 256, 256)] = grad_tile(r, od, u).astype(BF)
        gcopies.append(remote(gsend.at[u], grecv.at[u], xss.at[1 + u], xrs.at[1 + u], dp_peer))
        gcopies[u].start()

    def hcopy(i, o):
        return remote(hgs.at[i], hgr.at[o], ssh.at[i], rsh.at[o], (s, i * 2 + xl, d))

    for k in range(1, 4):
        hcopy(ypeer(k), y).start()

    def proj_tile(i, _):
        a = aold[pl.ds(pl.multiple_of(i * 128, 128), 128)]
        for h in range(2):
            r = jnp.dot(a, wf[h], preferred_element_type=F32)
            cols = pl.ds(h * 512, 512)
            lo, hi = r[:64], r[64:]
            pk[i, :, cols] = jnp.where(c == 0, hi, lo).astype(BF)
            pown[i, :, cols] = jnp.where(c == 0, lo, hi)
        return 0

    lax.fori_loop(0, nt, proj_tile, 0)
    ccopy = remote(pk, cp, xss.at[3], xrs.at[3], core_peer)
    ccopy.start()

    for u in range(2):
        for r in range(3):
            gown[u, pl.ds(r * 256, 256)] = grad_tile(r, d, u)

    ccopy.wait_recv()

    def qcopy(p, o):
        return remote(q.at[p], rq.at[o], ssq.at[p], rsq.at[o], (p * 2 + c, t, d))

    def go_q(k, _):
        p = chip(k)
        q[p] = (pown[p] + cp[p].astype(F32)).astype(BF)
        qcopy(p, z).start()
        return 0

    lax.fori_loop(1, 8, go_q, 0)
    rq[z] = (pown[z] + cp[z].astype(F32)).astype(BF)

    parts = [
        (ab0, pool0, xa0, fa0, sa0, sb0, xs0, xr0),
        (ab1, pool1, xa1, fa1, sa1, sb1, xs1, xr1),
        (ab2, pool2, xa2, fa2, sa2, sb2, xs2, xr2),
    ]

    def swap_copy(u):
        ab_, pool_ = parts[u][:2]
        return remote(ab_.at[oc], pool_.at[pl.ds(c * BLOCKS, BLOCKS)], rss.at[u, 0], rsr.at[u, 0], core_peer)

    def enter(u):
        ab_, pool_ = parts[u][:2]
        swap_copy(u).start()
        for b in range(BLOCKS):
            pool_[c * BLOCKS + b] = ab_[c, b]

    def copy_a(u, p, o):
        return remote(parts[u][4].at[p], parts[u][2].at[o], rss.at[u, 1 + p], rsr.at[u, 1 + o], (p * 2 + c, t, d))

    def copy_b(u, p, o):
        return remote(parts[u][5].at[p], parts[u][3].at[o], rss.at[u, 9 + p], rsr.at[u, 9 + o], (p * 2 + c, t, d))

    def copy_n(u, j):
        p = chip(1 if j == 0 else 7)
        return remote(parts[u][5].at[8 + j], parts[u][3].at[28 + j], rss.at[u, 17 + j], rsr.at[u, 17 + j], (p * 2 + c, t, d))

    order = (4, 3, 5, 2, 6, 1, 7)

    def round_a(u):
        _, pool_, xa_, _, sa_, _, _, _ = parts[u]
        swap_copy(u).wait_recv()
        for k in order:
            m = chip(k)
            sa_[m] = pool_[tab[56 + m]]
            copy_a(u, m, z).start()
        for l in range(12):
            xa_[8 + l] = pool_[l]
        xa_[z] = jnp.zeros(xa_.shape[1:], BF)

    def round_b(u):
        _, pool_, xa_, fa_, _, sb_, _, _ = parts[u]
        for k in order:
            m = chip(k)
            copy_a(u, m, m).wait_recv()
        for k in order:
            m = chip(k)
            sb_[m] = xa_[tab[64 + m]]
            copy_b(u, m, z).start()
        for j in range(2):
            sb_[8 + j] = xa_[tab[72 + j]]
            copy_n(u, j).start()
        for l in range(20):
            fa_[8 + l] = xa_[l]
        fa_[z] = jnp.zeros(fa_.shape[1:], BF)
        fa_[30] = jnp.zeros(fa_.shape[1:], BF)

    def back_copy(u):
        return remote(parts[u][6], parts[u][7], rss.at[u, 19], rsr.at[u, 19], core_peer)

    def arrive(u):
        _, _, _, fa_, _, _, xs_, _ = parts[u]
        for k in order:
            m = chip(k)
            copy_b(u, m, m).wait_recv()
        for j in range(2):
            copy_n(u, j).wait_recv()
        for k in range(RCAP):
            xs_[k] = fa_[tab[80 + oc * 8 + k]]
        back_copy(u).start()

    def drain(u):
        swap_copy(u).wait_send()
        back_copy(u).wait_send()
        for k in order:
            copy_a(u, chip(k), z).wait_send()
            copy_b(u, chip(k), z).wait_send()
        for j in range(2):
            copy_n(u, j).wait_send()

    def adam(u):
        gcopies[u].wait_recv()
        for b in range(BLOCKS):
            rows = pl.ds(b * 128, 128)
            for j in range(2):
                cols = pl.ds(j * 256 + u * 128, 128)
                here = pl.ds(j * 128, 128)
                g = gown[u, rows, here] + grecv[u, rows, here].astype(F32)
                f1 = 0.9 * fv[rows, cols] + 0.1 * g
                s1 = 0.999 * sv[rows, cols] + 0.001 * g * g
                parts[u][0][j, b] = (f1 / (jnp.sqrt(s1 / CORR_SECOND) + 1e-08)).astype(BF)
        enter(u)

    def place(u):
        fa_, xr_ = parts[u][3], parts[u][7]
        back_copy(u).wait_recv()
        mine = pl.ds(pl.multiple_of(c * 256 + u * 128, 128), 128)
        theirs = pl.ds(pl.multiple_of(oc * 256 + u * 128, 128), 128)
        for k in range(RCAP):
            step_out[k, :, mine] = fa_[tab[80 + c * 8 + k]]
            step_out[k, :, theirs] = xr_[k]

    locals_[3].wait()
    locals_[4].wait()
    adam(0)
    round_a(0)
    adam(1)

    for k in range(1, 4):
        p = ypeer(k)
        hcopy(p, p).wait_recv()
    for x in range(2):
        total = hown[x]
        for k in range(1, 4):
            total = total + hgr[ypeer(k), x].astype(F32)
        hown[x] = total
    hxs[...] = hown[1 - xl].astype(BF)
    hx = remote(hxs, hxr, xss.at[4], xrs.at[4], x_peer)
    hx.start()

    round_a(1)
    round_b(0)
    hx.wait_recv()
    hsum = hown[xl] + hxr[...].astype(F32)
    for b in range(BLOCKS):
        piece_ = hsum[:, b * 128:(b + 1) * 128].astype(BF)
        for j in range(2):
            ab2[j, b] = piece_[j * 64:(j + 1) * 64]
    enter(2)
    round_a(2)
    round_b(1)
    round_b(2)
    arrive(0)
    place(0)
    arrive(1)
    arrive(2)

    back_copy(2).wait_recv()
    mine = pl.ds(pl.multiple_of(c * 64, 64), 64)
    theirs = pl.ds(pl.multiple_of(oc * 64, 64), 64)
    for k in range(RCAP):
        send5[k, mine] = fa2[tab[80 + c * 8 + k]]
        send5[k, theirs] = xr2[k]

    def fcopy(p, o):
        rows = pl.ds(pl.multiple_of(o * 128, 128), 128)
        return remote(send5.at[p], hgf.at[rows], ss5.at[p], rs5.at[o], (s, p, d))

    def go5(k, _):
        fcopy(ten(k), t).start()
        return 0

    lax.fori_loop(1, nt, go5, 0)
    hgf[pl.ds(trow, 128)] = send5[t]
    place(1)

    def wr_q(k, _):
        p = chip(k)
        qcopy(p, p).wait_recv()
        return 0

    lax.fori_loop(1, 8, wr_q, 0)
    acc = rq[0].astype(F32)
    for p in range(1, 8):
        acc = acc + rq[p].astype(F32)
    proj_out[...] = acc.astype(BF)

    def wr5(k, _):
        p = ten(k)
        fcopy(p, p).wait_recv()
        return 0

    lax.fori_loop(1, nt, wr5, 0)
    hidden_out[...] = hgf[...]

    for u in range(3):
        drain(u)
    for cpy in (wcopy, gcopies[0], gcopies[1], ccopy, hx, gx):
        cpy.wait_send()
    for k in range(1, 4):
        piece(0, k, t, x_peer).wait_send()
        piece(0, 3 + k, tx, x_peer).wait_send()
        hcopy(ypeer(k), y).wait_send()

    def ws(k, _):
        acopy(sec(k), s).wait_send()
        return 0

    lax.fori_loop(1, ns, ws, 0)

    def ws5(k, _):
        fcopy(ten(k), t).wait_send()
        return 0

    lax.fori_loop(1, nt, ws5, 0)

    def ws_q(k, _):
        qcopy(chip(k), z).wait_send()
        return 0

    lax.fori_loop(1, 8, ws_q, 0)


def finish(proj, hidden, step, proj_out, hidden_out, step_out):
    proj_out[...] = proj[...]
    hidden_out[...] = hidden[...]
    for k in range(RCAP):
        step_out[pl.ds(k * 128, 128)] = step[k].astype(F32)


def shards(old_master, old_first, old_second, dest_section, dest_offset, hidden_acts, out_grad):
    any_ = pl.BlockSpec(memory_space=pl.ANY)
    smem = pl.BlockSpec(memory_space=pltpu.SMEM)
    vmem = pl.BlockSpec(memory_space=pltpu.VMEM)
    V = pltpu.VMEM
    dma = pltpu.SemaphoreType.DMA
    tab = pl.pallas_call(
        plan,
        out_shape=jax.ShapeDtypeStruct((128,), jnp.int32),
        in_specs=[smem, smem],
        out_specs=smem,
        scratch_shapes=[pltpu.SMEM((256,), jnp.int32)],
        name="plan",
    )(dest_section, dest_offset)
    out_shape = (
        jax.ShapeDtypeStruct((64, 1024), BF),
        jax.ShapeDtypeStruct((1024, 128), BF),
        jax.ShapeDtypeStruct((8, 128, 512), BF),
    )

    def call(body, scratch, number, name):
        return pl.pallas_call(
            body,
            out_shape=out_shape,
            in_specs=[smem, any_, any_, any_, any_, any_],
            out_specs=(vmem, vmem, vmem),
            scratch_shapes=scratch,
            compiler_params=pltpu.CompilerParams(
                collective_id=number, has_side_effects=True, vmem_limit_bytes=58 * 2**20),
            name=name,
        )

    padded = call(padded_kernel, [
        V((128, 1024), BF), V((8, 128, 128), BF), V((768, 512), F32), V((1024, 1024), BF), V((768, 512), F32), V((768, 512), F32),
        V((16, 128, 128), BF), V((16, 128, 128), BF), V((1024, 768), BF), V((2, 768, 512), BF),
        V((768, 512), BF), V((768, 512), BF), V((768, 512), F32),
        V((8, 64, 1024), BF), V((8, 64, 1024), F32), V((8, 64, 1024), BF), V((8, 64, 1024), BF), V((8, 64, 1024), BF),
        V((8, 128, 768), BF), V((8, 128, 768), BF), V((6, 128, 128), BF), V((16, 128, 128), BF), V((16, 128, 128), BF),
        V((8, 128, 128), BF), V((1024, 128), BF), V((6, 128, 512), BF), V((16, 128, 512), BF), V((16, 128, 512), BF),
        dma((5,)), dma((16,)), dma((16,)), dma((8,)), dma((8,)), dma((3,)), dma((3,)), dma((8,)), dma((8,)),
        dma((8,)), dma((8,)), dma((16,)), dma((16,)), dma((8,)), dma((8,)), dma((16,)), dma((16,)),
    ], 0, "padded")


    def buffers(rows):
        shapes = ((2, 6), (12,), (20,), (31,), (8,), (10,), (8,), (8,))
        return [V((*n, rows, 128), BF) for n in shapes]

    routed = call(routed_kernel, [
        V((128, 1024), BF), V((8, 128, 128), BF), V((768, 512), F32), V((1024, 1024), BF), V((768, 512), F32), V((768, 512), F32),
        V((16, 128, 128), BF), V((16, 128, 128), BF), V((1024, 768), BF), V((2, 768, 512), BF),
        V((2, 2, 1024, 256), BF), V((2, 768, 256), BF), V((2, 768, 256), BF), V((2, 768, 256), F32),
        V((8, 64, 1024), BF), V((8, 64, 1024), F32), V((8, 64, 1024), BF), V((8, 64, 1024), BF), V((8, 64, 1024), BF),
        V((4, 2, 128, 768), BF), V((4, 2, 128, 768), BF), V((128, 768), BF), V((128, 768), BF), V((2, 128, 768), F32),
        V((8, 128, 128), BF), V((1024, 128), BF),
        *buffers(128), *buffers(128), *buffers(64),
        dma((5,)), dma((16,)), dma((16,)), dma((8,)), dma((8,)), dma((5,)), dma((5,)), dma((8,)), dma((8,)),
        dma((4,)), dma((4,)), dma((8,)), dma((8,)), dma((3, 20)), dma((3, 20)),
    ], 1, "routed")

    args = (tab, old_master, old_first, old_second, hidden_acts[0], out_grad[0])
    proj, hidden, step = lax.cond(tab[96] == 1, routed, padded, *args)
    proj, hidden, step = pl.pallas_call(
        finish,
        out_shape=(
            jax.ShapeDtypeStruct((64, 1024), BF),
            jax.ShapeDtypeStruct((1024, 128), BF),
            jax.ShapeDtypeStruct((1024, 512), F32),
        ),
        in_specs=[vmem] * 3,
        out_specs=(vmem, vmem, vmem),
        compiler_params=pltpu.CompilerParams(vmem_limit_bytes=32 * 2**20),
        name="finish",
    )(proj, hidden, step)
    return proj[None], hidden[None], step


def solution(mesh):
    placed = (
        P("section", ("tensor", "dp")),
        P("section", ("tensor", "dp")),
        P("section", ("tensor", "dp")),
        P(),
        P(),
        P("dp", None, "section"),
        P("dp", None, "tensor"),
    )
    return jax.shard_map(
        shards,
        mesh=mesh,
        in_specs=placed,
        out_specs=(
            P("dp", "section", "tensor"),
            P("dp", None, ("section", "tensor")),
            P("section", ("tensor", "dp")),
        ),
        check_vma=False,
    )
```

```python
import jax
import jax.numpy as jnp
from jax import lax
from jax.experimental import pallas as pl
from jax.experimental.pallas import tpu as pltpu
from jax.sharding import PartitionSpec as P

ROWS = 128
BLOCKS = 6
RCAP = 8
CORR_SECOND = 0.6323045752
MESH = pl.DeviceIdType.MESH
BF = jnp.bfloat16
F32 = jnp.float32


def plan(dest, off, tab, ok, route, late):
    s = lax.axis_index("section")
    z = s // 2
    for i in range(112):
        tab[i] = 30 if 80 <= i < 96 else (8 if 64 <= i < 74 else 0)
    ok[0] = 1

    def clear(i, _):
        for j in range(16):
            route[i * 16 + j] = -1
        return 0

    lax.fori_loop(0, 12, clear, 0)

    def near(a, p):
        k = jnp.bitwise_and(p - a, 7)
        return (k == 1) | (k == 7)

    def rank(a, n):
        count = jnp.int32(0)
        for i in range(12):
            g = a * 12 + i
            o = a * 2 + i // 6
            q = dest[g]
            k = off[g]
            here = q == s
            tab[jnp.where(here, o, 112)] = k
            tab[jnp.where(here, 32 + k, 113)] = o
            tab[jnp.where(here, 40 + k, 114)] = 1
            p = lax.shift_right_logical(q, 1)
            r = jnp.bitwise_and(lax.shift_right_logical(count, p * 4), 15)
            count = count + lax.shift_left(jnp.int32(1), p * 4)
            fits = (r < 2) | ((r == 2) & near(a, p)) | (a == p)
            route[jnp.where(fits & (a != p), r * 64 + a * 8 + p, 192)] = g
            late[n] = g
            n = n + jnp.where(fits, 0, 1)
        return n

    n_late = lax.fori_loop(0, 8, rank, jnp.int32(0))
    for b in range(BLOCKS):
        p = dest[s * BLOCKS + b]
        tab[16 + p] = b
        tab[48 + b] = p

    def detour(i, _):
        g = late[i]
        a, p = g // 12, dest[g] // 2
        best = jnp.int32(-1)
        for k in (4, 3, 5, 2, 6, 1, 7):
            m = jnp.bitwise_and(p + k, 7)
            am, mp = a * 8 + m, m * 8 + p
            last = jnp.where(route[64 + mp] < 0, 1, 0)
            if k in (1, 7):
                last = jnp.where((last == 0) & (route[128 + mp] < 0), 2, last)
            held = route[am]
            direct = lax.shift_right_logical(dest[jnp.maximum(held, 0)], 1) == m
            second = jnp.where(route[64 + am] < 0, 1, jnp.where(near(a, m) & (route[128 + am] < 0), 2, 3))
            move = jnp.where(held < 0, 0, jnp.where(direct, second, 3))
            good = (last > 0) & (move < 3) & (m != a)
            best = jnp.where(good, m * 16 + last * 4 + move, best)

        @pl.when(best >= 0)
        def _():
            m = best // 16
            am = a * 8 + m
            move = jnp.bitwise_and(best, 3)
            last = jnp.bitwise_and(best // 4, 3)
            route[jnp.where(move > 0, move * 64 + am, 192)] = route[am]
            route[am] = g
            route[last * 64 + m * 8 + p] = g

        @pl.when(best < 0)
        def _():
            ok[0] = 0

        return 0

    lax.fori_loop(0, n_late, detour, 0)

    for m in range(8):
        g = route[z * 8 + m]
        tab[56 + m] = jnp.where((g >= 0) & (z != m), g - 12 * z, 0)
    for j in range(10):
        if j < 8:
            g = route[64 + z * 8 + j]
        else:
            g = route[128 + z * 8 + jnp.bitwise_and(z + (1 if j == 8 else 7), 7)]
        a = jnp.maximum(g, 0) // 12
        from_pool = 8 + g - 12 * z
        tab[64 + j] = jnp.where(g < 0, 8, jnp.where(a == z, from_pool, a))

    def final(g, source):
        h = jnp.maximum(g, 0)
        p = dest[h]
        mine = (g >= 0) & (lax.shift_right_logical(p, 1) == z)
        tab[jnp.where(mine, 80 + jnp.bitwise_and(p, 1) * 8 + off[h], 115)] = source

    for a in range(8):
        final(route[a * 8 + z], 8 + a)
        final(route[64 + a * 8 + z], a)
    final(route[128 + jnp.bitwise_and(z + 7, 7) * 8 + z], 28)
    final(route[128 + jnp.bitwise_and(z + 1, 7) * 8 + z], 29)
    for l in range(12):
        final(12 * z + l, 16 + l)


def padded_kernel(
    tab, master, first, second, acts, grads,
    proj_out, hidden_out, step_out,
    strip, blk, mv, gv, fv, sv,
    send1, recv1, aold, wf, gsend, grecv, gown, pk, pown, cp, q, rq,
    hgs, hgr, hb, send3, recv3, send5, hgf, ab, send4, recv4,
    lsem, ss1, rs1, ss2, rs2, xss, xrs, ssq, rsq, ssh, rsh, ss3, rs3, ss5, rs5, ss4, rs4,
):
    ns, nt = 16, 8
    s = lax.axis_index("section")
    t = lax.axis_index("tensor")
    d = lax.axis_index("dp")
    z, c = s // 2, s % 2
    od = 1 - d
    core_peer = (z * 2 + (1 - c), t, d)
    dp_peer = (s, t, od)

    def sec(k):
        return lax.rem(s + k, ns)

    def ten(k):
        return lax.rem(t + k, nt)

    trow = pl.multiple_of(t * 128, 128)
    locals_ = [
        pltpu.make_async_copy(acts.at[pl.ds(trow, 128)], strip, lsem.at[0]),
        pltpu.make_async_copy(master, mv, lsem.at[1]),
        pltpu.make_async_copy(grads, gv, lsem.at[2]),
        pltpu.make_async_copy(first, fv, lsem.at[3]),
        pltpu.make_async_copy(second, sv, lsem.at[4]),
    ]
    for cpy in locals_:
        cpy.start()

    bar = pltpu.get_barrier_semaphore()
    for k in range(1, ns):
        pl.semaphore_signal(bar, inc=1, device_id=(sec(k), t, d), device_id_type=MESH)
    for k in range(1, nt):
        pl.semaphore_signal(bar, inc=1, device_id=(s, ten(k), d), device_id_type=MESH)
    pl.semaphore_signal(bar, inc=1, device_id=dp_peer, device_id_type=MESH)

    slot_of = [tab[o] for o in range(ns)]
    block_for = [tab[16 + p] for p in range(ns)]
    owner_of = [tab[32 + k] for k in range(RCAP)]
    used = [tab[40 + k].astype(F32) for k in range(RCAP)]
    mine = [tab[48 + b] for b in range(BLOCKS)]

    locals_[0].wait()
    for k in range(RCAP):
        blk[k] = strip[:, pl.ds(k * 128, 128)]
    for o in range(ns):
        send1[o] = blk[slot_of[o]]
    locals_[1].wait()
    for b in range(BLOCKS):
        wf[d, pl.ds(b * 128, 128)] = mv[pl.ds(b * 128, 128)].astype(BF)

    pl.semaphore_wait(bar, ns - 1 + nt - 1 + 1)

    def to_sections(src, dst, sends, recvs):
        def copy(p):
            return pltpu.make_async_remote_copy(
                src_ref=src.at[p], dst_ref=dst.at[s],
                send_sem=sends.at[p], recv_sem=recvs.at[s],
                device_id=(p, t, d), device_id_type=MESH)

        def go(k, _):
            copy(sec(k)).start()
            return 0

        def wait_send(k, _):
            copy(sec(k)).wait_send()
            return 0

        def wait_recv(k, _):
            p = sec(k)
            pltpu.make_async_remote_copy(
                src_ref=src.at[p], dst_ref=dst.at[p],
                send_sem=sends.at[p], recv_sem=recvs.at[p],
                device_id=(p, t, d), device_id_type=MESH).wait_recv()
            return 0

        return (
            lambda: lax.fori_loop(1, ns, go, 0),
            lambda: lax.fori_loop(1, ns, wait_send, 0),
            lambda: lax.fori_loop(1, ns, wait_recv, 0),
        )

    go1, ws1, wr1 = to_sections(send1, recv1, ss1, rs1)
    go1()
    wcopy = pltpu.make_async_remote_copy(
        src_ref=wf.at[d], dst_ref=wf.at[d], send_sem=xss.at[0], recv_sem=xrs.at[0],
        device_id=dp_peer, device_id_type=MESH)
    wcopy.start()
    recv1[s] = send1[s]
    wr1()
    for b in range(BLOCKS):
        aold[pl.ds(trow, 128), pl.ds(b * 128, 128)] = recv1[mine[b]]

    def gather(p, q_):
        row = pl.multiple_of(q_ * 128, 128)
        return pltpu.make_async_remote_copy(
            src_ref=aold.at[pl.ds(row, 128)], dst_ref=aold.at[pl.ds(row, 128)],
            send_sem=ss2.at[p], recv_sem=rs2.at[q_],
            device_id=(s, p, d), device_id_type=MESH)

    def go2(k, _):
        gather(ten(k), t).start()
        return 0

    def wr2(k, _):
        p = ten(k)
        gather(p, p).wait_recv()
        return 0

    lax.fori_loop(1, nt, go2, 0)
    locals_[2].wait()
    lax.fori_loop(1, nt, wr2, 0)

    tn = (((0,), (0,)), ((), ()))
    nt_dims = (((1,), (1,)), ((), ()))

    def grad_tile(r, half):
        cols = pl.ds(pl.multiple_of(half * 512, 512), 512)
        return lax.dot_general(
            aold[:, pl.ds(r * 256, 256)], gv[:, cols], tn, preferred_element_type=F32
        ) * (1.0 / 2048.0)

    for r in range(3):
        gsend[pl.ds(r * 256, 256)] = grad_tile(r, od).astype(BF)
    gcopy = pltpu.make_async_remote_copy(
        src_ref=gsend, dst_ref=grecv, send_sem=xss.at[1], recv_sem=xrs.at[1],
        device_id=dp_peer, device_id_type=MESH)
    gcopy.start()

    wcopy.wait_recv()

    def proj_tile(i, _):
        row = pl.multiple_of(i * 128, 128)
        a = aold[pl.ds(row, 128)]
        for h in range(2):
            r = jnp.dot(a, wf[h], preferred_element_type=F32)
            cols = pl.ds(h * 512, 512)
            lo, hi = r[:64], r[64:]
            pk[i, :, cols] = jnp.where(c == 0, hi, lo).astype(BF)
            pown[i, :, cols] = jnp.where(c == 0, lo, hi)
        return 0

    lax.fori_loop(0, nt, proj_tile, 0)
    ccopy = pltpu.make_async_remote_copy(
        src_ref=pk, dst_ref=cp, send_sem=xss.at[2], recv_sem=xrs.at[2],
        device_id=core_peer, device_id_type=MESH)
    ccopy.start()

    def hid(i):
        row = pl.multiple_of(i * 128, 128)
        r = lax.dot_general(gv[pl.ds(row, 128), pl.ds(0, 512)], wf[0], nt_dims, preferred_element_type=F32)
        return r + lax.dot_general(gv[pl.ds(row, 128), pl.ds(512, 512)], wf[1], nt_dims, preferred_element_type=F32)

    def hcopy(p, q_):
        return pltpu.make_async_remote_copy(
            src_ref=hgs.at[p], dst_ref=hgr.at[q_], send_sem=ssh.at[p], recv_sem=rsh.at[q_],
            device_id=(s, p, d), device_id_type=MESH)

    def go_h(k, _):
        p = ten(k)
        hgs[p] = hid(p).astype(BF)
        hcopy(p, t).start()
        return 0

    lax.fori_loop(1, nt, go_h, 0)
    hown = hid(t)
    for b in range(BLOCKS):
        hgr[t, :, pl.ds(b * 128, 128)] = hown[:, b * 128:(b + 1) * 128].astype(BF)

    for r in range(3):
        gown[pl.ds(r * 256, 256)] = grad_tile(r, d)

    ccopy.wait_recv()

    def qcopy(p, q_):
        return pltpu.make_async_remote_copy(
            src_ref=q.at[p], dst_ref=rq.at[q_], send_sem=ssq.at[p], recv_sem=rsq.at[q_],
            device_id=(p * 2 + c, t, d), device_id_type=MESH)

    def go_q(k, _):
        p = lax.rem(z + k, 8)
        q[p] = (pown[p] + cp[p].astype(F32)).astype(BF)
        qcopy(p, z).start()
        return 0

    lax.fori_loop(1, 8, go_q, 0)
    rq[z] = (pown[z] + cp[z].astype(F32)).astype(BF)

    locals_[3].wait()
    locals_[4].wait()
    gcopy.wait_recv()
    for b in range(BLOCKS):
        rows = pl.ds(b * 128, 128)
        g = gown[rows] + grecv[rows].astype(F32)
        f1 = 0.9 * fv[rows] + 0.1 * g
        s1 = 0.999 * sv[rows] + 0.001 * g * g
        ab[b] = (f1 / (jnp.sqrt(s1 / CORR_SECOND) + 1e-08)).astype(BF)
    go4, ws4, wr4 = to_sections(send4, recv4, ss4, rs4)
    for p in range(ns):
        send4[p] = ab[block_for[p]]
    go4()
    recv4[s] = send4[s]

    def wr_h(k, _):
        p = ten(k)
        hcopy(p, p).wait_recv()
        return 0

    lax.fori_loop(1, nt, wr_h, 0)
    for b in range(BLOCKS):
        acc = hgr[0, :, pl.ds(b * 128, 128)].astype(F32)
        for p in range(1, nt):
            acc = acc + hgr[p, :, pl.ds(b * 128, 128)].astype(F32)
        hb[b] = acc.astype(BF)
    for p in range(ns):
        send3[p] = hb[block_for[p]]
    go3, ws3, wr3 = to_sections(send3, recv3, ss3, rs3)
    go3()
    recv3[s] = send3[s]
    wr3()
    for k in range(RCAP):
        send5[k] = (recv3[owner_of[k]].astype(F32) * used[k]).astype(BF)

    def fcopy(p, q_):
        row = pl.multiple_of(q_ * 128, 128)
        return pltpu.make_async_remote_copy(
            src_ref=send5.at[p], dst_ref=hgf.at[pl.ds(row, 128)], send_sem=ss5.at[p], recv_sem=rs5.at[q_],
            device_id=(s, p, d), device_id_type=MESH)

    def go5(k, _):
        fcopy(ten(k), t).start()
        return 0

    def wr5(k, _):
        p = ten(k)
        fcopy(p, p).wait_recv()
        return 0

    lax.fori_loop(1, nt, go5, 0)
    hgf[pl.ds(trow, 128)] = send5[t]

    def wr_q(k, _):
        p = lax.rem(z + k, 8)
        qcopy(p, p).wait_recv()
        return 0

    lax.fori_loop(1, 8, wr_q, 0)
    acc = rq[0].astype(F32)
    for p in range(1, 8):
        acc = acc + rq[p].astype(F32)
    proj_out[...] = acc.astype(BF)

    lax.fori_loop(1, nt, wr5, 0)
    hidden_out[...] = hgf[...]

    wr4()
    for k in range(RCAP):
        step_out[k] = (recv4[owner_of[k]].astype(F32) * used[k]).astype(BF)

    ws1()
    ws3()
    ws4()
    wcopy.wait_send()
    gcopy.wait_send()
    ccopy.wait_send()

    def ws_t(k, _):
        p = ten(k)
        gather(p, t).wait_send()
        hcopy(p, t).wait_send()
        fcopy(p, t).wait_send()
        return 0

    lax.fori_loop(1, nt, ws_t, 0)

    def ws_q(k, _):
        qcopy(lax.rem(z + k, 8), z).wait_send()
        return 0

    lax.fori_loop(1, 8, ws_q, 0)


def routed_kernel(
    tab, master, first, second, acts, grads,
    proj_out, hidden_out, step_out,
    strip, blk, mv, gv, fv, sv,
    send1, recv10, recv11, aold, wf, gq, gsend, grecv, gown, pk, pown, cp, qs, qr,
    hgs, hgr, hxs, hxr, hown, send5, hgf,
    ab0, pool0, xa0, fa0, sa0, sb0, xs0, xr0,
    ab1, pool1, xa1, fa1, sa1, sb1, xs1, xr1,
    ab2, pool2, xa2, fa2, sa2, sb2, xs2, xr2,
    lsem, ss1, rs1, ss2, rs2, xss, xrs, ssq, rsq, ssh, rsh, ss5, rs5, rss, rsr,
):
    ns, nt = 16, 8
    s = lax.axis_index("section")
    t = lax.axis_index("tensor")
    d = lax.axis_index("dp")
    z, c = s // 2, s % 2
    y, xl = t // 2, t % 2
    od, oc, tx = 1 - d, 1 - c, y * 2 + (1 - xl)
    core_peer = (z * 2 + oc, t, d)
    dp_peer = (s, t, od)
    x_peer = (s, tx, d)

    def sec(k):
        return lax.rem(s + k, ns)

    def ten(k):
        return lax.rem(t + k, nt)

    def ypeer(k):
        return lax.rem(y + k, 4)

    def chip(k):
        return lax.rem(z + k, 8)

    def remote(src, dst, sends, recvs, device):
        return pltpu.make_async_remote_copy(
            src_ref=src, dst_ref=dst, send_sem=sends, recv_sem=recvs,
            device_id=device, device_id_type=MESH)

    trow = pl.multiple_of(t * 128, 128)
    xrow = pl.multiple_of(tx * 128, 128)
    locals_ = [
        pltpu.make_async_copy(acts.at[pl.ds(trow, 128)], strip, lsem.at[0]),
        pltpu.make_async_copy(master, mv, lsem.at[1]),
        pltpu.make_async_copy(grads, gv, lsem.at[2]),
        pltpu.make_async_copy(first, fv, lsem.at[3]),
        pltpu.make_async_copy(second, sv, lsem.at[4]),
    ]
    for cpy in locals_:
        cpy.start()

    bar = pltpu.get_barrier_semaphore()
    for k in range(1, ns):
        pl.semaphore_signal(bar, inc=1, device_id=(sec(k), t, d), device_id_type=MESH)
    for k in range(1, nt):
        pl.semaphore_signal(bar, inc=1, device_id=(s, ten(k), d), device_id_type=MESH)
    pl.semaphore_signal(bar, inc=1, device_id=dp_peer, device_id_type=MESH)

    locals_[0].wait()
    for k in range(RCAP):
        blk[k] = strip[:, pl.ds(k * 128, 128)]
    for o in range(ns):
        both = blk[tab[o]]
        for h in range(2):
            send1[h, o] = both[h * 64:(h + 1) * 64]
    locals_[1].wait()
    for b in range(BLOCKS):
        wf[d, pl.ds(b * 128, 128)] = mv[pl.ds(b * 128, 128)].astype(BF)

    pl.semaphore_wait(bar, ns - 1 + nt - 1 + 1)

    recv1 = (recv10, recv11)

    def acopy(h, p, o):
        return remote(send1.at[h, p], recv1[h].at[o], ss1.at[h, p], rs1.at[h, o], (p, t, d))

    def go1(h):
        def go(k, _):
            acopy(h, sec(k), s).start()
            return 0

        lax.fori_loop(1, ns, go, 0)

    def weights(h):
        rows = wf.at[d, pl.ds(h * 384, 384)]
        return remote(rows, rows, xss.at[5 + h], xrs.at[5 + h], dp_peer)

    go1(0)
    weights(0).start()
    go1(1)
    for h in range(2):
        recv1[h][s] = send1[h, s]

    locals_[2].wait()
    for u in range(2):
        for j in range(2):
            src = j * 256 + u * 128
            for h in range(2):
                gq[h, u, :, pl.ds(j * 128, 128)] = gv[:, pl.ds(h * 512 + src, 128)]

    def wr1(h):
        def wait(k, _):
            p = sec(k)
            acopy(h, p, p).wait_recv()
            return 0

        lax.fori_loop(1, ns, wait, 0)

    def piece(h, sends, owner, device):
        rows = aold.at[pl.ds(pl.multiple_of(owner * 128 + h * 64, 64), 64)]
        return remote(rows, rows, ss2.at[h, sends], rs2.at[h, owner], device)

    for h in range(2):
        wr1(h)
        for b in range(BLOCKS):
            aold[pl.ds(pl.multiple_of(t * 128 + h * 64, 64), 64), pl.ds(b * 128, 128)] = recv1[h][tab[48 + b]]
        piece(h, 0, t, x_peer).start()
        for k in range(1, 4):
            piece(h, k, t, (s, ypeer(k) * 2 + xl, d)).start()
    weights(1).start()
    for h in range(2):
        piece(h, 0, tx, x_peer).wait_recv()
        for k in range(1, 4):
            piece(h, 3 + k, tx, (s, ypeer(k) * 2 + xl, d)).start()

    nt_dims = (((1,), (1,)), ((), ()))
    tn = (((0,), (0,)), ((), ()))
    for h in range(2):
        weights(h).wait_recv()

    def hid(i):
        row = pl.multiple_of(i * 128, 128)
        r = lax.dot_general(gv[pl.ds(row, 128), pl.ds(0, 512)], wf[0], nt_dims, preferred_element_type=F32)
        return r + lax.dot_general(gv[pl.ds(row, 128), pl.ds(512, 512)], wf[1], nt_dims, preferred_element_type=F32)

    def hid_y(k, _):
        i = ypeer(k)
        for x in range(2):
            hgs[i, x] = hid(i * 2 + x).astype(BF)
        return 0

    lax.fori_loop(1, 4, hid_y, 0)
    for x in range(2):
        hown[x] = hid(y * 2 + x)

    for k in range(1, 4):
        for h in range(2):
            piece(h, 0, ypeer(k) * 2 + xl, x_peer).wait_recv()
            piece(h, 0, ypeer(k) * 2 + (1 - xl), x_peer).wait_recv()

    def grad_tile(r, h, u):
        return lax.dot_general(
            aold[:, pl.ds(r * 256, 256)], gq[h, u], tn, preferred_element_type=F32) * (1.0 / 2048.0)

    gcopies = []
    for u in range(2):
        for r in range(3):
            gsend[u, pl.ds(r * 256, 256)] = grad_tile(r, od, u).astype(BF)
        gcopies.append(remote(gsend.at[u], grecv.at[u], xss.at[1 + u], xrs.at[1 + u], dp_peer))
        gcopies[u].start()

    def hcopy(i, o):
        return remote(hgs.at[i], hgr.at[o], ssh.at[i], rsh.at[o], (s, i * 2 + xl, d))

    for k in range(1, 4):
        hcopy(ypeer(k), y).start()

    def proj_tile(i, _):
        a = aold[pl.ds(pl.multiple_of(i * 128, 128), 128)]
        for h in range(2):
            r = jnp.dot(a, wf[h], preferred_element_type=F32)
            cols = pl.ds(h * 512, 512)
            lo, hi = r[:64], r[64:]
            pk[i, :, cols] = jnp.where(c == 0, hi, lo).astype(BF)
            pown[i, :, cols] = jnp.where(c == 0, lo, hi)
        return 0

    lax.fori_loop(0, nt, proj_tile, 0)
    ccopy = remote(pk, cp, xss.at[3], xrs.at[3], core_peer)
    ccopy.start()

    for u in range(2):
        for r in range(3):
            gown[u, pl.ds(r * 256, 256)] = grad_tile(r, d, u)

    ccopy.wait_recv()

    lo, hi = pl.ds(0, 32), pl.ds(32, 32)

    def ring(n, way):
        rows = pl.ds(0, 64) if n > 1 else (lo if way == 0 else hi)
        return remote(
            qs.at[way, n - 1, rows], qr.at[way, n - 1, rows], ssq.at[way, n - 1], rsq.at[way, n - 1],
            (chip(1 if way == 0 else 7) * 2 + c, t, d))

    def partial_(p, rows):
        return pown[p, rows] + cp[p, rows].astype(F32)

    def ring_step(n):
        for way in range(2):
            p = chip(5 - n if way == 0 else n + 3)
            first_rows, other_rows = (lo, hi) if way == 0 else (hi, lo)
            if n > 1:
                ring(n - 1, way).wait_recv()
            if n == 1:
                qs[way, 0, first_rows] = partial_(p, first_rows).astype(BF)
            elif n == 2:
                qs[way, 1, first_rows] = (partial_(p, first_rows) + qr[way, 0, first_rows].astype(F32)).astype(BF)
                qs[way, 1, other_rows] = partial_(p, other_rows).astype(BF)
            else:
                qs[way, n - 1] = (partial_(p, pl.ds(0, 64)) + qr[way, n - 2].astype(F32)).astype(BF)
            ring(n, way).start()

    ring_step(1)

    parts = [
        (ab0, pool0, xa0, fa0, sa0, sb0, xs0, xr0),
        (ab1, pool1, xa1, fa1, sa1, sb1, xs1, xr1),
        (ab2, pool2, xa2, fa2, sa2, sb2, xs2, xr2),
    ]

    def swap_copy(u):
        ab_, pool_ = parts[u][:2]
        return remote(ab_.at[oc], pool_.at[pl.ds(c * BLOCKS, BLOCKS)], rss.at[u, 0], rsr.at[u, 0], core_peer)

    def enter(u):
        ab_, pool_ = parts[u][:2]
        swap_copy(u).start()
        for b in range(BLOCKS):
            pool_[c * BLOCKS + b] = ab_[c, b]

    def copy_a(u, p, o):
        return remote(parts[u][4].at[p], parts[u][2].at[o], rss.at[u, 1 + p], rsr.at[u, 1 + o], (p * 2 + c, t, d))

    def copy_b(u, p, o):
        return remote(parts[u][5].at[p], parts[u][3].at[o], rss.at[u, 9 + p], rsr.at[u, 9 + o], (p * 2 + c, t, d))

    def copy_n(u, j):
        p = chip(1 if j == 0 else 7)
        return remote(parts[u][5].at[8 + j], parts[u][3].at[28 + j], rss.at[u, 17 + j], rsr.at[u, 17 + j], (p * 2 + c, t, d))

    order = (4, 3, 5, 2, 6, 1, 7)

    def round_a(u):
        _, pool_, xa_, _, sa_, _, _, _ = parts[u]
        swap_copy(u).wait_recv()
        for k in order:
            m = chip(k)
            sa_[m] = pool_[tab[56 + m]]
            copy_a(u, m, z).start()
        for l in range(12):
            xa_[8 + l] = pool_[l]
        xa_[z] = jnp.zeros(xa_.shape[1:], BF)

    def round_b(u):
        _, pool_, xa_, fa_, _, sb_, _, _ = parts[u]
        for k in order:
            m = chip(k)
            copy_a(u, m, m).wait_recv()
        for k in order:
            m = chip(k)
            sb_[m] = xa_[tab[64 + m]]
            copy_b(u, m, z).start()
        for j in range(2):
            sb_[8 + j] = xa_[tab[72 + j]]
            copy_n(u, j).start()
        for l in range(20):
            fa_[8 + l] = xa_[l]
        fa_[z] = jnp.zeros(fa_.shape[1:], BF)
        fa_[30] = jnp.zeros(fa_.shape[1:], BF)

    def back_copy(u):
        return remote(parts[u][6], parts[u][7], rss.at[u, 19], rsr.at[u, 19], core_peer)

    def arrive(u):
        _, _, _, fa_, _, _, xs_, _ = parts[u]
        for k in order:
            m = chip(k)
            copy_b(u, m, m).wait_recv()
        for j in range(2):
            copy_n(u, j).wait_recv()
        for k in range(RCAP):
            xs_[k] = fa_[tab[80 + oc * 8 + k]]
        back_copy(u).start()

    def drain(u):
        swap_copy(u).wait_send()
        back_copy(u).wait_send()
        for k in order:
            copy_a(u, chip(k), z).wait_send()
            copy_b(u, chip(k), z).wait_send()
        for j in range(2):
            copy_n(u, j).wait_send()

    def adam(u):
        gcopies[u].wait_recv()
        for b in range(BLOCKS):
            rows = pl.ds(b * 128, 128)
            for j in range(2):
                cols = pl.ds(j * 256 + u * 128, 128)
                here = pl.ds(j * 128, 128)
                g = gown[u, rows, here] + grecv[u, rows, here].astype(F32)
                f1 = 0.9 * fv[rows, cols] + 0.1 * g
                s1 = 0.999 * sv[rows, cols] + 0.001 * g * g
                parts[u][0][j, b] = (f1 / (jnp.sqrt(s1 / CORR_SECOND) + 1e-08)).astype(BF)
        enter(u)

    def place(u):
        fa_, xr_ = parts[u][3], parts[u][7]
        back_copy(u).wait_recv()
        mine = pl.ds(pl.multiple_of(c * 256 + u * 128, 128), 128)
        theirs = pl.ds(pl.multiple_of(oc * 256 + u * 128, 128), 128)
        for k in range(RCAP):
            step_out[k, :, mine] = fa_[tab[80 + c * 8 + k]]
            step_out[k, :, theirs] = xr_[k]

    locals_[3].wait()
    locals_[4].wait()
    adam(0)
    ring_step(2)
    round_a(0)
    ring_step(3)
    adam(1)
    ring_step(4)

    for k in range(1, 4):
        p = ypeer(k)
        hcopy(p, p).wait_recv()
    for x in range(2):
        total = hown[x]
        for k in range(1, 4):
            total = total + hgr[ypeer(k), x].astype(F32)
        hown[x] = total
    hxs[...] = hown[1 - xl].astype(BF)
    hx = remote(hxs, hxr, xss.at[4], xrs.at[4], x_peer)
    hx.start()

    round_a(1)
    round_b(0)
    hx.wait_recv()
    hsum = hown[xl] + hxr[...].astype(F32)
    for b in range(BLOCKS):
        piece_ = hsum[:, b * 128:(b + 1) * 128].astype(BF)
        for j in range(2):
            ab2[j, b] = piece_[j * 64:(j + 1) * 64]
    enter(2)
    round_a(2)
    round_b(1)
    round_b(2)
    arrive(0)
    place(0)
    arrive(1)
    arrive(2)

    back_copy(2).wait_recv()
    mine = pl.ds(pl.multiple_of(c * 64, 64), 64)
    theirs = pl.ds(pl.multiple_of(oc * 64, 64), 64)
    for k in range(RCAP):
        send5[k, mine] = fa2[tab[80 + c * 8 + k]]
        send5[k, theirs] = xr2[k]

    def fcopy(p, o):
        rows = pl.ds(pl.multiple_of(o * 128, 128), 128)
        return remote(send5.at[p], hgf.at[rows], ss5.at[p], rs5.at[o], (s, p, d))

    def go5(k, _):
        fcopy(ten(k), t).start()
        return 0

    lax.fori_loop(1, nt, go5, 0)
    hgf[pl.ds(trow, 128)] = send5[t]
    place(1)

    for way in range(2):
        ring(4, way).wait_recv()
    proj_out[...] = (partial_(z, pl.ds(0, 64)) + qr[0, 3].astype(F32) + qr[1, 3].astype(F32)).astype(BF)

    def wr5(k, _):
        p = ten(k)
        fcopy(p, p).wait_recv()
        return 0

    lax.fori_loop(1, nt, wr5, 0)
    hidden_out[...] = hgf[...]

    for u in range(3):
        drain(u)
    for cpy in (gcopies[0], gcopies[1], ccopy, hx):
        cpy.wait_send()
    for h in range(2):
        weights(h).wait_send()
        for i in range(7):
            piece(h, i, t, x_peer).wait_send()

        def ws(k, _):
            acopy(h, sec(k), s).wait_send()
            return 0

        lax.fori_loop(1, ns, ws, 0)
    for k in range(1, 4):
        hcopy(ypeer(k), y).wait_send()
    for n in range(1, 5):
        for way in range(2):
            ring(n, way).wait_send()

    def ws5(k, _):
        fcopy(ten(k), t).wait_send()
        return 0

    lax.fori_loop(1, nt, ws5, 0)


def finish(proj, hidden, step, proj_out, hidden_out, step_out):
    proj_out[...] = proj[...]
    hidden_out[...] = hidden[...]
    for k in range(RCAP):
        step_out[pl.ds(k * 128, 128)] = step[k].astype(F32)


def shards(old_master, old_first, old_second, dest_section, dest_offset, hidden_acts, out_grad):
    any_ = pl.BlockSpec(memory_space=pl.ANY)
    smem = pl.BlockSpec(memory_space=pltpu.SMEM)
    vmem = pl.BlockSpec(memory_space=pltpu.VMEM)
    V = pltpu.VMEM
    dma = pltpu.SemaphoreType.DMA
    tab, ok = pl.pallas_call(
        plan,
        out_shape=(jax.ShapeDtypeStruct((128,), jnp.int32), jax.ShapeDtypeStruct((1,), jnp.int32)),
        in_specs=[smem, smem],
        out_specs=(smem, smem),
        scratch_shapes=[pltpu.SMEM((256,), jnp.int32), pltpu.SMEM((128,), jnp.int32)],
        name="plan",
    )(dest_section, dest_offset)
    out_shape = (
        jax.ShapeDtypeStruct((64, 1024), BF),
        jax.ShapeDtypeStruct((1024, 128), BF),
        jax.ShapeDtypeStruct((8, 128, 512), BF),
    )

    def call(body, scratch, number, name):
        return pl.pallas_call(
            body,
            out_shape=out_shape,
            in_specs=[smem, any_, any_, any_, any_, any_],
            out_specs=(vmem, vmem, vmem),
            scratch_shapes=scratch,
            compiler_params=pltpu.CompilerParams(
                collective_id=number, has_side_effects=True, vmem_limit_bytes=58 * 2**20),
            name=name,
        )

    padded = call(padded_kernel, [
        V((128, 1024), BF), V((8, 128, 128), BF), V((768, 512), F32), V((1024, 1024), BF), V((768, 512), F32), V((768, 512), F32),
        V((16, 128, 128), BF), V((16, 128, 128), BF), V((1024, 768), BF), V((2, 768, 512), BF),
        V((768, 512), BF), V((768, 512), BF), V((768, 512), F32),
        V((8, 64, 1024), BF), V((8, 64, 1024), F32), V((8, 64, 1024), BF), V((8, 64, 1024), BF), V((8, 64, 1024), BF),
        V((8, 128, 768), BF), V((8, 128, 768), BF), V((6, 128, 128), BF), V((16, 128, 128), BF), V((16, 128, 128), BF),
        V((8, 128, 128), BF), V((1024, 128), BF), V((6, 128, 512), BF), V((16, 128, 512), BF), V((16, 128, 512), BF),
        dma((5,)), dma((16,)), dma((16,)), dma((8,)), dma((8,)), dma((3,)), dma((3,)), dma((8,)), dma((8,)),
        dma((8,)), dma((8,)), dma((16,)), dma((16,)), dma((8,)), dma((8,)), dma((16,)), dma((16,)),
    ], 0, "padded")


    def buffers(rows):
        shapes = ((2, 6), (12,), (20,), (31,), (8,), (10,), (8,), (8,))
        return [V((*n, rows, 128), BF) for n in shapes]

    routed = call(routed_kernel, [
        V((128, 1024), BF), V((8, 128, 128), BF), V((768, 512), F32), V((1024, 1024), BF), V((768, 512), F32), V((768, 512), F32),
        V((2, 16, 64, 128), BF), V((16, 64, 128), BF), V((16, 64, 128), BF), V((1024, 768), BF), V((2, 768, 512), BF),
        V((2, 2, 1024, 256), BF), V((2, 768, 256), BF), V((2, 768, 256), BF), V((2, 768, 256), F32),
        V((8, 64, 1024), BF), V((8, 64, 1024), F32), V((8, 64, 1024), BF), V((2, 4, 64, 1024), BF), V((2, 4, 64, 1024), BF),
        V((4, 2, 128, 768), BF), V((4, 2, 128, 768), BF), V((128, 768), BF), V((128, 768), BF), V((2, 128, 768), F32),
        V((8, 128, 128), BF), V((1024, 128), BF),
        *buffers(128), *buffers(128), *buffers(64),
        dma((5,)), dma((2, 16)), dma((2, 16)), dma((2, 8)), dma((2, 8)), dma((7,)), dma((7,)), dma((2, 4)), dma((2, 4)),
        dma((4,)), dma((4,)), dma((8,)), dma((8,)), dma((3, 20)), dma((3, 20)),
    ], 1, "routed")

    args = (tab, old_master, old_first, old_second, hidden_acts[0], out_grad[0])
    proj, hidden, step = lax.cond(ok[0] == 1, routed, padded, *args)
    proj, hidden, step = pl.pallas_call(
        finish,
        out_shape=(
            jax.ShapeDtypeStruct((64, 1024), BF),
            jax.ShapeDtypeStruct((1024, 128), BF),
            jax.ShapeDtypeStruct((1024, 512), F32),
        ),
        in_specs=[vmem] * 3,
        out_specs=(vmem, vmem, vmem),
        compiler_params=pltpu.CompilerParams(vmem_limit_bytes=32 * 2**20),
        name="finish",
    )(proj, hidden, step)
    return proj[None], hidden[None], step


def solution(mesh):
    placed = (
        P("section", ("tensor", "dp")),
        P("section", ("tensor", "dp")),
        P("section", ("tensor", "dp")),
        P(),
        P(),
        P("dp", None, "section"),
        P("dp", None, "tensor"),
    )
    return jax.shard_map(
        shards,
        mesh=mesh,
        in_specs=placed,
        out_specs=(
            P("dp", "section", "tensor"),
            P("dp", None, ("section", "tensor")),
            P("section", ("tensor", "dp")),
        ),
        check_vma=False,
    )
```

```python
import jax
import jax.numpy as jnp
from jax import lax
from jax.experimental import pallas as pl
from jax.experimental.pallas import tpu as pltpu
from jax.sharding import PartitionSpec as P

ROWS = 128
BLOCKS = 6
RCAP = 8
CORR_SECOND = 0.6323045752
MESH = pl.DeviceIdType.MESH
BF = jnp.bfloat16
F32 = jnp.float32


def plan(dest, off, tab, ok, route, late):
    s = lax.axis_index("section")
    z = s // 2
    for i in range(112):
        tab[i] = 30 if 80 <= i < 96 else (8 if 64 <= i < 74 else 0)
    ok[0] = 1

    def clear(i, _):
        for j in range(16):
            route[i * 16 + j] = -1
        return 0

    lax.fori_loop(0, 12, clear, 0)

    def near(a, p):
        k = jnp.bitwise_and(p - a, 7)
        return (k == 1) | (k == 7)

    def rank(a, n):
        count = jnp.int32(0)
        for i in range(12):
            g = a * 12 + i
            o = a * 2 + i // 6
            q = dest[g]
            k = off[g]
            here = q == s
            tab[jnp.where(here, o, 112)] = k
            tab[jnp.where(here, 32 + k, 113)] = o
            tab[jnp.where(here, 40 + k, 114)] = 1
            p = lax.shift_right_logical(q, 1)
            r = jnp.bitwise_and(lax.shift_right_logical(count, p * 4), 15)
            count = count + lax.shift_left(jnp.int32(1), p * 4)
            fits = (r < 2) | ((r == 2) & near(a, p)) | (a == p)
            route[jnp.where(fits & (a != p), r * 64 + a * 8 + p, 192)] = g
            late[n] = g
            n = n + jnp.where(fits, 0, 1)
        return n

    n_late = lax.fori_loop(0, 8, rank, jnp.int32(0))
    for b in range(BLOCKS):
        p = dest[s * BLOCKS + b]
        tab[16 + p] = b
        tab[48 + b] = p

    def detour(i, _):
        g = late[i]
        a, p = g // 12, dest[g] // 2
        best = jnp.int32(-1)
        for k in (4, 3, 5, 2, 6, 1, 7):
            m = jnp.bitwise_and(p + k, 7)
            am, mp = a * 8 + m, m * 8 + p
            last = jnp.where(route[64 + mp] < 0, 1, 0)
            if k in (1, 7):
                last = jnp.where((last == 0) & (route[128 + mp] < 0), 2, last)
            held = route[am]
            direct = lax.shift_right_logical(dest[jnp.maximum(held, 0)], 1) == m
            second = jnp.where(route[64 + am] < 0, 1, jnp.where(near(a, m) & (route[128 + am] < 0), 2, 3))
            move = jnp.where(held < 0, 0, jnp.where(direct, second, 3))
            good = (last > 0) & (move < 3) & (m != a)
            best = jnp.where(good, m * 16 + last * 4 + move, best)

        @pl.when(best >= 0)
        def _():
            m = best // 16
            am = a * 8 + m
            move = jnp.bitwise_and(best, 3)
            last = jnp.bitwise_and(best // 4, 3)
            route[jnp.where(move > 0, move * 64 + am, 192)] = route[am]
            route[am] = g
            route[last * 64 + m * 8 + p] = g

        @pl.when(best < 0)
        def _():
            ok[0] = 0

        return 0

    lax.fori_loop(0, n_late, detour, 0)

    for m in range(8):
        g = route[z * 8 + m]
        tab[56 + m] = jnp.where((g >= 0) & (z != m), g - 12 * z, 0)
    for j in range(10):
        if j < 8:
            g = route[64 + z * 8 + j]
        else:
            g = route[128 + z * 8 + jnp.bitwise_and(z + (1 if j == 8 else 7), 7)]
        a = jnp.maximum(g, 0) // 12
        from_pool = 8 + g - 12 * z
        tab[64 + j] = jnp.where(g < 0, 8, jnp.where(a == z, from_pool, a))

    def final(g, source):
        h = jnp.maximum(g, 0)
        p = dest[h]
        mine = (g >= 0) & (lax.shift_right_logical(p, 1) == z)
        tab[jnp.where(mine, 80 + jnp.bitwise_and(p, 1) * 8 + off[h], 115)] = source

    for a in range(8):
        final(route[a * 8 + z], 8 + a)
        final(route[64 + a * 8 + z], a)
    final(route[128 + jnp.bitwise_and(z + 7, 7) * 8 + z], 28)
    final(route[128 + jnp.bitwise_and(z + 1, 7) * 8 + z], 29)
    for l in range(12):
        final(12 * z + l, 16 + l)


def padded_kernel(
    tab, master, first, second, acts, grads,
    proj_out, hidden_out, step_out,
    strip, blk, mv, gv, fv, sv,
    send1, recv1, aold, wf, gsend, grecv, gown, pk, pown, cp, q, rq,
    hgs, hgr, hb, send3, recv3, send5, hgf, ab, send4, recv4,
    lsem, ss1, rs1, ss2, rs2, xss, xrs, ssq, rsq, ssh, rsh, ss3, rs3, ss5, rs5, ss4, rs4,
):
    ns, nt = 16, 8
    s = lax.axis_index("section")
    t = lax.axis_index("tensor")
    d = lax.axis_index("dp")
    z, c = s // 2, s % 2
    od = 1 - d
    core_peer = (z * 2 + (1 - c), t, d)
    dp_peer = (s, t, od)

    def sec(k):
        return lax.rem(s + k, ns)

    def ten(k):
        return lax.rem(t + k, nt)

    trow = pl.multiple_of(t * 128, 128)
    locals_ = [
        pltpu.make_async_copy(acts.at[pl.ds(trow, 128)], strip, lsem.at[0]),
        pltpu.make_async_copy(master, mv, lsem.at[1]),
        pltpu.make_async_copy(grads, gv, lsem.at[2]),
        pltpu.make_async_copy(first, fv, lsem.at[3]),
        pltpu.make_async_copy(second, sv, lsem.at[4]),
    ]
    for cpy in locals_:
        cpy.start()

    bar = pltpu.get_barrier_semaphore()
    for k in range(1, ns):
        pl.semaphore_signal(bar, inc=1, device_id=(sec(k), t, d), device_id_type=MESH)
    for k in range(1, nt):
        pl.semaphore_signal(bar, inc=1, device_id=(s, ten(k), d), device_id_type=MESH)
    pl.semaphore_signal(bar, inc=1, device_id=dp_peer, device_id_type=MESH)

    slot_of = [tab[o] for o in range(ns)]
    block_for = [tab[16 + p] for p in range(ns)]
    owner_of = [tab[32 + k] for k in range(RCAP)]
    used = [tab[40 + k].astype(F32) for k in range(RCAP)]
    mine = [tab[48 + b] for b in range(BLOCKS)]

    locals_[0].wait()
    for k in range(RCAP):
        blk[k] = strip[:, pl.ds(k * 128, 128)]
    for o in range(ns):
        send1[o] = blk[slot_of[o]]
    locals_[1].wait()
    for b in range(BLOCKS):
        wf[d, pl.ds(b * 128, 128)] = mv[pl.ds(b * 128, 128)].astype(BF)

    pl.semaphore_wait(bar, ns - 1 + nt - 1 + 1)

    def to_sections(src, dst, sends, recvs):
        def copy(p):
            return pltpu.make_async_remote_copy(
                src_ref=src.at[p], dst_ref=dst.at[s],
                send_sem=sends.at[p], recv_sem=recvs.at[s],
                device_id=(p, t, d), device_id_type=MESH)

        def go(k, _):
            copy(sec(k)).start()
            return 0

        def wait_send(k, _):
            copy(sec(k)).wait_send()
            return 0

        def wait_recv(k, _):
            p = sec(k)
            pltpu.make_async_remote_copy(
                src_ref=src.at[p], dst_ref=dst.at[p],
                send_sem=sends.at[p], recv_sem=recvs.at[p],
                device_id=(p, t, d), device_id_type=MESH).wait_recv()
            return 0

        return (
            lambda: lax.fori_loop(1, ns, go, 0),
            lambda: lax.fori_loop(1, ns, wait_send, 0),
            lambda: lax.fori_loop(1, ns, wait_recv, 0),
        )

    go1, ws1, wr1 = to_sections(send1, recv1, ss1, rs1)
    go1()
    wcopy = pltpu.make_async_remote_copy(
        src_ref=wf.at[d], dst_ref=wf.at[d], send_sem=xss.at[0], recv_sem=xrs.at[0],
        device_id=dp_peer, device_id_type=MESH)
    wcopy.start()
    recv1[s] = send1[s]
    wr1()
    for b in range(BLOCKS):
        aold[pl.ds(trow, 128), pl.ds(b * 128, 128)] = recv1[mine[b]]

    def gather(p, q_):
        row = pl.multiple_of(q_ * 128, 128)
        return pltpu.make_async_remote_copy(
            src_ref=aold.at[pl.ds(row, 128)], dst_ref=aold.at[pl.ds(row, 128)],
            send_sem=ss2.at[p], recv_sem=rs2.at[q_],
            device_id=(s, p, d), device_id_type=MESH)

    def go2(k, _):
        gather(ten(k), t).start()
        return 0

    def wr2(k, _):
        p = ten(k)
        gather(p, p).wait_recv()
        return 0

    lax.fori_loop(1, nt, go2, 0)
    locals_[2].wait()
    lax.fori_loop(1, nt, wr2, 0)

    tn = (((0,), (0,)), ((), ()))
    nt_dims = (((1,), (1,)), ((), ()))

    def grad_tile(r, half):
        cols = pl.ds(pl.multiple_of(half * 512, 512), 512)
        return lax.dot_general(
            aold[:, pl.ds(r * 256, 256)], gv[:, cols], tn, preferred_element_type=F32
        ) * (1.0 / 2048.0)

    for r in range(3):
        gsend[pl.ds(r * 256, 256)] = grad_tile(r, od).astype(BF)
    gcopy = pltpu.make_async_remote_copy(
        src_ref=gsend, dst_ref=grecv, send_sem=xss.at[1], recv_sem=xrs.at[1],
        device_id=dp_peer, device_id_type=MESH)
    gcopy.start()

    wcopy.wait_recv()

    def proj_tile(i, _):
        row = pl.multiple_of(i * 128, 128)
        a = aold[pl.ds(row, 128)]
        for h in range(2):
            r = jnp.dot(a, wf[h], preferred_element_type=F32)
            cols = pl.ds(h * 512, 512)
            lo, hi = r[:64], r[64:]
            pk[i, :, cols] = jnp.where(c == 0, hi, lo).astype(BF)
            pown[i, :, cols] = jnp.where(c == 0, lo, hi)
        return 0

    lax.fori_loop(0, nt, proj_tile, 0)
    ccopy = pltpu.make_async_remote_copy(
        src_ref=pk, dst_ref=cp, send_sem=xss.at[2], recv_sem=xrs.at[2],
        device_id=core_peer, device_id_type=MESH)
    ccopy.start()

    def hid(i):
        row = pl.multiple_of(i * 128, 128)
        r = lax.dot_general(gv[pl.ds(row, 128), pl.ds(0, 512)], wf[0], nt_dims, preferred_element_type=F32)
        return r + lax.dot_general(gv[pl.ds(row, 128), pl.ds(512, 512)], wf[1], nt_dims, preferred_element_type=F32)

    def hcopy(p, q_):
        return pltpu.make_async_remote_copy(
            src_ref=hgs.at[p], dst_ref=hgr.at[q_], send_sem=ssh.at[p], recv_sem=rsh.at[q_],
            device_id=(s, p, d), device_id_type=MESH)

    def go_h(k, _):
        p = ten(k)
        hgs[p] = hid(p).astype(BF)
        hcopy(p, t).start()
        return 0

    lax.fori_loop(1, nt, go_h, 0)
    hown = hid(t)
    for b in range(BLOCKS):
        hgr[t, :, pl.ds(b * 128, 128)] = hown[:, b * 128:(b + 1) * 128].astype(BF)

    for r in range(3):
        gown[pl.ds(r * 256, 256)] = grad_tile(r, d)

    ccopy.wait_recv()

    def qcopy(p, q_):
        return pltpu.make_async_remote_copy(
            src_ref=q.at[p], dst_ref=rq.at[q_], send_sem=ssq.at[p], recv_sem=rsq.at[q_],
            device_id=(p * 2 + c, t, d), device_id_type=MESH)

    def go_q(k, _):
        p = lax.rem(z + k, 8)
        q[p] = (pown[p] + cp[p].astype(F32)).astype(BF)
        qcopy(p, z).start()
        return 0

    lax.fori_loop(1, 8, go_q, 0)
    rq[z] = (pown[z] + cp[z].astype(F32)).astype(BF)

    locals_[3].wait()
    locals_[4].wait()
    gcopy.wait_recv()
    for b in range(BLOCKS):
        rows = pl.ds(b * 128, 128)
        g = gown[rows] + grecv[rows].astype(F32)
        f1 = 0.9 * fv[rows] + 0.1 * g
        s1 = 0.999 * sv[rows] + 0.001 * g * g
        ab[b] = (f1 / (jnp.sqrt(s1 / CORR_SECOND) + 1e-08)).astype(BF)
    go4, ws4, wr4 = to_sections(send4, recv4, ss4, rs4)
    for p in range(ns):
        send4[p] = ab[block_for[p]]
    go4()
    recv4[s] = send4[s]

    def wr_h(k, _):
        p = ten(k)
        hcopy(p, p).wait_recv()
        return 0

    lax.fori_loop(1, nt, wr_h, 0)
    for b in range(BLOCKS):
        acc = hgr[0, :, pl.ds(b * 128, 128)].astype(F32)
        for p in range(1, nt):
            acc = acc + hgr[p, :, pl.ds(b * 128, 128)].astype(F32)
        hb[b] = acc.astype(BF)
    for p in range(ns):
        send3[p] = hb[block_for[p]]
    go3, ws3, wr3 = to_sections(send3, recv3, ss3, rs3)
    go3()
    recv3[s] = send3[s]
    wr3()
    for k in range(RCAP):
        send5[k] = (recv3[owner_of[k]].astype(F32) * used[k]).astype(BF)

    def fcopy(p, q_):
        row = pl.multiple_of(q_ * 128, 128)
        return pltpu.make_async_remote_copy(
            src_ref=send5.at[p], dst_ref=hgf.at[pl.ds(row, 128)], send_sem=ss5.at[p], recv_sem=rs5.at[q_],
            device_id=(s, p, d), device_id_type=MESH)

    def go5(k, _):
        fcopy(ten(k), t).start()
        return 0

    def wr5(k, _):
        p = ten(k)
        fcopy(p, p).wait_recv()
        return 0

    lax.fori_loop(1, nt, go5, 0)
    hgf[pl.ds(trow, 128)] = send5[t]

    def wr_q(k, _):
        p = lax.rem(z + k, 8)
        qcopy(p, p).wait_recv()
        return 0

    lax.fori_loop(1, 8, wr_q, 0)
    acc = rq[0].astype(F32)
    for p in range(1, 8):
        acc = acc + rq[p].astype(F32)
    proj_out[...] = acc.astype(BF)

    lax.fori_loop(1, nt, wr5, 0)
    hidden_out[...] = hgf[...]

    wr4()
    for k in range(RCAP):
        step_out[k] = (recv4[owner_of[k]].astype(F32) * used[k]).astype(BF)

    ws1()
    ws3()
    ws4()
    wcopy.wait_send()
    gcopy.wait_send()
    ccopy.wait_send()

    def ws_t(k, _):
        p = ten(k)
        gather(p, t).wait_send()
        hcopy(p, t).wait_send()
        fcopy(p, t).wait_send()
        return 0

    lax.fori_loop(1, nt, ws_t, 0)

    def ws_q(k, _):
        qcopy(lax.rem(z + k, 8), z).wait_send()
        return 0

    lax.fori_loop(1, 8, ws_q, 0)


def routed_kernel(
    tab, master, first, second, acts, grads,
    proj_out, hidden_out, step_out,
    strip, blk, mv, gv, fv, sv,
    send1, recv10, recv11, aold, wf, gq, gsend, grecv, gown, pk, pown, cp, qs, qr,
    hgs, hgr, hxs, hxr, hown, send5, hgf,
    ab0, pool0, xa0, fa0, sa0, sb0, xs0, xr0,
    ab1, pool1, xa1, fa1, sa1, sb1, xs1, xr1,
    ab2, pool2, xa2, fa2, sa2, sb2, xs2, xr2,
    lsem, ss1, rs1, ss2, rs2, xss, xrs, ssq, rsq, ssh, rsh, ss5, rs5, rss, rsr,
):
    ns, nt = 16, 8
    s = lax.axis_index("section")
    t = lax.axis_index("tensor")
    d = lax.axis_index("dp")
    z, c = s // 2, s % 2
    y, xl = t // 2, t % 2
    od, oc, tx = 1 - d, 1 - c, y * 2 + (1 - xl)
    core_peer = (z * 2 + oc, t, d)
    dp_peer = (s, t, od)
    x_peer = (s, tx, d)

    def sec(k):
        return lax.rem(s + k, ns)

    def ten(k):
        return lax.rem(t + k, nt)

    def ypeer(k):
        return lax.rem(y + k, 4)

    def chip(k):
        return lax.rem(z + k, 8)

    def remote(src, dst, sends, recvs, device):
        return pltpu.make_async_remote_copy(
            src_ref=src, dst_ref=dst, send_sem=sends, recv_sem=recvs,
            device_id=device, device_id_type=MESH)

    trow = pl.multiple_of(t * 128, 128)
    xrow = pl.multiple_of(tx * 128, 128)
    locals_ = [
        pltpu.make_async_copy(acts.at[pl.ds(trow, 128)], strip, lsem.at[0]),
        pltpu.make_async_copy(master, mv, lsem.at[1]),
        pltpu.make_async_copy(grads, gv, lsem.at[2]),
        pltpu.make_async_copy(first, fv, lsem.at[3]),
        pltpu.make_async_copy(second, sv, lsem.at[4]),
    ]
    for cpy in locals_:
        cpy.start()

    bar = pltpu.get_barrier_semaphore()
    for k in range(1, ns):
        pl.semaphore_signal(bar, inc=1, device_id=(sec(k), t, d), device_id_type=MESH)
    for k in range(1, nt):
        pl.semaphore_signal(bar, inc=1, device_id=(s, ten(k), d), device_id_type=MESH)
    pl.semaphore_signal(bar, inc=1, device_id=dp_peer, device_id_type=MESH)

    locals_[0].wait()
    for k in range(RCAP):
        blk[k] = strip[:, pl.ds(k * 128, 128)]
    for o in range(ns):
        both = blk[tab[o]]
        for h in range(2):
            send1[h, o] = both[h * 64:(h + 1) * 64]
    locals_[1].wait()
    for b in range(BLOCKS):
        wf[d, pl.ds(b * 128, 128)] = mv[pl.ds(b * 128, 128)].astype(BF)

    pl.semaphore_wait(bar, ns - 1 + nt - 1 + 1)

    recv1 = (recv10, recv11)

    def acopy(h, p, o):
        return remote(send1.at[h, p], recv1[h].at[o], ss1.at[h, p], rs1.at[h, o], (p, t, d))

    def go1(h):
        def go(k, _):
            acopy(h, sec(k), s).start()
            return 0

        lax.fori_loop(1, ns, go, 0)

    def weights(h):
        rows = wf.at[d, pl.ds(h * 384, 384)]
        return remote(rows, rows, xss.at[5 + h], xrs.at[5 + h], dp_peer)

    go1(0)
    weights(0).start()
    go1(1)
    for h in range(2):
        recv1[h][s] = send1[h, s]

    locals_[2].wait()
    for u in range(2):
        for j in range(2):
            src = j * 256 + u * 128
            for h in range(2):
                gq[h, u, :, pl.ds(j * 128, 128)] = gv[:, pl.ds(h * 512 + src, 128)]

    def wr1(h):
        def wait(k, _):
            p = sec(k)
            acopy(h, p, p).wait_recv()
            return 0

        lax.fori_loop(1, ns, wait, 0)

    def piece(h, sends, owner, device):
        rows = aold.at[pl.ds(pl.multiple_of(owner * 128 + h * 64, 64), 64)]
        return remote(rows, rows, ss2.at[h, sends], rs2.at[h, owner], device)

    up, down = ypeer(1), ypeer(3)

    def at_y(q):
        return (s, q * 2 + xl, d)

    for h in range(2):
        wr1(h)
        for b in range(BLOCKS):
            aold[pl.ds(pl.multiple_of(t * 128 + h * 64, 64), 64), pl.ds(b * 128, 128)] = recv1[h][tab[48 + b]]
        piece(h, 0, t, x_peer).start()
        piece(h, 1, t, at_y(up)).start()
        piece(h, 2, t, at_y(down)).start()
    for h in range(2):
        piece(h, 0, tx, x_peer).wait_recv()
        piece(h, 3, tx, at_y(up)).start()
        piece(h, 4, tx, at_y(down)).start()
        piece(h, 0, up * 2 + xl, x_peer).wait_recv()
        piece(h, 5, up * 2 + xl, at_y(down)).start()
    weights(1).start()
    for h in range(2):
        piece(h, 0, down * 2 + (1 - xl), x_peer).wait_recv()
        piece(h, 6, down * 2 + (1 - xl), at_y(up)).start()
    nt_dims = (((1,), (1,)), ((), ()))
    tn = (((0,), (0,)), ((), ()))
    far = ypeer(2)
    for h in range(2):
        piece(h, 0, down * 2 + xl, x_peer).wait_recv()
        piece(h, 0, up * 2 + (1 - xl), x_peer).wait_recv()
        piece(h, 0, far * 2 + xl, x_peer).wait_recv()
        piece(h, 0, far * 2 + (1 - xl), x_peer).wait_recv()

    def grad_tile(r, h, u):
        return lax.dot_general(
            aold[:, pl.ds(r * 256, 256)], gq[h, u], tn, preferred_element_type=F32) * (1.0 / 2048.0)

    gcopies = []
    for u in range(2):
        for r in range(3):
            gsend[u, pl.ds(r * 256, 256)] = grad_tile(r, od, u).astype(BF)
        gcopies.append(remote(gsend.at[u], grecv.at[u], xss.at[1 + u], xrs.at[1 + u], dp_peer))
        gcopies[u].start()

    for h in range(2):
        weights(h).wait_recv()

    def proj_tile(i, _):
        a = aold[pl.ds(pl.multiple_of(i * 256, 256), 256)]
        for h in range(2):
            r = jnp.dot(a, wf[h], preferred_element_type=F32)
            cols = pl.ds(h * 512, 512)
            for j in range(2):
                lo, hi = r[j * 128:j * 128 + 64], r[j * 128 + 64:j * 128 + 128]
                pk[i * 2 + j, :, cols] = jnp.where(c == 0, hi, lo).astype(BF)
                pown[i * 2 + j, :, cols] = jnp.where(c == 0, lo, hi)
        return 0

    lax.fori_loop(0, 4, proj_tile, 0)
    ccopy = remote(pk, cp, xss.at[3], xrs.at[3], core_peer)
    ccopy.start()

    def hcopy(i, o):
        return remote(hgs.at[i], hgr.at[o], ssh.at[i], rsh.at[o], (s, i * 2 + xl, d))

    def hid(i):
        row = pl.multiple_of(i * 256, 256)
        r = lax.dot_general(gv[pl.ds(row, 256), pl.ds(0, 512)], wf[0], nt_dims, preferred_element_type=F32)
        return r + lax.dot_general(gv[pl.ds(row, 256), pl.ds(512, 512)], wf[1], nt_dims, preferred_element_type=F32)

    def hid_y(k, _):
        i = ypeer(k)
        r = hid(i).astype(BF)
        for x in range(2):
            hgs[i, x] = r[x * 128:(x + 1) * 128]
        hcopy(i, y).start()
        return 0

    lax.fori_loop(1, 4, hid_y, 0)
    r = hid(y)
    for x in range(2):
        hown[x] = r[x * 128:(x + 1) * 128]

    ccopy.wait_recv()

    lo, hi = pl.ds(0, 32), pl.ds(32, 32)

    def ring(n, way):
        rows = pl.ds(0, 64) if n > 1 else (lo if way == 0 else hi)
        return remote(
            qs.at[way, n - 1, rows], qr.at[way, n - 1, rows], ssq.at[way, n - 1], rsq.at[way, n - 1],
            (chip(1 if way == 0 else 7) * 2 + c, t, d))

    def partial_(p, rows):
        return pown[p, rows] + cp[p, rows].astype(F32)

    def ring_step(n):
        for way in range(2):
            p = chip(5 - n if way == 0 else n + 3)
            first_rows, other_rows = (lo, hi) if way == 0 else (hi, lo)
            if n > 1:
                ring(n - 1, way).wait_recv()
            if n == 1:
                qs[way, 0, first_rows] = partial_(p, first_rows).astype(BF)
            elif n == 2:
                qs[way, 1, first_rows] = (partial_(p, first_rows) + qr[way, 0, first_rows].astype(F32)).astype(BF)
                qs[way, 1, other_rows] = partial_(p, other_rows).astype(BF)
            else:
                qs[way, n - 1] = (partial_(p, pl.ds(0, 64)) + qr[way, n - 2].astype(F32)).astype(BF)
            ring(n, way).start()

    ring_step(1)
    for u in range(2):
        for r in range(3):
            gown[u, pl.ds(r * 256, 256)] = grad_tile(r, d, u)

    parts = [
        (ab0, pool0, xa0, fa0, sa0, sb0, xs0, xr0),
        (ab1, pool1, xa1, fa1, sa1, sb1, xs1, xr1),
        (ab2, pool2, xa2, fa2, sa2, sb2, xs2, xr2),
    ]

    def swap_copy(u):
        ab_, pool_ = parts[u][:2]
        return remote(ab_.at[oc], pool_.at[pl.ds(c * BLOCKS, BLOCKS)], rss.at[u, 0], rsr.at[u, 0], core_peer)

    def enter(u):
        ab_, pool_ = parts[u][:2]
        swap_copy(u).start()
        for b in range(BLOCKS):
            pool_[c * BLOCKS + b] = ab_[c, b]

    def copy_a(u, p, o):
        return remote(parts[u][4].at[p], parts[u][2].at[o], rss.at[u, 1 + p], rsr.at[u, 1 + o], (p * 2 + c, t, d))

    def copy_b(u, p, o):
        return remote(parts[u][5].at[p], parts[u][3].at[o], rss.at[u, 9 + p], rsr.at[u, 9 + o], (p * 2 + c, t, d))

    def copy_n(u, j):
        p = chip(1 if j == 0 else 7)
        return remote(parts[u][5].at[8 + j], parts[u][3].at[28 + j], rss.at[u, 17 + j], rsr.at[u, 17 + j], (p * 2 + c, t, d))

    order = (4, 3, 5, 2, 6, 1, 7)

    def round_a(u):
        _, pool_, xa_, _, sa_, _, _, _ = parts[u]
        swap_copy(u).wait_recv()
        for k in order:
            m = chip(k)
            sa_[m] = pool_[tab[56 + m]]
            copy_a(u, m, z).start()
        for l in range(12):
            xa_[8 + l] = pool_[l]
        xa_[z] = jnp.zeros(xa_.shape[1:], BF)

    def round_b(u):
        _, pool_, xa_, fa_, _, sb_, _, _ = parts[u]
        for k in order:
            m = chip(k)
            copy_a(u, m, m).wait_recv()
        for k in order:
            m = chip(k)
            sb_[m] = xa_[tab[64 + m]]
            copy_b(u, m, z).start()
        for j in range(2):
            sb_[8 + j] = xa_[tab[72 + j]]
            copy_n(u, j).start()
        for l in range(20):
            fa_[8 + l] = xa_[l]
        fa_[z] = jnp.zeros(fa_.shape[1:], BF)
        fa_[30] = jnp.zeros(fa_.shape[1:], BF)

    def back_copy(u):
        return remote(parts[u][6], parts[u][7], rss.at[u, 19], rsr.at[u, 19], core_peer)

    def arrive(u):
        _, _, _, fa_, _, _, xs_, _ = parts[u]
        for k in order:
            m = chip(k)
            copy_b(u, m, m).wait_recv()
        for j in range(2):
            copy_n(u, j).wait_recv()
        for k in range(RCAP):
            xs_[k] = fa_[tab[80 + oc * 8 + k]]
        back_copy(u).start()

    def drain(u):
        swap_copy(u).wait_send()
        back_copy(u).wait_send()
        for k in order:
            copy_a(u, chip(k), z).wait_send()
            copy_b(u, chip(k), z).wait_send()
        for j in range(2):
            copy_n(u, j).wait_send()

    def adam(u):
        gcopies[u].wait_recv()
        for b in range(BLOCKS):
            rows = pl.ds(b * 128, 128)
            for j in range(2):
                cols = pl.ds(j * 256 + u * 128, 128)
                here = pl.ds(j * 128, 128)
                g = gown[u, rows, here] + grecv[u, rows, here].astype(F32)
                f1 = 0.9 * fv[rows, cols] + 0.1 * g
                s1 = 0.999 * sv[rows, cols] + 0.001 * g * g
                parts[u][0][j, b] = (f1 / (jnp.sqrt(s1 / CORR_SECOND) + 1e-08)).astype(BF)
        enter(u)

    def place(u):
        fa_, xr_ = parts[u][3], parts[u][7]
        back_copy(u).wait_recv()
        mine = pl.ds(pl.multiple_of(c * 256 + u * 128, 128), 128)
        theirs = pl.ds(pl.multiple_of(oc * 256 + u * 128, 128), 128)
        for k in range(RCAP):
            step_out[k, :, mine] = fa_[tab[80 + c * 8 + k]]
            step_out[k, :, theirs] = xr_[k]

    locals_[3].wait()
    locals_[4].wait()
    adam(0)
    ring_step(2)
    round_a(0)
    ring_step(3)
    round_b(0)
    ring_step(4)
    adam(1)
    round_a(1)

    for k in range(1, 4):
        p = ypeer(k)
        hcopy(p, p).wait_recv()
    for x in range(2):
        total = hown[x]
        for k in range(1, 4):
            total = total + hgr[ypeer(k), x].astype(F32)
        hown[x] = total
    hxs[...] = hown[1 - xl].astype(BF)
    hx = remote(hxs, hxr, xss.at[4], xrs.at[4], x_peer)
    hx.start()
    hx.wait_recv()
    hsum = hown[xl] + hxr[...].astype(F32)
    for b in range(BLOCKS):
        piece_ = hsum[:, b * 128:(b + 1) * 128].astype(BF)
        for j in range(2):
            ab2[j, b] = piece_[j * 64:(j + 1) * 64]
    enter(2)
    round_a(2)
    arrive(0)
    round_b(2)
    round_b(1)
    place(0)
    arrive(2)

    back_copy(2).wait_recv()
    mine = pl.ds(pl.multiple_of(c * 64, 64), 64)
    theirs = pl.ds(pl.multiple_of(oc * 64, 64), 64)
    for k in range(RCAP):
        send5[k, mine] = fa2[tab[80 + c * 8 + k]]
        send5[k, theirs] = xr2[k]

    def fcopy(p, o):
        rows = pl.ds(pl.multiple_of(o * 128, 128), 128)
        return remote(send5.at[p], hgf.at[rows], ss5.at[p], rs5.at[o], (s, p, d))

    def go5(k, _):
        fcopy(ten(k), t).start()
        return 0

    lax.fori_loop(1, nt, go5, 0)
    hgf[pl.ds(trow, 128)] = send5[t]
    arrive(1)

    for way in range(2):
        ring(4, way).wait_recv()
    proj_out[...] = (partial_(z, pl.ds(0, 64)) + qr[0, 3].astype(F32) + qr[1, 3].astype(F32)).astype(BF)

    place(1)

    def wr5(k, _):
        p = ten(k)
        fcopy(p, p).wait_recv()
        return 0

    lax.fori_loop(1, nt, wr5, 0)
    hidden_out[...] = hgf[...]

    for u in range(3):
        drain(u)
    for cpy in (gcopies[0], gcopies[1], ccopy, hx):
        cpy.wait_send()
    for h in range(2):
        weights(h).wait_send()
        for i in range(7):
            piece(h, i, t, x_peer).wait_send()

        def ws(k, _):
            acopy(h, sec(k), s).wait_send()
            return 0

        lax.fori_loop(1, ns, ws, 0)
    for k in range(1, 4):
        hcopy(ypeer(k), y).wait_send()
    for n in range(1, 5):
        for way in range(2):
            ring(n, way).wait_send()

    def ws5(k, _):
        fcopy(ten(k), t).wait_send()
        return 0

    lax.fori_loop(1, nt, ws5, 0)


def finish(proj, hidden, step, proj_out, hidden_out, step_out):
    proj_out[...] = proj[...]
    hidden_out[...] = hidden[...]
    for k in range(RCAP):
        step_out[pl.ds(k * 128, 128)] = step[k].astype(F32)


def shards(old_master, old_first, old_second, dest_section, dest_offset, hidden_acts, out_grad):
    any_ = pl.BlockSpec(memory_space=pl.ANY)
    smem = pl.BlockSpec(memory_space=pltpu.SMEM)
    vmem = pl.BlockSpec(memory_space=pltpu.VMEM)
    V = pltpu.VMEM
    dma = pltpu.SemaphoreType.DMA
    tab, ok = pl.pallas_call(
        plan,
        out_shape=(jax.ShapeDtypeStruct((128,), jnp.int32), jax.ShapeDtypeStruct((1,), jnp.int32)),
        in_specs=[smem, smem],
        out_specs=(smem, smem),
        scratch_shapes=[pltpu.SMEM((256,), jnp.int32), pltpu.SMEM((128,), jnp.int32)],
        name="plan",
    )(dest_section, dest_offset)
    out_shape = (
        jax.ShapeDtypeStruct((64, 1024), BF),
        jax.ShapeDtypeStruct((1024, 128), BF),
        jax.ShapeDtypeStruct((8, 128, 512), BF),
    )

    def call(body, scratch, number, name):
        return pl.pallas_call(
            body,
            out_shape=out_shape,
            in_specs=[smem, any_, any_, any_, any_, any_],
            out_specs=(vmem, vmem, vmem),
            scratch_shapes=scratch,
            compiler_params=pltpu.CompilerParams(
                collective_id=number, has_side_effects=True, vmem_limit_bytes=58 * 2**20),
            name=name,
        )

    padded = call(padded_kernel, [
        V((128, 1024), BF), V((8, 128, 128), BF), V((768, 512), F32), V((1024, 1024), BF), V((768, 512), F32), V((768, 512), F32),
        V((16, 128, 128), BF), V((16, 128, 128), BF), V((1024, 768), BF), V((2, 768, 512), BF),
        V((768, 512), BF), V((768, 512), BF), V((768, 512), F32),
        V((8, 64, 1024), BF), V((8, 64, 1024), F32), V((8, 64, 1024), BF), V((8, 64, 1024), BF), V((8, 64, 1024), BF),
        V((8, 128, 768), BF), V((8, 128, 768), BF), V((6, 128, 128), BF), V((16, 128, 128), BF), V((16, 128, 128), BF),
        V((8, 128, 128), BF), V((1024, 128), BF), V((6, 128, 512), BF), V((16, 128, 512), BF), V((16, 128, 512), BF),
        dma((5,)), dma((16,)), dma((16,)), dma((8,)), dma((8,)), dma((3,)), dma((3,)), dma((8,)), dma((8,)),
        dma((8,)), dma((8,)), dma((16,)), dma((16,)), dma((8,)), dma((8,)), dma((16,)), dma((16,)),
    ], 0, "padded")


    def buffers(rows):
        shapes = ((2, 6), (12,), (20,), (31,), (8,), (10,), (8,), (8,))
        return [V((*n, rows, 128), BF) for n in shapes]

    routed = call(routed_kernel, [
        V((128, 1024), BF), V((8, 128, 128), BF), V((768, 512), F32), V((1024, 1024), BF), V((768, 512), F32), V((768, 512), F32),
        V((2, 16, 64, 128), BF), V((16, 64, 128), BF), V((16, 64, 128), BF), V((1024, 768), BF), V((2, 768, 512), BF),
        V((2, 2, 1024, 256), BF), V((2, 768, 256), BF), V((2, 768, 256), BF), V((2, 768, 256), F32),
        V((8, 64, 1024), BF), V((8, 64, 1024), F32), V((8, 64, 1024), BF), V((2, 4, 64, 1024), BF), V((2, 4, 64, 1024), BF),
        V((4, 2, 128, 768), BF), V((4, 2, 128, 768), BF), V((128, 768), BF), V((128, 768), BF), V((2, 128, 768), F32),
        V((8, 128, 128), BF), V((1024, 128), BF),
        *buffers(128), *buffers(128), *buffers(64),
        dma((5,)), dma((2, 16)), dma((2, 16)), dma((2, 8)), dma((2, 8)), dma((7,)), dma((7,)), dma((2, 4)), dma((2, 4)),
        dma((4,)), dma((4,)), dma((8,)), dma((8,)), dma((3, 20)), dma((3, 20)),
    ], 1, "routed")

    args = (tab, old_master, old_first, old_second, hidden_acts[0], out_grad[0])
    proj, hidden, step = lax.cond(ok[0] == 1, routed, padded, *args)
    proj, hidden, step = pl.pallas_call(
        finish,
        out_shape=(
            jax.ShapeDtypeStruct((64, 1024), BF),
            jax.ShapeDtypeStruct((1024, 128), BF),
            jax.ShapeDtypeStruct((1024, 512), F32),
        ),
        in_specs=[vmem] * 3,
        out_specs=(vmem, vmem, vmem),
        compiler_params=pltpu.CompilerParams(vmem_limit_bytes=32 * 2**20),
        name="finish",
    )(proj, hidden, step)
    return proj[None], hidden[None], step


def solution(mesh):
    placed = (
        P("section", ("tensor", "dp")),
        P("section", ("tensor", "dp")),
        P("section", ("tensor", "dp")),
        P(),
        P(),
        P("dp", None, "section"),
        P("dp", None, "tensor"),
    )
    return jax.shard_map(
        shards,
        mesh=mesh,
        in_specs=placed,
        out_specs=(
            P("dp", "section", "tensor"),
            P("dp", None, ("section", "tensor")),
            P("section", ("tensor", "dp")),
        ),
        check_vma=False,
    )
```

```python
import jax
import jax.numpy as jnp
from jax import lax
from jax.experimental import pallas as pl
from jax.experimental.pallas import tpu as pltpu
from jax.sharding import PartitionSpec as P

ROWS = 128
BLOCKS = 6
RCAP = 8
CORR_SECOND = 0.6323045752
MESH = pl.DeviceIdType.MESH
BF = jnp.bfloat16
F32 = jnp.float32


def plan(dest, off, tab, ok, route, late):
    s = lax.axis_index("section")
    z = s // 2
    for i in range(112):
        tab[i] = 30 if 80 <= i < 96 else (8 if 64 <= i < 74 else 0)
    ok[0] = 1

    def clear(i, _):
        for j in range(16):
            route[i * 16 + j] = -1
        return 0

    lax.fori_loop(0, 12, clear, 0)

    def near(a, p):
        k = jnp.bitwise_and(p - a, 7)
        return (k == 1) | (k == 7)

    def rank(a, n):
        count = jnp.int32(0)
        for i in range(12):
            g = a * 12 + i
            o = a * 2 + i // 6
            q = dest[g]
            k = off[g]
            here = q == s
            tab[jnp.where(here, o, 112)] = k
            tab[jnp.where(here, 32 + k, 113)] = o
            tab[jnp.where(here, 40 + k, 114)] = 1
            p = lax.shift_right_logical(q, 1)
            r = jnp.bitwise_and(lax.shift_right_logical(count, p * 4), 15)
            count = count + lax.shift_left(jnp.int32(1), p * 4)
            fits = (r < 2) | ((r == 2) & near(a, p)) | (a == p)
            route[jnp.where(fits & (a != p), r * 64 + a * 8 + p, 192)] = g
            late[n] = g
            n = n + jnp.where(fits, 0, 1)
        return n

    n_late = lax.fori_loop(0, 8, rank, jnp.int32(0))
    for b in range(BLOCKS):
        p = dest[s * BLOCKS + b]
        tab[16 + p] = b
        tab[48 + b] = p

    def detour(i, _):
        g = late[i]
        a, p = g // 12, dest[g] // 2
        best = jnp.int32(-1)
        for k in (4, 3, 5, 2, 6, 1, 7):
            m = jnp.bitwise_and(p + k, 7)
            am, mp = a * 8 + m, m * 8 + p
            last = jnp.where(route[64 + mp] < 0, 1, 0)
            if k in (1, 7):
                last = jnp.where((last == 0) & (route[128 + mp] < 0), 2, last)
            held = route[am]
            direct = lax.shift_right_logical(dest[jnp.maximum(held, 0)], 1) == m
            second = jnp.where(route[64 + am] < 0, 1, jnp.where(near(a, m) & (route[128 + am] < 0), 2, 3))
            move = jnp.where(held < 0, 0, jnp.where(direct, second, 3))
            good = (last > 0) & (move < 3) & (m != a)
            best = jnp.where(good, m * 16 + last * 4 + move, best)

        @pl.when(best >= 0)
        def _():
            m = best // 16
            am = a * 8 + m
            move = jnp.bitwise_and(best, 3)
            last = jnp.bitwise_and(best // 4, 3)
            route[jnp.where(move > 0, move * 64 + am, 192)] = route[am]
            route[am] = g
            route[last * 64 + m * 8 + p] = g

        @pl.when(best < 0)
        def _():
            ok[0] = 0

        return 0

    lax.fori_loop(0, n_late, detour, 0)

    for m in range(8):
        g = route[z * 8 + m]
        tab[56 + m] = jnp.where((g >= 0) & (z != m), g - 12 * z, 0)
    for j in range(10):
        if j < 8:
            g = route[64 + z * 8 + j]
        else:
            g = route[128 + z * 8 + jnp.bitwise_and(z + (1 if j == 8 else 7), 7)]
        a = jnp.maximum(g, 0) // 12
        from_pool = 8 + g - 12 * z
        tab[64 + j] = jnp.where(g < 0, 8, jnp.where(a == z, from_pool, a))

    def final(g, source):
        h = jnp.maximum(g, 0)
        p = dest[h]
        mine = (g >= 0) & (lax.shift_right_logical(p, 1) == z)
        tab[jnp.where(mine, 80 + jnp.bitwise_and(p, 1) * 8 + off[h], 115)] = source

    for a in range(8):
        final(route[a * 8 + z], 8 + a)
        final(route[64 + a * 8 + z], a)
    final(route[128 + jnp.bitwise_and(z + 7, 7) * 8 + z], 28)
    final(route[128 + jnp.bitwise_and(z + 1, 7) * 8 + z], 29)
    for l in range(12):
        final(12 * z + l, 16 + l)


def padded_kernel(
    tab, master, first, second, acts, grads,
    proj_out, hidden_out, step_out,
    strip, blk, mv, gv, fv, sv,
    send1, recv1, aold, wf, gsend, grecv, gown, pk, pown, cp, q, rq,
    hgs, hgr, hb, send3, recv3, send5, hgf, ab, send4, recv4,
    lsem, ss1, rs1, ss2, rs2, xss, xrs, ssq, rsq, ssh, rsh, ss3, rs3, ss5, rs5, ss4, rs4,
):
    ns, nt = 16, 8
    s = lax.axis_index("section")
    t = lax.axis_index("tensor")
    d = lax.axis_index("dp")
    z, c = s // 2, s % 2
    od = 1 - d
    core_peer = (z * 2 + (1 - c), t, d)
    dp_peer = (s, t, od)

    def sec(k):
        return lax.rem(s + k, ns)

    def ten(k):
        return lax.rem(t + k, nt)

    trow = pl.multiple_of(t * 128, 128)
    locals_ = [
        pltpu.make_async_copy(acts.at[pl.ds(trow, 128)], strip, lsem.at[0]),
        pltpu.make_async_copy(master, mv, lsem.at[1]),
        pltpu.make_async_copy(grads, gv, lsem.at[2]),
        pltpu.make_async_copy(first, fv, lsem.at[3]),
        pltpu.make_async_copy(second, sv, lsem.at[4]),
    ]
    for cpy in locals_:
        cpy.start()

    bar = pltpu.get_barrier_semaphore()
    for k in range(1, ns):
        pl.semaphore_signal(bar, inc=1, device_id=(sec(k), t, d), device_id_type=MESH)
    for k in range(1, nt):
        pl.semaphore_signal(bar, inc=1, device_id=(s, ten(k), d), device_id_type=MESH)
    pl.semaphore_signal(bar, inc=1, device_id=dp_peer, device_id_type=MESH)

    slot_of = [tab[o] for o in range(ns)]
    block_for = [tab[16 + p] for p in range(ns)]
    owner_of = [tab[32 + k] for k in range(RCAP)]
    used = [tab[40 + k].astype(F32) for k in range(RCAP)]
    mine = [tab[48 + b] for b in range(BLOCKS)]

    locals_[0].wait()
    for k in range(RCAP):
        blk[k] = strip[:, pl.ds(k * 128, 128)]
    for o in range(ns):
        send1[o] = blk[slot_of[o]]
    locals_[1].wait()
    for b in range(BLOCKS):
        wf[d, pl.ds(b * 128, 128)] = mv[pl.ds(b * 128, 128)].astype(BF)

    pl.semaphore_wait(bar, ns - 1 + nt - 1 + 1)

    def to_sections(src, dst, sends, recvs):
        def copy(p):
            return pltpu.make_async_remote_copy(
                src_ref=src.at[p], dst_ref=dst.at[s],
                send_sem=sends.at[p], recv_sem=recvs.at[s],
                device_id=(p, t, d), device_id_type=MESH)

        def go(k, _):
            copy(sec(k)).start()
            return 0

        def wait_send(k, _):
            copy(sec(k)).wait_send()
            return 0

        def wait_recv(k, _):
            p = sec(k)
            pltpu.make_async_remote_copy(
                src_ref=src.at[p], dst_ref=dst.at[p],
                send_sem=sends.at[p], recv_sem=recvs.at[p],
                device_id=(p, t, d), device_id_type=MESH).wait_recv()
            return 0

        return (
            lambda: lax.fori_loop(1, ns, go, 0),
            lambda: lax.fori_loop(1, ns, wait_send, 0),
            lambda: lax.fori_loop(1, ns, wait_recv, 0),
        )

    go1, ws1, wr1 = to_sections(send1, recv1, ss1, rs1)
    go1()
    wcopy = pltpu.make_async_remote_copy(
        src_ref=wf.at[d], dst_ref=wf.at[d], send_sem=xss.at[0], recv_sem=xrs.at[0],
        device_id=dp_peer, device_id_type=MESH)
    wcopy.start()
    recv1[s] = send1[s]
    wr1()
    for b in range(BLOCKS):
        aold[pl.ds(trow, 128), pl.ds(b * 128, 128)] = recv1[mine[b]]

    def gather(p, q_):
        row = pl.multiple_of(q_ * 128, 128)
        return pltpu.make_async_remote_copy(
            src_ref=aold.at[pl.ds(row, 128)], dst_ref=aold.at[pl.ds(row, 128)],
            send_sem=ss2.at[p], recv_sem=rs2.at[q_],
            device_id=(s, p, d), device_id_type=MESH)

    def go2(k, _):
        gather(ten(k), t).start()
        return 0

    def wr2(k, _):
        p = ten(k)
        gather(p, p).wait_recv()
        return 0

    lax.fori_loop(1, nt, go2, 0)
    locals_[2].wait()
    lax.fori_loop(1, nt, wr2, 0)

    tn = (((0,), (0,)), ((), ()))
    nt_dims = (((1,), (1,)), ((), ()))

    def grad_tile(r, half):
        cols = pl.ds(pl.multiple_of(half * 512, 512), 512)
        return lax.dot_general(
            aold[:, pl.ds(r * 256, 256)], gv[:, cols], tn, preferred_element_type=F32
        ) * (1.0 / 2048.0)

    for r in range(3):
        gsend[pl.ds(r * 256, 256)] = grad_tile(r, od).astype(BF)
    gcopy = pltpu.make_async_remote_copy(
        src_ref=gsend, dst_ref=grecv, send_sem=xss.at[1], recv_sem=xrs.at[1],
        device_id=dp_peer, device_id_type=MESH)
    gcopy.start()

    wcopy.wait_recv()

    def proj_tile(i, _):
        row = pl.multiple_of(i * 128, 128)
        a = aold[pl.ds(row, 128)]
        for h in range(2):
            r = jnp.dot(a, wf[h], preferred_element_type=F32)
            cols = pl.ds(h * 512, 512)
            lo, hi = r[:64], r[64:]
            pk[i, :, cols] = jnp.where(c == 0, hi, lo).astype(BF)
            pown[i, :, cols] = jnp.where(c == 0, lo, hi)
        return 0

    lax.fori_loop(0, nt, proj_tile, 0)
    ccopy = pltpu.make_async_remote_copy(
        src_ref=pk, dst_ref=cp, send_sem=xss.at[2], recv_sem=xrs.at[2],
        device_id=core_peer, device_id_type=MESH)
    ccopy.start()

    def hid(i):
        row = pl.multiple_of(i * 128, 128)
        r = lax.dot_general(gv[pl.ds(row, 128), pl.ds(0, 512)], wf[0], nt_dims, preferred_element_type=F32)
        return r + lax.dot_general(gv[pl.ds(row, 128), pl.ds(512, 512)], wf[1], nt_dims, preferred_element_type=F32)

    def hcopy(p, q_):
        return pltpu.make_async_remote_copy(
            src_ref=hgs.at[p], dst_ref=hgr.at[q_], send_sem=ssh.at[p], recv_sem=rsh.at[q_],
            device_id=(s, p, d), device_id_type=MESH)

    def go_h(k, _):
        p = ten(k)
        hgs[p] = hid(p).astype(BF)
        hcopy(p, t).start()
        return 0

    lax.fori_loop(1, nt, go_h, 0)
    hown = hid(t)
    for b in range(BLOCKS):
        hgr[t, :, pl.ds(b * 128, 128)] = hown[:, b * 128:(b + 1) * 128].astype(BF)

    for r in range(3):
        gown[pl.ds(r * 256, 256)] = grad_tile(r, d)

    ccopy.wait_recv()

    def qcopy(p, q_):
        return pltpu.make_async_remote_copy(
            src_ref=q.at[p], dst_ref=rq.at[q_], send_sem=ssq.at[p], recv_sem=rsq.at[q_],
            device_id=(p * 2 + c, t, d), device_id_type=MESH)

    def go_q(k, _):
        p = lax.rem(z + k, 8)
        q[p] = (pown[p] + cp[p].astype(F32)).astype(BF)
        qcopy(p, z).start()
        return 0

    lax.fori_loop(1, 8, go_q, 0)
    rq[z] = (pown[z] + cp[z].astype(F32)).astype(BF)

    locals_[3].wait()
    locals_[4].wait()
    gcopy.wait_recv()
    for b in range(BLOCKS):
        rows = pl.ds(b * 128, 128)
        g = gown[rows] + grecv[rows].astype(F32)
        f1 = 0.9 * fv[rows] + 0.1 * g
        s1 = 0.999 * sv[rows] + 0.001 * g * g
        ab[b] = (f1 / (jnp.sqrt(s1 / CORR_SECOND) + 1e-08)).astype(BF)
    go4, ws4, wr4 = to_sections(send4, recv4, ss4, rs4)
    for p in range(ns):
        send4[p] = ab[block_for[p]]
    go4()
    recv4[s] = send4[s]

    def wr_h(k, _):
        p = ten(k)
        hcopy(p, p).wait_recv()
        return 0

    lax.fori_loop(1, nt, wr_h, 0)
    for b in range(BLOCKS):
        acc = hgr[0, :, pl.ds(b * 128, 128)].astype(F32)
        for p in range(1, nt):
            acc = acc + hgr[p, :, pl.ds(b * 128, 128)].astype(F32)
        hb[b] = acc.astype(BF)
    for p in range(ns):
        send3[p] = hb[block_for[p]]
    go3, ws3, wr3 = to_sections(send3, recv3, ss3, rs3)
    go3()
    recv3[s] = send3[s]
    wr3()
    for k in range(RCAP):
        send5[k] = (recv3[owner_of[k]].astype(F32) * used[k]).astype(BF)

    def fcopy(p, q_):
        row = pl.multiple_of(q_ * 128, 128)
        return pltpu.make_async_remote_copy(
            src_ref=send5.at[p], dst_ref=hgf.at[pl.ds(row, 128)], send_sem=ss5.at[p], recv_sem=rs5.at[q_],
            device_id=(s, p, d), device_id_type=MESH)

    def go5(k, _):
        fcopy(ten(k), t).start()
        return 0

    def wr5(k, _):
        p = ten(k)
        fcopy(p, p).wait_recv()
        return 0

    lax.fori_loop(1, nt, go5, 0)
    hgf[pl.ds(trow, 128)] = send5[t]

    def wr_q(k, _):
        p = lax.rem(z + k, 8)
        qcopy(p, p).wait_recv()
        return 0

    lax.fori_loop(1, 8, wr_q, 0)
    acc = rq[0].astype(F32)
    for p in range(1, 8):
        acc = acc + rq[p].astype(F32)
    proj_out[...] = acc.astype(BF)

    lax.fori_loop(1, nt, wr5, 0)
    hidden_out[...] = hgf[...]

    wr4()
    for k in range(RCAP):
        step_out[k] = (recv4[owner_of[k]].astype(F32) * used[k]).astype(BF)

    ws1()
    ws3()
    ws4()
    wcopy.wait_send()
    gcopy.wait_send()
    ccopy.wait_send()

    def ws_t(k, _):
        p = ten(k)
        gather(p, t).wait_send()
        hcopy(p, t).wait_send()
        fcopy(p, t).wait_send()
        return 0

    lax.fori_loop(1, nt, ws_t, 0)

    def ws_q(k, _):
        qcopy(lax.rem(z + k, 8), z).wait_send()
        return 0

    lax.fori_loop(1, 8, ws_q, 0)


def routed_kernel(
    tab, master, first, second, acts, grads,
    proj_out, hidden_out, step_out,
    strip, blk, mv, gv, fv, sv, av,
    send1, recv10, recv11, aold, wf, gq, gsend, grecv, gown, gsend0, grecv0, gown0, pk, pown, cp, qs, qr,
    hgs, hgr, hxs, hxr, hown, send5, hgf,
    ab0, pool0, xa0, fa0, sa0, sb0, xs0, xr0,
    ab1, pool1, xa1, fa1, sa1, sb1, xs1, xr1,
    ab2, pool2, xa2, fa2, sa2, sb2, xs2, xr2,
    lsem, ss1, rs1, ss2, rs2, xss, xrs, ssq, rsq, ssh, rsh, ss5, rs5, rss, rsr,
):
    ns, nt = 16, 8
    s = lax.axis_index("section")
    t = lax.axis_index("tensor")
    d = lax.axis_index("dp")
    z, c = s // 2, s % 2
    y, xl = t // 2, t % 2
    od, oc, tx = 1 - d, 1 - c, y * 2 + (1 - xl)
    core_peer = (z * 2 + oc, t, d)
    dp_peer = (s, t, od)
    x_peer = (s, tx, d)

    def sec(k):
        return lax.rem(s + k, ns)

    def ten(k):
        return lax.rem(t + k, nt)

    def ypeer(k):
        return lax.rem(y + k, 4)

    def chip(k):
        return lax.rem(z + k, 8)

    def remote(src, dst, sends, recvs, device):
        return pltpu.make_async_remote_copy(
            src_ref=src, dst_ref=dst, send_sem=sends, recv_sem=recvs,
            device_id=device, device_id_type=MESH)

    trow = pl.multiple_of(t * 128, 128)
    xrow = pl.multiple_of(tx * 128, 128)
    locals_ = [
        pltpu.make_async_copy(acts.at[pl.ds(trow, 128)], strip, lsem.at[0]),
        pltpu.make_async_copy(master, mv, lsem.at[1]),
        pltpu.make_async_copy(first, fv, lsem.at[3]),
        pltpu.make_async_copy(second, sv, lsem.at[4]),
        pltpu.make_async_copy(grads, gv, lsem.at[2]),
        pltpu.make_async_copy(acts, av, lsem.at[5]),
    ]
    for cpy in locals_:
        cpy.start()

    bar = pltpu.get_barrier_semaphore()
    for k in range(1, ns):
        pl.semaphore_signal(bar, inc=1, device_id=(sec(k), t, d), device_id_type=MESH)
    for k in range(1, nt):
        pl.semaphore_signal(bar, inc=1, device_id=(s, ten(k), d), device_id_type=MESH)
    pl.semaphore_signal(bar, inc=1, device_id=dp_peer, device_id_type=MESH)

    locals_[0].wait()
    for k in range(RCAP):
        blk[k] = strip[:, pl.ds(k * 128, 128)]
    for o in range(ns):
        both = blk[tab[o]]
        for h in range(2):
            send1[h, o] = both[h * 64:(h + 1) * 64]
    locals_[1].wait()
    for b in range(BLOCKS):
        wf[d, pl.ds(b * 128, 128)] = mv[pl.ds(b * 128, 128)].astype(BF)

    pl.semaphore_wait(bar, ns - 1 + nt - 1 + 1)

    parts = [
        (ab0, pool0, xa0, fa0, sa0, sb0, xs0, xr0),
        (ab1, pool1, xa1, fa1, sa1, sb1, xs1, xr1),
        (ab2, pool2, xa2, fa2, sa2, sb2, xs2, xr2),
    ]

    def swap_copy(u):
        ab_, pool_ = parts[u][:2]
        return remote(ab_.at[oc], pool_.at[pl.ds(c * BLOCKS, BLOCKS)], rss.at[u, 0], rsr.at[u, 0], core_peer)

    def enter(u):
        ab_, pool_ = parts[u][:2]
        swap_copy(u).start()
        for b in range(BLOCKS):
            pool_[c * BLOCKS + b] = ab_[c, b]

    def copy_a(u, p, o):
        return remote(parts[u][4].at[p], parts[u][2].at[o], rss.at[u, 1 + p], rsr.at[u, 1 + o], (p * 2 + c, t, d))

    def copy_b(u, p, o):
        return remote(parts[u][5].at[p], parts[u][3].at[o], rss.at[u, 9 + p], rsr.at[u, 9 + o], (p * 2 + c, t, d))

    def copy_n(u, j):
        p = chip(1 if j == 0 else 7)
        return remote(parts[u][5].at[8 + j], parts[u][3].at[28 + j], rss.at[u, 17 + j], rsr.at[u, 17 + j], (p * 2 + c, t, d))

    order = (4, 3, 5, 2, 6, 1, 7)

    def round_a(u):
        _, pool_, xa_, _, sa_, _, _, _ = parts[u]
        swap_copy(u).wait_recv()
        for k in order:
            m = chip(k)
            sa_[m] = pool_[tab[56 + m]]
            copy_a(u, m, z).start()
        for l in range(12):
            xa_[8 + l] = pool_[l]
        xa_[z] = jnp.zeros(xa_.shape[1:], BF)

    def round_b(u):
        _, pool_, xa_, fa_, _, sb_, _, _ = parts[u]
        for k in order:
            m = chip(k)
            copy_a(u, m, m).wait_recv()
        for k in order:
            m = chip(k)
            sb_[m] = xa_[tab[64 + m]]
            copy_b(u, m, z).start()
        for j in range(2):
            sb_[8 + j] = xa_[tab[72 + j]]
            copy_n(u, j).start()
        for l in range(20):
            fa_[8 + l] = xa_[l]
        fa_[z] = jnp.zeros(fa_.shape[1:], BF)
        fa_[30] = jnp.zeros(fa_.shape[1:], BF)

    def back_copy(u):
        return remote(parts[u][6], parts[u][7], rss.at[u, 19], rsr.at[u, 19], core_peer)

    def arrive(u):
        _, _, _, fa_, _, _, xs_, _ = parts[u]
        for k in order:
            m = chip(k)
            copy_b(u, m, m).wait_recv()
        for j in range(2):
            copy_n(u, j).wait_recv()
        for k in range(RCAP):
            xs_[k] = fa_[tab[80 + oc * 8 + k]]
        back_copy(u).start()

    def drain(u):
        swap_copy(u).wait_send()
        back_copy(u).wait_send()
        for k in order:
            copy_a(u, chip(k), z).wait_send()
            copy_b(u, chip(k), z).wait_send()
        for j in range(2):
            copy_n(u, j).wait_send()

    def step_of(f0, s0, own, other):
        g = own + other.astype(F32)
        f1 = 0.9 * f0 + 0.1 * g
        s1 = 0.999 * s0 + 0.001 * g * g
        return (f1 / (jnp.sqrt(s1 / CORR_SECOND) + 1e-08)).astype(BF)

    recv1 = (recv10, recv11)

    def acopy(h, p, o):
        return remote(send1.at[h, p], recv1[h].at[o], ss1.at[h, p], rs1.at[h, o], (p, t, d))

    def go1(h):
        def go(k, _):
            acopy(h, sec(k), s).start()
            return 0

        lax.fori_loop(1, ns, go, 0)

    def weights(h):
        rows = wf.at[d, pl.ds(h * 384, 384)]
        return remote(rows, rows, xss.at[5 + h], xrs.at[5 + h], dp_peer)

    go1(0)
    weights(0).start()
    go1(1)
    for h in range(2):
        recv1[h][s] = send1[h, s]

    locals_[2].wait()
    locals_[3].wait()
    for b in range(BLOCKS):
        rows = pl.ds(b * 128, 128)
        for j in range(2):
            ab0[j, b, pl.ds(0, 128)] = fv[rows, pl.ds(j * 256, 128)].astype(BF)
            ab0[j, b, pl.ds(128, 128)] = sv[rows, pl.ds(j * 256, 128)].astype(BF)
    enter(0)

    locals_[4].wait()
    for u in range(2):
        for j in range(2):
            src = j * 256 + u * 128
            for h in range(2):
                gq[h, u, :, pl.ds(j * 128, 128)] = gv[:, pl.ds(h * 512 + src, 128)]

    nt_dims = (((1,), (1,)), ((), ()))
    tn = (((0,), (0,)), ((), ()))
    locals_[5].wait()

    def grad_here(r, h):
        return lax.dot_general(
            av[:, pl.ds(r * 256, 256)], gq[h, 0], tn, preferred_element_type=F32) * (1.0 / 2048.0)

    for r in range(4):
        gsend0[pl.ds(r * 256, 256)] = grad_here(r, od).astype(BF)
        gown0[pl.ds(r * 256, 256)] = grad_here(r, d)
    gcopy0 = remote(gsend0, grecv0, xss.at[1], xrs.at[1], dp_peer)

    def wr1(h):
        def wait(k, _):
            p = sec(k)
            acopy(h, p, p).wait_recv()
            return 0

        lax.fori_loop(1, ns, wait, 0)

    def piece(h, sends, owner, device):
        rows = aold.at[pl.ds(pl.multiple_of(owner * 128 + h * 64, 64), 64)]
        return remote(rows, rows, ss2.at[h, sends], rs2.at[h, owner], device)

    up, down = ypeer(1), ypeer(3)

    def at_y(q):
        return (s, q * 2 + xl, d)

    for h in range(2):
        wr1(h)
        for b in range(BLOCKS):
            aold[pl.ds(pl.multiple_of(t * 128 + h * 64, 64), 64), pl.ds(b * 128, 128)] = recv1[h][tab[48 + b]]
        piece(h, 0, t, x_peer).start()
        piece(h, 1, t, at_y(up)).start()
        piece(h, 2, t, at_y(down)).start()
        if h == 1:
            round_a(0)
        piece(h, 0, tx, x_peer).wait_recv()
        piece(h, 3, tx, at_y(up)).start()
        piece(h, 4, tx, at_y(down)).start()
        if h == 0:
            weights(1).start()
        piece(h, 0, up * 2 + xl, x_peer).wait_recv()
        piece(h, 5, up * 2 + xl, at_y(down)).start()
        piece(h, 0, down * 2 + (1 - xl), x_peer).wait_recv()
        piece(h, 6, down * 2 + (1 - xl), at_y(up)).start()

    for h in range(2):
        weights(h).wait_recv()

    def hcopy(i, o):
        return remote(hgs.at[i], hgr.at[o], ssh.at[i], rsh.at[o], (s, i * 2 + xl, d))

    def hid(i):
        row = pl.multiple_of(i * 256, 256)
        r = lax.dot_general(gv[pl.ds(row, 256), pl.ds(0, 512)], wf[0], nt_dims, preferred_element_type=F32)
        return r + lax.dot_general(gv[pl.ds(row, 256), pl.ds(512, 512)], wf[1], nt_dims, preferred_element_type=F32)

    def hid_y(k, _):
        i = ypeer(k)
        r = hid(i).astype(BF)
        for x in range(2):
            hgs[i, x] = r[x * 128:(x + 1) * 128]
        hcopy(i, y).start()
        return 0

    lax.fori_loop(1, 4, hid_y, 0)
    r = hid(y)
    for x in range(2):
        hown[x] = r[x * 128:(x + 1) * 128]
    far = ypeer(2)
    for h in range(2):
        piece(h, 0, down * 2 + xl, x_peer).wait_recv()
        piece(h, 0, up * 2 + (1 - xl), x_peer).wait_recv()
        piece(h, 0, far * 2 + xl, x_peer).wait_recv()
        piece(h, 0, far * 2 + (1 - xl), x_peer).wait_recv()

    def grad_tile(r, h):
        return lax.dot_general(
            aold[:, pl.ds(r * 256, 256)], gq[h, 1], tn, preferred_element_type=F32) * (1.0 / 2048.0)

    for r in range(3):
        gsend[pl.ds(r * 256, 256)] = grad_tile(r, od).astype(BF)
    gcopy = remote(gsend, grecv, xss.at[2], xrs.at[2], dp_peer)
    gcopy.start()
    round_b(0)

    def proj_tile(i, _):
        a = aold[pl.ds(pl.multiple_of(i * 256, 256), 256)]
        for h in range(2):
            r = jnp.dot(a, wf[h], preferred_element_type=F32)
            cols = pl.ds(h * 512, 512)
            for j in range(2):
                lo, hi = r[j * 128:j * 128 + 64], r[j * 128 + 64:j * 128 + 128]
                pk[i * 2 + j, :, cols] = jnp.where(c == 0, hi, lo).astype(BF)
                pown[i * 2 + j, :, cols] = jnp.where(c == 0, lo, hi)
        return 0

    lax.fori_loop(0, 4, proj_tile, 0)
    ccopy = remote(pk, cp, xss.at[3], xrs.at[3], core_peer)
    ccopy.start()

    for r in range(3):
        gown[pl.ds(r * 256, 256)] = grad_tile(r, d)

    ccopy.wait_recv()

    lo, hi = pl.ds(0, 32), pl.ds(32, 32)

    def ring(n, way):
        rows = pl.ds(0, 64) if n > 1 else (lo if way == 0 else hi)
        return remote(
            qs.at[way, n - 1, rows], qr.at[way, n - 1, rows], ssq.at[way, n - 1], rsq.at[way, n - 1],
            (chip(1 if way == 0 else 7) * 2 + c, t, d))

    def partial_(p, rows):
        return pown[p, rows] + cp[p, rows].astype(F32)

    def ring_step(n):
        for way in range(2):
            p = chip(5 - n if way == 0 else n + 3)
            first_rows, other_rows = (lo, hi) if way == 0 else (hi, lo)
            if n > 1:
                ring(n - 1, way).wait_recv()
            if n == 1:
                qs[way, 0, first_rows] = partial_(p, first_rows).astype(BF)
            elif n == 2:
                qs[way, 1, first_rows] = (partial_(p, first_rows) + qr[way, 0, first_rows].astype(F32)).astype(BF)
                qs[way, 1, other_rows] = partial_(p, other_rows).astype(BF)
            else:
                qs[way, n - 1] = (partial_(p, pl.ds(0, 64)) + qr[way, n - 2].astype(F32)).astype(BF)
            ring(n, way).start()

    def adam():
        gcopy.wait_recv()
        for b in range(BLOCKS):
            rows = pl.ds(b * 128, 128)
            for j in range(2):
                cols = pl.ds(j * 256 + 128, 128)
                here = pl.ds(j * 128, 128)
                ab1[j, b] = step_of(fv[rows, cols], sv[rows, cols], gown[rows, here], grecv[rows, here])
        enter(1)

    def place_mine():
        back_copy(0).wait_recv()
        gcopy0.wait_recv()
        for k in range(RCAP):
            used = tab[40 + k].astype(F32)
            rows = pl.ds(k * 128, 128)
            for j in range(2):
                both = fa0[tab[80 + c * 8 + k]] if j == 0 else xr0[k]
                half = c if j == 0 else oc
                here = pl.ds(pl.multiple_of(half * 128, 128), 128)
                st = step_of(both[:128].astype(F32), both[128:].astype(F32), gown0[rows, here], grecv0[rows, here])
                step_out[k, :, pl.ds(pl.multiple_of(half * 256, 128), 128)] = (st.astype(F32) * used).astype(BF)

    def place(u):
        fa_, xr_ = parts[u][3], parts[u][7]
        back_copy(u).wait_recv()
        mine = pl.ds(pl.multiple_of(c * 256 + u * 128, 128), 128)
        theirs = pl.ds(pl.multiple_of(oc * 256 + u * 128, 128), 128)
        for k in range(RCAP):
            step_out[k, :, mine] = fa_[tab[80 + c * 8 + k]]
            step_out[k, :, theirs] = xr_[k]

    ring_step(1)
    adam()
    gcopy0.start()
    ring_step(2)
    round_a(1)
    ring_step(3)

    for k in range(1, 4):
        p = ypeer(k)
        hcopy(p, p).wait_recv()
    for x in range(2):
        total = hown[x]
        for k in range(1, 4):
            total = total + hgr[ypeer(k), x].astype(F32)
        hown[x] = total
    hxs[...] = hown[1 - xl].astype(BF)
    hx = remote(hxs, hxr, xss.at[4], xrs.at[4], x_peer)
    hx.start()
    ring_step(4)
    hx.wait_recv()
    hsum = hown[xl] + hxr[...].astype(F32)
    for b in range(BLOCKS):
        piece_ = hsum[:, b * 128:(b + 1) * 128].astype(BF)
        for j in range(2):
            ab2[j, b] = piece_[j * 64:(j + 1) * 64]
    enter(2)
    round_a(2)
    arrive(0)
    round_b(2)
    round_b(1)
    place_mine()
    arrive(2)

    back_copy(2).wait_recv()
    mine = pl.ds(pl.multiple_of(c * 64, 64), 64)
    theirs = pl.ds(pl.multiple_of(oc * 64, 64), 64)
    for k in range(RCAP):
        send5[k, mine] = fa2[tab[80 + c * 8 + k]]
        send5[k, theirs] = xr2[k]

    def fcopy(p, o):
        rows = pl.ds(pl.multiple_of(o * 128, 128), 128)
        return remote(send5.at[p], hgf.at[rows], ss5.at[p], rs5.at[o], (s, p, d))

    def go5(k, _):
        fcopy(ten(k), t).start()
        return 0

    lax.fori_loop(1, nt, go5, 0)
    hgf[pl.ds(trow, 128)] = send5[t]
    arrive(1)

    for way in range(2):
        ring(4, way).wait_recv()
    proj_out[...] = (partial_(z, pl.ds(0, 64)) + qr[0, 3].astype(F32) + qr[1, 3].astype(F32)).astype(BF)

    place(1)

    def wr5(k, _):
        p = ten(k)
        fcopy(p, p).wait_recv()
        return 0

    lax.fori_loop(1, nt, wr5, 0)
    hidden_out[...] = hgf[...]

    for u in range(3):
        drain(u)
    for cpy in (gcopy0, gcopy, ccopy, hx):
        cpy.wait_send()
    for h in range(2):
        weights(h).wait_send()
        for i in range(7):
            piece(h, i, t, x_peer).wait_send()

        def ws(k, _):
            acopy(h, sec(k), s).wait_send()
            return 0

        lax.fori_loop(1, ns, ws, 0)
    for k in range(1, 4):
        hcopy(ypeer(k), y).wait_send()
    for n in range(1, 5):
        for way in range(2):
            ring(n, way).wait_send()

    def ws5(k, _):
        fcopy(ten(k), t).wait_send()
        return 0

    lax.fori_loop(1, nt, ws5, 0)


def finish(proj, hidden, step, proj_out, hidden_out, step_out):
    proj_out[...] = proj[...]
    hidden_out[...] = hidden[...]
    for k in range(RCAP):
        step_out[pl.ds(k * 128, 128)] = step[k].astype(F32)


def shards(old_master, old_first, old_second, dest_section, dest_offset, hidden_acts, out_grad):
    any_ = pl.BlockSpec(memory_space=pl.ANY)
    smem = pl.BlockSpec(memory_space=pltpu.SMEM)
    vmem = pl.BlockSpec(memory_space=pltpu.VMEM)
    V = pltpu.VMEM
    dma = pltpu.SemaphoreType.DMA
    tab, ok = pl.pallas_call(
        plan,
        out_shape=(jax.ShapeDtypeStruct((128,), jnp.int32), jax.ShapeDtypeStruct((1,), jnp.int32)),
        in_specs=[smem, smem],
        out_specs=(smem, smem),
        scratch_shapes=[pltpu.SMEM((256,), jnp.int32), pltpu.SMEM((128,), jnp.int32)],
        name="plan",
    )(dest_section, dest_offset)
    out_shape = (
        jax.ShapeDtypeStruct((64, 1024), BF),
        jax.ShapeDtypeStruct((1024, 128), BF),
        jax.ShapeDtypeStruct((8, 128, 512), BF),
    )

    def call(body, scratch, number, name):
        return pl.pallas_call(
            body,
            out_shape=out_shape,
            in_specs=[smem, any_, any_, any_, any_, any_],
            out_specs=(vmem, vmem, vmem),
            scratch_shapes=scratch,
            compiler_params=pltpu.CompilerParams(
                collective_id=number, has_side_effects=True, vmem_limit_bytes=58 * 2**20),
            name=name,
        )

    padded = call(padded_kernel, [
        V((128, 1024), BF), V((8, 128, 128), BF), V((768, 512), F32), V((1024, 1024), BF), V((768, 512), F32), V((768, 512), F32),
        V((16, 128, 128), BF), V((16, 128, 128), BF), V((1024, 768), BF), V((2, 768, 512), BF),
        V((768, 512), BF), V((768, 512), BF), V((768, 512), F32),
        V((8, 64, 1024), BF), V((8, 64, 1024), F32), V((8, 64, 1024), BF), V((8, 64, 1024), BF), V((8, 64, 1024), BF),
        V((8, 128, 768), BF), V((8, 128, 768), BF), V((6, 128, 128), BF), V((16, 128, 128), BF), V((16, 128, 128), BF),
        V((8, 128, 128), BF), V((1024, 128), BF), V((6, 128, 512), BF), V((16, 128, 512), BF), V((16, 128, 512), BF),
        dma((5,)), dma((16,)), dma((16,)), dma((8,)), dma((8,)), dma((3,)), dma((3,)), dma((8,)), dma((8,)),
        dma((8,)), dma((8,)), dma((16,)), dma((16,)), dma((8,)), dma((8,)), dma((16,)), dma((16,)),
    ], 0, "padded")


    def buffers(rows):
        shapes = ((2, 6), (12,), (20,), (31,), (8,), (10,), (8,), (8,))
        return [V((*n, rows, 128), BF) for n in shapes]

    routed = call(routed_kernel, [
        V((128, 1024), BF), V((8, 128, 128), BF), V((768, 512), F32), V((1024, 1024), BF), V((768, 512), F32), V((768, 512), F32), V((1024, 1024), BF),
        V((2, 16, 64, 128), BF), V((16, 64, 128), BF), V((16, 64, 128), BF), V((1024, 768), BF), V((2, 768, 512), BF),
        V((2, 2, 1024, 256), BF), V((768, 256), BF), V((768, 256), BF), V((768, 256), F32),
        V((1024, 256), BF), V((1024, 256), BF), V((1024, 256), F32),
        V((8, 64, 1024), BF), V((8, 64, 1024), F32), V((8, 64, 1024), BF), V((2, 4, 64, 1024), BF), V((2, 4, 64, 1024), BF),
        V((4, 2, 128, 768), BF), V((4, 2, 128, 768), BF), V((128, 768), BF), V((128, 768), BF), V((2, 128, 768), F32),
        V((8, 128, 128), BF), V((1024, 128), BF),
        *buffers(256), *buffers(128), *buffers(64),
        dma((6,)), dma((2, 16)), dma((2, 16)), dma((2, 8)), dma((2, 8)), dma((7,)), dma((7,)), dma((2, 4)), dma((2, 4)),
        dma((4,)), dma((4,)), dma((8,)), dma((8,)), dma((3, 20)), dma((3, 20)),
    ], 1, "routed")

    args = (tab, old_master, old_first, old_second, hidden_acts[0], out_grad[0])
    proj, hidden, step = lax.cond(ok[0] == 1, routed, padded, *args)
    proj, hidden, step = pl.pallas_call(
        finish,
        out_shape=(
            jax.ShapeDtypeStruct((64, 1024), BF),
            jax.ShapeDtypeStruct((1024, 128), BF),
            jax.ShapeDtypeStruct((1024, 512), F32),
        ),
        in_specs=[vmem] * 3,
        out_specs=(vmem, vmem, vmem),
        compiler_params=pltpu.CompilerParams(vmem_limit_bytes=32 * 2**20),
        name="finish",
    )(proj, hidden, step)
    return proj[None], hidden[None], step


def solution(mesh):
    placed = (
        P("section", ("tensor", "dp")),
        P("section", ("tensor", "dp")),
        P("section", ("tensor", "dp")),
        P(),
        P(),
        P("dp", None, "section"),
        P("dp", None, "tensor"),
    )
    return jax.shard_map(
        shards,
        mesh=mesh,
        in_specs=placed,
        out_specs=(
            P("dp", "section", "tensor"),
            P("dp", None, ("section", "tensor")),
            P("section", ("tensor", "dp")),
        ),
        check_vma=False,
    )
```

```python
import jax
import jax.numpy as jnp
from jax import lax
from jax.experimental import pallas as pl
from jax.experimental.pallas import tpu as pltpu
from jax.sharding import PartitionSpec as P

ROWS = 128
BLOCKS = 6
RCAP = 8
CORR_SECOND = 0.6323045752
MESH = pl.DeviceIdType.MESH
BF = jnp.bfloat16
F32 = jnp.float32


def plan(dest, off, tab, ok, route, late):
    s = lax.axis_index("section")
    z = s // 2
    for i in range(112):
        tab[i] = 30 if 80 <= i < 96 else (8 if 64 <= i < 74 else 0)
    ok[0] = 1

    def clear(i, _):
        for j in range(16):
            route[i * 16 + j] = -1
        return 0

    lax.fori_loop(0, 12, clear, 0)

    def near(a, p):
        k = jnp.bitwise_and(p - a, 7)
        return (k == 1) | (k == 7)

    def rank(a, n):
        count = jnp.int32(0)
        for i in range(12):
            g = a * 12 + i
            o = a * 2 + i // 6
            q = dest[g]
            k = off[g]
            here = q == s
            tab[jnp.where(here, o, 112)] = k
            tab[jnp.where(here, 32 + k, 113)] = o
            tab[jnp.where(here, 40 + k, 114)] = 1
            p = lax.shift_right_logical(q, 1)
            r = jnp.bitwise_and(lax.shift_right_logical(count, p * 4), 15)
            count = count + lax.shift_left(jnp.int32(1), p * 4)
            fits = (r < 2) | ((r == 2) & near(a, p)) | (a == p)
            route[jnp.where(fits & (a != p), r * 64 + a * 8 + p, 192)] = g
            late[n] = g
            n = n + jnp.where(fits, 0, 1)
        return n

    n_late = lax.fori_loop(0, 8, rank, jnp.int32(0))
    for b in range(BLOCKS):
        p = dest[s * BLOCKS + b]
        tab[16 + p] = b
        tab[48 + b] = p

    def detour(i, _):
        g = late[i]
        a, p = g // 12, dest[g] // 2
        best = jnp.int32(-1)
        for k in (4, 3, 5, 2, 6, 1, 7):
            m = jnp.bitwise_and(p + k, 7)
            am, mp = a * 8 + m, m * 8 + p
            last = jnp.where(route[64 + mp] < 0, 1, 0)
            if k in (1, 7):
                last = jnp.where((last == 0) & (route[128 + mp] < 0), 2, last)
            held = route[am]
            direct = lax.shift_right_logical(dest[jnp.maximum(held, 0)], 1) == m
            second = jnp.where(route[64 + am] < 0, 1, jnp.where(near(a, m) & (route[128 + am] < 0), 2, 3))
            move = jnp.where(held < 0, 0, jnp.where(direct, second, 3))
            good = (last > 0) & (move < 3) & (m != a)
            best = jnp.where(good, m * 16 + last * 4 + move, best)

        @pl.when(best >= 0)
        def _():
            m = best // 16
            am = a * 8 + m
            move = jnp.bitwise_and(best, 3)
            last = jnp.bitwise_and(best // 4, 3)
            route[jnp.where(move > 0, move * 64 + am, 192)] = route[am]
            route[am] = g
            route[last * 64 + m * 8 + p] = g

        @pl.when(best < 0)
        def _():
            ok[0] = 0

        return 0

    lax.fori_loop(0, n_late, detour, 0)

    for m in range(8):
        g = route[z * 8 + m]
        tab[56 + m] = jnp.where((g >= 0) & (z != m), g - 12 * z, 0)
    for j in range(10):
        if j < 8:
            g = route[64 + z * 8 + j]
        else:
            g = route[128 + z * 8 + jnp.bitwise_and(z + (1 if j == 8 else 7), 7)]
        a = jnp.maximum(g, 0) // 12
        from_pool = 8 + g - 12 * z
        tab[64 + j] = jnp.where(g < 0, 8, jnp.where(a == z, from_pool, a))

    def final(g, source):
        h = jnp.maximum(g, 0)
        p = dest[h]
        mine = (g >= 0) & (lax.shift_right_logical(p, 1) == z)
        tab[jnp.where(mine, 80 + jnp.bitwise_and(p, 1) * 8 + off[h], 115)] = source

    for a in range(8):
        final(route[a * 8 + z], 8 + a)
        final(route[64 + a * 8 + z], a)
    final(route[128 + jnp.bitwise_and(z + 7, 7) * 8 + z], 28)
    final(route[128 + jnp.bitwise_and(z + 1, 7) * 8 + z], 29)
    for l in range(12):
        final(12 * z + l, 16 + l)


def padded_kernel(
    tab, master, first, second, acts, grads,
    proj_out, hidden_out, step_out,
    strip, blk, mv, gv, fv, sv,
    send1, recv1, aold, wf, gsend, grecv, gown, pk, pown, cp, q, rq,
    hgs, hgr, hb, send3, recv3, send5, hgf, ab, send4, recv4,
    lsem, ss1, rs1, ss2, rs2, xss, xrs, ssq, rsq, ssh, rsh, ss3, rs3, ss5, rs5, ss4, rs4,
):
    ns, nt = 16, 8
    s = lax.axis_index("section")
    t = lax.axis_index("tensor")
    d = lax.axis_index("dp")
    z, c = s // 2, s % 2
    od = 1 - d
    core_peer = (z * 2 + (1 - c), t, d)
    dp_peer = (s, t, od)

    def sec(k):
        return lax.rem(s + k, ns)

    def ten(k):
        return lax.rem(t + k, nt)

    trow = pl.multiple_of(t * 128, 128)
    locals_ = [
        pltpu.make_async_copy(acts.at[pl.ds(trow, 128)], strip, lsem.at[0]),
        pltpu.make_async_copy(master, mv, lsem.at[1]),
        pltpu.make_async_copy(grads, gv, lsem.at[2]),
        pltpu.make_async_copy(first, fv, lsem.at[3]),
        pltpu.make_async_copy(second, sv, lsem.at[4]),
    ]
    for cpy in locals_:
        cpy.start()

    bar = pltpu.get_barrier_semaphore()
    for k in range(1, ns):
        pl.semaphore_signal(bar, inc=1, device_id=(sec(k), t, d), device_id_type=MESH)
    for k in range(1, nt):
        pl.semaphore_signal(bar, inc=1, device_id=(s, ten(k), d), device_id_type=MESH)
    pl.semaphore_signal(bar, inc=1, device_id=dp_peer, device_id_type=MESH)

    slot_of = [tab[o] for o in range(ns)]
    block_for = [tab[16 + p] for p in range(ns)]
    owner_of = [tab[32 + k] for k in range(RCAP)]
    used = [tab[40 + k].astype(F32) for k in range(RCAP)]
    mine = [tab[48 + b] for b in range(BLOCKS)]

    locals_[0].wait()
    for k in range(RCAP):
        blk[k] = strip[:, pl.ds(k * 128, 128)]
    for o in range(ns):
        send1[o] = blk[slot_of[o]]
    locals_[1].wait()
    for b in range(BLOCKS):
        wf[d, pl.ds(b * 128, 128)] = mv[pl.ds(b * 128, 128)].astype(BF)

    pl.semaphore_wait(bar, ns - 1 + nt - 1 + 1)

    def to_sections(src, dst, sends, recvs):
        def copy(p):
            return pltpu.make_async_remote_copy(
                src_ref=src.at[p], dst_ref=dst.at[s],
                send_sem=sends.at[p], recv_sem=recvs.at[s],
                device_id=(p, t, d), device_id_type=MESH)

        def go(k, _):
            copy(sec(k)).start()
            return 0

        def wait_send(k, _):
            copy(sec(k)).wait_send()
            return 0

        def wait_recv(k, _):
            p = sec(k)
            pltpu.make_async_remote_copy(
                src_ref=src.at[p], dst_ref=dst.at[p],
                send_sem=sends.at[p], recv_sem=recvs.at[p],
                device_id=(p, t, d), device_id_type=MESH).wait_recv()
            return 0

        return (
            lambda: lax.fori_loop(1, ns, go, 0),
            lambda: lax.fori_loop(1, ns, wait_send, 0),
            lambda: lax.fori_loop(1, ns, wait_recv, 0),
        )

    go1, ws1, wr1 = to_sections(send1, recv1, ss1, rs1)
    go1()
    wcopy = pltpu.make_async_remote_copy(
        src_ref=wf.at[d], dst_ref=wf.at[d], send_sem=xss.at[0], recv_sem=xrs.at[0],
        device_id=dp_peer, device_id_type=MESH)
    wcopy.start()
    recv1[s] = send1[s]
    wr1()
    for b in range(BLOCKS):
        aold[pl.ds(trow, 128), pl.ds(b * 128, 128)] = recv1[mine[b]]

    def gather(p, q_):
        row = pl.multiple_of(q_ * 128, 128)
        return pltpu.make_async_remote_copy(
            src_ref=aold.at[pl.ds(row, 128)], dst_ref=aold.at[pl.ds(row, 128)],
            send_sem=ss2.at[p], recv_sem=rs2.at[q_],
            device_id=(s, p, d), device_id_type=MESH)

    def go2(k, _):
        gather(ten(k), t).start()
        return 0

    def wr2(k, _):
        p = ten(k)
        gather(p, p).wait_recv()
        return 0

    lax.fori_loop(1, nt, go2, 0)
    locals_[2].wait()
    lax.fori_loop(1, nt, wr2, 0)

    tn = (((0,), (0,)), ((), ()))
    nt_dims = (((1,), (1,)), ((), ()))

    def grad_tile(r, half):
        cols = pl.ds(pl.multiple_of(half * 512, 512), 512)
        return lax.dot_general(
            aold[:, pl.ds(r * 256, 256)], gv[:, cols], tn, preferred_element_type=F32
        ) * (1.0 / 2048.0)

    for r in range(3):
        gsend[pl.ds(r * 256, 256)] = grad_tile(r, od).astype(BF)
    gcopy = pltpu.make_async_remote_copy(
        src_ref=gsend, dst_ref=grecv, send_sem=xss.at[1], recv_sem=xrs.at[1],
        device_id=dp_peer, device_id_type=MESH)
    gcopy.start()

    wcopy.wait_recv()

    def proj_tile(i, _):
        row = pl.multiple_of(i * 128, 128)
        a = aold[pl.ds(row, 128)]
        for h in range(2):
            r = jnp.dot(a, wf[h], preferred_element_type=F32)
            cols = pl.ds(h * 512, 512)
            lo, hi = r[:64], r[64:]
            pk[i, :, cols] = jnp.where(c == 0, hi, lo).astype(BF)
            pown[i, :, cols] = jnp.where(c == 0, lo, hi)
        return 0

    lax.fori_loop(0, nt, proj_tile, 0)
    ccopy = pltpu.make_async_remote_copy(
        src_ref=pk, dst_ref=cp, send_sem=xss.at[2], recv_sem=xrs.at[2],
        device_id=core_peer, device_id_type=MESH)
    ccopy.start()

    def hid(i):
        row = pl.multiple_of(i * 128, 128)
        r = lax.dot_general(gv[pl.ds(row, 128), pl.ds(0, 512)], wf[0], nt_dims, preferred_element_type=F32)
        return r + lax.dot_general(gv[pl.ds(row, 128), pl.ds(512, 512)], wf[1], nt_dims, preferred_element_type=F32)

    def hcopy(p, q_):
        return pltpu.make_async_remote_copy(
            src_ref=hgs.at[p], dst_ref=hgr.at[q_], send_sem=ssh.at[p], recv_sem=rsh.at[q_],
            device_id=(s, p, d), device_id_type=MESH)

    def go_h(k, _):
        p = ten(k)
        hgs[p] = hid(p).astype(BF)
        hcopy(p, t).start()
        return 0

    lax.fori_loop(1, nt, go_h, 0)
    hown = hid(t)
    for b in range(BLOCKS):
        hgr[t, :, pl.ds(b * 128, 128)] = hown[:, b * 128:(b + 1) * 128].astype(BF)

    for r in range(3):
        gown[pl.ds(r * 256, 256)] = grad_tile(r, d)

    ccopy.wait_recv()

    def qcopy(p, q_):
        return pltpu.make_async_remote_copy(
            src_ref=q.at[p], dst_ref=rq.at[q_], send_sem=ssq.at[p], recv_sem=rsq.at[q_],
            device_id=(p * 2 + c, t, d), device_id_type=MESH)

    def go_q(k, _):
        p = lax.rem(z + k, 8)
        q[p] = (pown[p] + cp[p].astype(F32)).astype(BF)
        qcopy(p, z).start()
        return 0

    lax.fori_loop(1, 8, go_q, 0)
    rq[z] = (pown[z] + cp[z].astype(F32)).astype(BF)

    locals_[3].wait()
    locals_[4].wait()
    gcopy.wait_recv()
    for b in range(BLOCKS):
        rows = pl.ds(b * 128, 128)
        g = gown[rows] + grecv[rows].astype(F32)
        f1 = 0.9 * fv[rows] + 0.1 * g
        s1 = 0.999 * sv[rows] + 0.001 * g * g
        ab[b] = (f1 / (jnp.sqrt(s1 / CORR_SECOND) + 1e-08)).astype(BF)
    go4, ws4, wr4 = to_sections(send4, recv4, ss4, rs4)
    for p in range(ns):
        send4[p] = ab[block_for[p]]
    go4()
    recv4[s] = send4[s]

    def wr_h(k, _):
        p = ten(k)
        hcopy(p, p).wait_recv()
        return 0

    lax.fori_loop(1, nt, wr_h, 0)
    for b in range(BLOCKS):
        acc = hgr[0, :, pl.ds(b * 128, 128)].astype(F32)
        for p in range(1, nt):
            acc = acc + hgr[p, :, pl.ds(b * 128, 128)].astype(F32)
        hb[b] = acc.astype(BF)
    for p in range(ns):
        send3[p] = hb[block_for[p]]
    go3, ws3, wr3 = to_sections(send3, recv3, ss3, rs3)
    go3()
    recv3[s] = send3[s]
    wr3()
    for k in range(RCAP):
        send5[k] = (recv3[owner_of[k]].astype(F32) * used[k]).astype(BF)

    def fcopy(p, q_):
        row = pl.multiple_of(q_ * 128, 128)
        return pltpu.make_async_remote_copy(
            src_ref=send5.at[p], dst_ref=hgf.at[pl.ds(row, 128)], send_sem=ss5.at[p], recv_sem=rs5.at[q_],
            device_id=(s, p, d), device_id_type=MESH)

    def go5(k, _):
        fcopy(ten(k), t).start()
        return 0

    def wr5(k, _):
        p = ten(k)
        fcopy(p, p).wait_recv()
        return 0

    lax.fori_loop(1, nt, go5, 0)
    hgf[pl.ds(trow, 128)] = send5[t]

    def wr_q(k, _):
        p = lax.rem(z + k, 8)
        qcopy(p, p).wait_recv()
        return 0

    lax.fori_loop(1, 8, wr_q, 0)
    acc = rq[0].astype(F32)
    for p in range(1, 8):
        acc = acc + rq[p].astype(F32)
    proj_out[...] = acc.astype(BF)

    lax.fori_loop(1, nt, wr5, 0)
    hidden_out[...] = hgf[...]

    wr4()
    for k in range(RCAP):
        step_out[k] = (recv4[owner_of[k]].astype(F32) * used[k]).astype(BF)

    ws1()
    ws3()
    ws4()
    wcopy.wait_send()
    gcopy.wait_send()
    ccopy.wait_send()

    def ws_t(k, _):
        p = ten(k)
        gather(p, t).wait_send()
        hcopy(p, t).wait_send()
        fcopy(p, t).wait_send()
        return 0

    lax.fori_loop(1, nt, ws_t, 0)

    def ws_q(k, _):
        qcopy(lax.rem(z + k, 8), z).wait_send()
        return 0

    lax.fori_loop(1, 8, ws_q, 0)


def routed_kernel(
    tab, master, first, second, acts, grads,
    proj_out, hidden_out, step_out,
    strip, blk, mv, gv, fv, sv, av,
    send1, recv10, recv11, aold, wf, gq, gsend, grecv, gown, gsend0, grecv0, gown0, pk, pown, cp, qs, qr,
    hgs, hgr, hxs, hxr, hown, send5, hgf,
    ab0, pool0, xa0, fa0, sa0, sb0, xs0, xr0,
    ab1, pool1, xa1, fa1, sa1, sb1, xs1, xr1,
    ab2, pool2, xa2, fa2, sa2, sb2, xs2, xr2,
    lsem, ss1, rs1, ss2, rs2, xss, xrs, ssq, rsq, ssh, rsh, ss5, rs5, rss, rsr,
):
    ns, nt = 16, 8
    s = lax.axis_index("section")
    t = lax.axis_index("tensor")
    d = lax.axis_index("dp")
    z, c = s // 2, s % 2
    y, xl = t // 2, t % 2
    od, oc, tx = 1 - d, 1 - c, y * 2 + (1 - xl)
    core_peer = (z * 2 + oc, t, d)
    dp_peer = (s, t, od)
    x_peer = (s, tx, d)

    def sec(k):
        return lax.rem(s + k, ns)

    def ten(k):
        return lax.rem(t + k, nt)

    def ypeer(k):
        return lax.rem(y + k, 4)

    def chip(k):
        return lax.rem(z + k, 8)

    def remote(src, dst, sends, recvs, device):
        return pltpu.make_async_remote_copy(
            src_ref=src, dst_ref=dst, send_sem=sends, recv_sem=recvs,
            device_id=device, device_id_type=MESH)

    trow = pl.multiple_of(t * 128, 128)
    xrow = pl.multiple_of(tx * 128, 128)
    locals_ = [
        pltpu.make_async_copy(acts.at[pl.ds(trow, 128)], strip, lsem.at[0]),
        pltpu.make_async_copy(master, mv, lsem.at[1]),
        pltpu.make_async_copy(first, fv, lsem.at[3]),
        pltpu.make_async_copy(second, sv, lsem.at[4]),
        pltpu.make_async_copy(grads, gv, lsem.at[2]),
        pltpu.make_async_copy(acts, av, lsem.at[5]),
    ]
    for cpy in locals_:
        cpy.start()

    bar = pltpu.get_barrier_semaphore()
    for k in range(1, ns):
        pl.semaphore_signal(bar, inc=1, device_id=(sec(k), t, d), device_id_type=MESH)
    for k in range(1, nt):
        pl.semaphore_signal(bar, inc=1, device_id=(s, ten(k), d), device_id_type=MESH)
    pl.semaphore_signal(bar, inc=1, device_id=dp_peer, device_id_type=MESH)

    locals_[0].wait()
    for k in range(RCAP):
        blk[k] = strip[:, pl.ds(k * 128, 128)]
    for o in range(ns):
        both = blk[tab[o]]
        for h in range(2):
            send1[h, o] = both[h * 64:(h + 1) * 64]
    locals_[1].wait()
    for b in range(BLOCKS):
        wf[d, pl.ds(b * 128, 128)] = mv[pl.ds(b * 128, 128)].astype(BF)

    pl.semaphore_wait(bar, ns - 1 + nt - 1 + 1)

    parts = [
        (ab0, pool0, xa0, fa0, sa0, sb0, xs0, xr0),
        (ab1, pool1, xa1, fa1, sa1, sb1, xs1, xr1),
        (ab2, pool2, xa2, fa2, sa2, sb2, xs2, xr2),
    ]

    def swap_copy(u):
        ab_, pool_ = parts[u][:2]
        return remote(ab_.at[oc], pool_.at[pl.ds(c * BLOCKS, BLOCKS)], rss.at[u, 0], rsr.at[u, 0], core_peer)

    def enter(u):
        ab_, pool_ = parts[u][:2]
        swap_copy(u).start()
        for b in range(BLOCKS):
            pool_[c * BLOCKS + b] = ab_[c, b]

    def copy_a(u, p, o):
        return remote(parts[u][4].at[p], parts[u][2].at[o], rss.at[u, 1 + p], rsr.at[u, 1 + o], (p * 2 + c, t, d))

    def copy_b(u, p, o):
        return remote(parts[u][5].at[p], parts[u][3].at[o], rss.at[u, 9 + p], rsr.at[u, 9 + o], (p * 2 + c, t, d))

    def copy_n(u, j):
        p = chip(1 if j == 0 else 7)
        return remote(parts[u][5].at[8 + j], parts[u][3].at[28 + j], rss.at[u, 17 + j], rsr.at[u, 17 + j], (p * 2 + c, t, d))

    order = (4, 3, 5, 2, 6, 1, 7)

    def round_a(u):
        _, pool_, xa_, _, sa_, _, _, _ = parts[u]
        swap_copy(u).wait_recv()
        for k in order:
            m = chip(k)
            sa_[m] = pool_[tab[56 + m]]
            copy_a(u, m, z).start()
        for l in range(12):
            xa_[8 + l] = pool_[l]
        xa_[z] = jnp.zeros(xa_.shape[1:], BF)

    def round_b(u):
        _, pool_, xa_, fa_, _, sb_, _, _ = parts[u]
        for k in order:
            m = chip(k)
            copy_a(u, m, m).wait_recv()
        for k in order:
            m = chip(k)
            sb_[m] = xa_[tab[64 + m]]
            copy_b(u, m, z).start()
        for j in range(2):
            sb_[8 + j] = xa_[tab[72 + j]]
            copy_n(u, j).start()
        for l in range(20):
            fa_[8 + l] = xa_[l]
        fa_[z] = jnp.zeros(fa_.shape[1:], BF)
        fa_[30] = jnp.zeros(fa_.shape[1:], BF)

    def back_copy(u):
        return remote(parts[u][6], parts[u][7], rss.at[u, 19], rsr.at[u, 19], core_peer)

    def arrive(u):
        _, _, _, fa_, _, _, xs_, _ = parts[u]
        for k in order:
            m = chip(k)
            copy_b(u, m, m).wait_recv()
        for j in range(2):
            copy_n(u, j).wait_recv()
        for k in range(RCAP):
            xs_[k] = fa_[tab[80 + oc * 8 + k]]
        back_copy(u).start()

    def drain(u):
        swap_copy(u).wait_send()
        back_copy(u).wait_send()
        for k in order:
            copy_a(u, chip(k), z).wait_send()
            copy_b(u, chip(k), z).wait_send()
        for j in range(2):
            copy_n(u, j).wait_send()

    def step_of(f0, s0, own, other):
        g = own + other.astype(F32)
        f1 = 0.9 * f0 + 0.1 * g
        s1 = 0.999 * s0 + 0.001 * g * g
        return (f1 / (jnp.sqrt(s1 / CORR_SECOND) + 1e-08)).astype(BF)

    recv1 = (recv10, recv11)

    def acopy(h, p, o):
        return remote(send1.at[h, p], recv1[h].at[o], ss1.at[h, p], rs1.at[h, o], (p, t, d))

    def go1(h):
        for k in (4, 3, 5, 2, 6, 1, 7):
            for e in (c, oc):
                acopy(h, chip(k) * 2 + e, s).start()
        acopy(h, z * 2 + oc, s).start()

    def weights(h):
        rows = wf.at[d, pl.ds(h * 384, 384)]
        return remote(rows, rows, xss.at[5 + h], xrs.at[5 + h], dp_peer)

    go1(0)
    weights(0).start()
    go1(1)
    for h in range(2):
        recv1[h][s] = send1[h, s]

    locals_[2].wait()
    locals_[3].wait()
    for b in range(BLOCKS):
        rows = pl.ds(b * 128, 128)
        for j in range(2):
            ab0[j, b, pl.ds(0, 128)] = fv[rows, pl.ds(j * 256, 128)].astype(BF)
            ab0[j, b, pl.ds(128, 128)] = sv[rows, pl.ds(j * 256, 128)].astype(BF)
    enter(0)

    locals_[4].wait()
    for u in range(2):
        for j in range(2):
            src = j * 256 + u * 128
            for h in range(2):
                gq[h, u, :, pl.ds(j * 128, 128)] = gv[:, pl.ds(h * 512 + src, 128)]

    nt_dims = (((1,), (1,)), ((), ()))
    tn = (((0,), (0,)), ((), ()))
    locals_[5].wait()

    def grad_here(r, h):
        return lax.dot_general(
            av[:, pl.ds(r * 256, 256)], gq[h, 0], tn, preferred_element_type=F32) * (1.0 / 2048.0)

    for r in range(4):
        gsend0[pl.ds(r * 256, 256)] = grad_here(r, od).astype(BF)
        gown0[pl.ds(r * 256, 256)] = grad_here(r, d)
    gcopy0 = remote(gsend0, grecv0, xss.at[1], xrs.at[1], dp_peer)

    def wr1(h):
        def wait(k, _):
            p = sec(k)
            acopy(h, p, p).wait_recv()
            return 0

        lax.fori_loop(1, ns, wait, 0)

    def piece(h, sends, owner, device):
        rows = aold.at[pl.ds(pl.multiple_of(owner * 128 + h * 64, 64), 64)]
        return remote(rows, rows, ss2.at[h, sends], rs2.at[h, owner], device)

    up, down = ypeer(1), ypeer(3)

    def at_y(q):
        return (s, q * 2 + xl, d)

    for h in range(2):
        wr1(h)
        for b in range(BLOCKS):
            aold[pl.ds(pl.multiple_of(t * 128 + h * 64, 64), 64), pl.ds(b * 128, 128)] = recv1[h][tab[48 + b]]
        piece(h, 0, t, x_peer).start()
        piece(h, 1, t, at_y(up)).start()
        piece(h, 2, t, at_y(down)).start()
    round_a(0)
    for h in range(2):
        piece(h, 0, tx, x_peer).wait_recv()
        piece(h, 3, tx, at_y(up)).start()
        piece(h, 4, tx, at_y(down)).start()
        piece(h, 0, up * 2 + xl, x_peer).wait_recv()
        piece(h, 5, up * 2 + xl, at_y(down)).start()
    weights(1).start()
    for h in range(2):
        piece(h, 0, down * 2 + (1 - xl), x_peer).wait_recv()
        piece(h, 6, down * 2 + (1 - xl), at_y(up)).start()

    far = ypeer(2)
    for h in range(2):
        piece(h, 0, down * 2 + xl, x_peer).wait_recv()
        piece(h, 0, up * 2 + (1 - xl), x_peer).wait_recv()
        piece(h, 0, far * 2 + xl, x_peer).wait_recv()
        piece(h, 0, far * 2 + (1 - xl), x_peer).wait_recv()

    def grad_tile(r, h):
        return lax.dot_general(
            aold[:, pl.ds(r * 256, 256)], gq[h, 1], tn, preferred_element_type=F32) * (1.0 / 2048.0)

    for r in range(3):
        gsend[pl.ds(r * 256, 256)] = grad_tile(r, od).astype(BF)
    gcopy = remote(gsend, grecv, xss.at[2], xrs.at[2], dp_peer)
    gcopy.start()
    round_b(0)

    for h in range(2):
        weights(h).wait_recv()

    def proj_tile(i, _):
        a = aold[pl.ds(pl.multiple_of(i * 256, 256), 256)]
        for h in range(2):
            r = jnp.dot(a, wf[h], preferred_element_type=F32)
            cols = pl.ds(h * 512, 512)
            for j in range(2):
                lo, hi = r[j * 128:j * 128 + 64], r[j * 128 + 64:j * 128 + 128]
                pk[i * 2 + j, :, cols] = jnp.where(c == 0, hi, lo).astype(BF)
                pown[i * 2 + j, :, cols] = jnp.where(c == 0, lo, hi)
        return 0

    lax.fori_loop(0, 4, proj_tile, 0)
    ccopy = remote(pk, cp, xss.at[3], xrs.at[3], core_peer)
    ccopy.start()

    def hcopy(i, o):
        return remote(hgs.at[i], hgr.at[o], ssh.at[i], rsh.at[o], (s, i * 2 + xl, d))

    def hid(i):
        row = pl.multiple_of(i * 256, 256)
        r = lax.dot_general(gv[pl.ds(row, 256), pl.ds(0, 512)], wf[0], nt_dims, preferred_element_type=F32)
        return r + lax.dot_general(gv[pl.ds(row, 256), pl.ds(512, 512)], wf[1], nt_dims, preferred_element_type=F32)

    def hid_y(k, _):
        i = ypeer(k)
        r = hid(i).astype(BF)
        for x in range(2):
            hgs[i, x] = r[x * 128:(x + 1) * 128]
        hcopy(i, y).start()
        return 0

    lax.fori_loop(1, 4, hid_y, 0)
    r = hid(y)
    for x in range(2):
        hown[x] = r[x * 128:(x + 1) * 128]


    for r in range(3):
        gown[pl.ds(r * 256, 256)] = grad_tile(r, d)

    ccopy.wait_recv()

    lo, hi = pl.ds(0, 32), pl.ds(32, 32)

    def ring(n, way):
        rows = pl.ds(0, 64) if n > 1 else (lo if way == 0 else hi)
        return remote(
            qs.at[way, n - 1, rows], qr.at[way, n - 1, rows], ssq.at[way, n - 1], rsq.at[way, n - 1],
            (chip(1 if way == 0 else 7) * 2 + c, t, d))

    def partial_(p, rows):
        return pown[p, rows] + cp[p, rows].astype(F32)

    def ring_step(n):
        for way in range(2):
            p = chip(5 - n if way == 0 else n + 3)
            first_rows, other_rows = (lo, hi) if way == 0 else (hi, lo)
            if n > 1:
                ring(n - 1, way).wait_recv()
            if n == 1:
                qs[way, 0, first_rows] = partial_(p, first_rows).astype(BF)
            elif n == 2:
                qs[way, 1, first_rows] = (partial_(p, first_rows) + qr[way, 0, first_rows].astype(F32)).astype(BF)
                qs[way, 1, other_rows] = partial_(p, other_rows).astype(BF)
            else:
                qs[way, n - 1] = (partial_(p, pl.ds(0, 64)) + qr[way, n - 2].astype(F32)).astype(BF)
            ring(n, way).start()

    def adam():
        gcopy.wait_recv()
        for b in range(BLOCKS):
            rows = pl.ds(b * 128, 128)
            for j in range(2):
                cols = pl.ds(j * 256 + 128, 128)
                here = pl.ds(j * 128, 128)
                ab1[j, b] = step_of(fv[rows, cols], sv[rows, cols], gown[rows, here], grecv[rows, here])
        enter(1)

    def place_mine():
        back_copy(0).wait_recv()
        gcopy0.wait_recv()
        for k in range(RCAP):
            used = tab[40 + k].astype(F32)
            rows = pl.ds(k * 128, 128)
            for j in range(2):
                both = fa0[tab[80 + c * 8 + k]] if j == 0 else xr0[k]
                half = c if j == 0 else oc
                here = pl.ds(pl.multiple_of(half * 128, 128), 128)
                st = step_of(both[:128].astype(F32), both[128:].astype(F32), gown0[rows, here], grecv0[rows, here])
                step_out[k, :, pl.ds(pl.multiple_of(half * 256, 128), 128)] = (st.astype(F32) * used).astype(BF)

    def place(u):
        fa_, xr_ = parts[u][3], parts[u][7]
        back_copy(u).wait_recv()
        mine = pl.ds(pl.multiple_of(c * 256 + u * 128, 128), 128)
        theirs = pl.ds(pl.multiple_of(oc * 256 + u * 128, 128), 128)
        for k in range(RCAP):
            step_out[k, :, mine] = fa_[tab[80 + c * 8 + k]]
            step_out[k, :, theirs] = xr_[k]

    ring_step(1)
    adam()
    gcopy0.start()
    ring_step(2)
    round_a(1)
    ring_step(3)

    for k in range(1, 4):
        p = ypeer(k)
        hcopy(p, p).wait_recv()
    for x in range(2):
        total = hown[x]
        for k in range(1, 4):
            total = total + hgr[ypeer(k), x].astype(F32)
        hown[x] = total
    hxs[...] = hown[1 - xl].astype(BF)
    hx = remote(hxs, hxr, xss.at[4], xrs.at[4], x_peer)
    hx.start()
    ring_step(4)
    hx.wait_recv()
    hsum = hown[xl] + hxr[...].astype(F32)
    for b in range(BLOCKS):
        piece_ = hsum[:, b * 128:(b + 1) * 128].astype(BF)
        for j in range(2):
            ab2[j, b] = piece_[j * 64:(j + 1) * 64]
    enter(2)
    round_a(2)
    arrive(0)
    round_b(2)
    round_b(1)
    place_mine()
    arrive(2)

    back_copy(2).wait_recv()
    mine = pl.ds(pl.multiple_of(c * 64, 64), 64)
    theirs = pl.ds(pl.multiple_of(oc * 64, 64), 64)
    for k in range(RCAP):
        send5[k, mine] = fa2[tab[80 + c * 8 + k]]
        send5[k, theirs] = xr2[k]

    def fcopy(p, o):
        rows = pl.ds(pl.multiple_of(o * 128, 128), 128)
        return remote(send5.at[p], hgf.at[rows], ss5.at[p], rs5.at[o], (s, p, d))

    def go5(k, _):
        fcopy(ten(k), t).start()
        return 0

    lax.fori_loop(1, nt, go5, 0)
    hgf[pl.ds(trow, 128)] = send5[t]
    arrive(1)

    for way in range(2):
        ring(4, way).wait_recv()
    proj_out[...] = (partial_(z, pl.ds(0, 64)) + qr[0, 3].astype(F32) + qr[1, 3].astype(F32)).astype(BF)

    place(1)

    def wr5(k, _):
        p = ten(k)
        fcopy(p, p).wait_recv()
        return 0

    lax.fori_loop(1, nt, wr5, 0)
    hidden_out[...] = hgf[...]

    for u in range(3):
        drain(u)
    for cpy in (gcopy0, gcopy, ccopy, hx):
        cpy.wait_send()
    for h in range(2):
        weights(h).wait_send()
        for i in range(7):
            piece(h, i, t, x_peer).wait_send()

        def ws(k, _):
            acopy(h, sec(k), s).wait_send()
            return 0

        lax.fori_loop(1, ns, ws, 0)
    for k in range(1, 4):
        hcopy(ypeer(k), y).wait_send()
    for n in range(1, 5):
        for way in range(2):
            ring(n, way).wait_send()

    def ws5(k, _):
        fcopy(ten(k), t).wait_send()
        return 0

    lax.fori_loop(1, nt, ws5, 0)


def finish(proj, hidden, step, proj_out, hidden_out, step_out):
    proj_out[...] = proj[...]
    hidden_out[...] = hidden[...]
    for k in range(RCAP):
        step_out[pl.ds(k * 128, 128)] = step[k].astype(F32)


def shards(old_master, old_first, old_second, dest_section, dest_offset, hidden_acts, out_grad):
    any_ = pl.BlockSpec(memory_space=pl.ANY)
    smem = pl.BlockSpec(memory_space=pltpu.SMEM)
    vmem = pl.BlockSpec(memory_space=pltpu.VMEM)
    V = pltpu.VMEM
    dma = pltpu.SemaphoreType.DMA
    tab, ok = pl.pallas_call(
        plan,
        out_shape=(jax.ShapeDtypeStruct((128,), jnp.int32), jax.ShapeDtypeStruct((1,), jnp.int32)),
        in_specs=[smem, smem],
        out_specs=(smem, smem),
        scratch_shapes=[pltpu.SMEM((256,), jnp.int32), pltpu.SMEM((128,), jnp.int32)],
        name="plan",
    )(dest_section, dest_offset)
    out_shape = (
        jax.ShapeDtypeStruct((64, 1024), BF),
        jax.ShapeDtypeStruct((1024, 128), BF),
        jax.ShapeDtypeStruct((8, 128, 512), BF),
    )

    def call(body, scratch, number, name):
        return pl.pallas_call(
            body,
            out_shape=out_shape,
            in_specs=[smem, any_, any_, any_, any_, any_],
            out_specs=(vmem, vmem, vmem),
            scratch_shapes=scratch,
            compiler_params=pltpu.CompilerParams(
                collective_id=number, has_side_effects=True, vmem_limit_bytes=58 * 2**20),
            name=name,
        )

    padded = call(padded_kernel, [
        V((128, 1024), BF), V((8, 128, 128), BF), V((768, 512), F32), V((1024, 1024), BF), V((768, 512), F32), V((768, 512), F32),
        V((16, 128, 128), BF), V((16, 128, 128), BF), V((1024, 768), BF), V((2, 768, 512), BF),
        V((768, 512), BF), V((768, 512), BF), V((768, 512), F32),
        V((8, 64, 1024), BF), V((8, 64, 1024), F32), V((8, 64, 1024), BF), V((8, 64, 1024), BF), V((8, 64, 1024), BF),
        V((8, 128, 768), BF), V((8, 128, 768), BF), V((6, 128, 128), BF), V((16, 128, 128), BF), V((16, 128, 128), BF),
        V((8, 128, 128), BF), V((1024, 128), BF), V((6, 128, 512), BF), V((16, 128, 512), BF), V((16, 128, 512), BF),
        dma((5,)), dma((16,)), dma((16,)), dma((8,)), dma((8,)), dma((3,)), dma((3,)), dma((8,)), dma((8,)),
        dma((8,)), dma((8,)), dma((16,)), dma((16,)), dma((8,)), dma((8,)), dma((16,)), dma((16,)),
    ], 0, "padded")


    def buffers(rows):
        shapes = ((2, 6), (12,), (20,), (31,), (8,), (10,), (8,), (8,))
        return [V((*n, rows, 128), BF) for n in shapes]

    routed = call(routed_kernel, [
        V((128, 1024), BF), V((8, 128, 128), BF), V((768, 512), F32), V((1024, 1024), BF), V((768, 512), F32), V((768, 512), F32), V((1024, 1024), BF),
        V((2, 16, 64, 128), BF), V((16, 64, 128), BF), V((16, 64, 128), BF), V((1024, 768), BF), V((2, 768, 512), BF),
        V((2, 2, 1024, 256), BF), V((768, 256), BF), V((768, 256), BF), V((768, 256), F32),
        V((1024, 256), BF), V((1024, 256), BF), V((1024, 256), F32),
        V((8, 64, 1024), BF), V((8, 64, 1024), F32), V((8, 64, 1024), BF), V((2, 4, 64, 1024), BF), V((2, 4, 64, 1024), BF),
        V((4, 2, 128, 768), BF), V((4, 2, 128, 768), BF), V((128, 768), BF), V((128, 768), BF), V((2, 128, 768), F32),
        V((8, 128, 128), BF), V((1024, 128), BF),
        *buffers(256), *buffers(128), *buffers(64),
        dma((6,)), dma((2, 16)), dma((2, 16)), dma((2, 8)), dma((2, 8)), dma((7,)), dma((7,)), dma((2, 4)), dma((2, 4)),
        dma((4,)), dma((4,)), dma((8,)), dma((8,)), dma((3, 20)), dma((3, 20)),
    ], 1, "routed")

    args = (tab, old_master, old_first, old_second, hidden_acts[0], out_grad[0])
    proj, hidden, step = lax.cond(ok[0] == 1, routed, padded, *args)
    proj, hidden, step = pl.pallas_call(
        finish,
        out_shape=(
            jax.ShapeDtypeStruct((64, 1024), BF),
            jax.ShapeDtypeStruct((1024, 128), BF),
            jax.ShapeDtypeStruct((1024, 512), F32),
        ),
        in_specs=[vmem] * 3,
        out_specs=(vmem, vmem, vmem),
        compiler_params=pltpu.CompilerParams(vmem_limit_bytes=32 * 2**20),
        name="finish",
    )(proj, hidden, step)
    return proj[None], hidden[None], step


def solution(mesh):
    placed = (
        P("section", ("tensor", "dp")),
        P("section", ("tensor", "dp")),
        P("section", ("tensor", "dp")),
        P(),
        P(),
        P("dp", None, "section"),
        P("dp", None, "tensor"),
    )
    return jax.shard_map(
        shards,
        mesh=mesh,
        in_specs=placed,
        out_specs=(
            P("dp", "section", "tensor"),
            P("dp", None, ("section", "tensor")),
            P("section", ("tensor", "dp")),
        ),
        check_vma=False,
    )
```

```python
import jax
import jax.numpy as jnp
from jax import lax
from jax.experimental import pallas as pl
from jax.experimental.pallas import tpu as pltpu
from jax.sharding import PartitionSpec as P

ROWS = 128
BLOCKS = 6
RCAP = 8
CORR_SECOND = 0.6323045752
MESH = pl.DeviceIdType.MESH
BF = jnp.bfloat16
F32 = jnp.float32


def plan(dest, off, tab, ok, route, late):
    s = lax.axis_index("section")
    z = s // 2
    for i in range(112):
        tab[i] = 30 if 80 <= i < 96 else (8 if 64 <= i < 74 else 0)
    ok[0] = 1

    def clear(i, _):
        for j in range(16):
            route[i * 16 + j] = -1
        return 0

    lax.fori_loop(0, 12, clear, 0)

    def near(a, p):
        k = jnp.bitwise_and(p - a, 7)
        return (k == 1) | (k == 7)

    def rank(a, n):
        count = jnp.int32(0)
        for i in range(12):
            g = a * 12 + i
            o = a * 2 + i // 6
            q = dest[g]
            k = off[g]
            here = q == s
            tab[jnp.where(here, o, 112)] = k
            tab[jnp.where(here, 32 + k, 113)] = o
            tab[jnp.where(here, 40 + k, 114)] = 1
            p = lax.shift_right_logical(q, 1)
            r = jnp.bitwise_and(lax.shift_right_logical(count, p * 4), 15)
            count = count + lax.shift_left(jnp.int32(1), p * 4)
            fits = (r < 2) | ((r == 2) & near(a, p)) | (a == p)
            route[jnp.where(fits & (a != p), r * 64 + a * 8 + p, 192)] = g
            late[n] = g
            n = n + jnp.where(fits, 0, 1)
        return n

    n_late = lax.fori_loop(0, 8, rank, jnp.int32(0))
    for b in range(BLOCKS):
        p = dest[s * BLOCKS + b]
        tab[16 + p] = b
        tab[48 + b] = p

    def detour(i, _):
        g = late[i]
        a, p = g // 12, dest[g] // 2
        best = jnp.int32(-1)
        for k in (4, 3, 5, 2, 6, 1, 7):
            m = jnp.bitwise_and(p + k, 7)
            am, mp = a * 8 + m, m * 8 + p
            last = jnp.where(route[64 + mp] < 0, 1, 0)
            if k in (1, 7):
                last = jnp.where((last == 0) & (route[128 + mp] < 0), 2, last)
            held = route[am]
            direct = lax.shift_right_logical(dest[jnp.maximum(held, 0)], 1) == m
            second = jnp.where(route[64 + am] < 0, 1, jnp.where(near(a, m) & (route[128 + am] < 0), 2, 3))
            move = jnp.where(held < 0, 0, jnp.where(direct, second, 3))
            good = (last > 0) & (move < 3) & (m != a)
            best = jnp.where(good, m * 16 + last * 4 + move, best)

        @pl.when(best >= 0)
        def _():
            m = best // 16
            am = a * 8 + m
            move = jnp.bitwise_and(best, 3)
            last = jnp.bitwise_and(best // 4, 3)
            route[jnp.where(move > 0, move * 64 + am, 192)] = route[am]
            route[am] = g
            route[last * 64 + m * 8 + p] = g

        @pl.when(best < 0)
        def _():
            ok[0] = 0

        return 0

    lax.fori_loop(0, n_late, detour, 0)

    for m in range(8):
        g = route[z * 8 + m]
        tab[56 + m] = jnp.where((g >= 0) & (z != m), g - 12 * z, 0)
    for j in range(10):
        if j < 8:
            g = route[64 + z * 8 + j]
        else:
            g = route[128 + z * 8 + jnp.bitwise_and(z + (1 if j == 8 else 7), 7)]
        a = jnp.maximum(g, 0) // 12
        from_pool = 8 + g - 12 * z
        tab[64 + j] = jnp.where(g < 0, 8, jnp.where(a == z, from_pool, a))

    def final(g, source):
        h = jnp.maximum(g, 0)
        p = dest[h]
        mine = (g >= 0) & (lax.shift_right_logical(p, 1) == z)
        tab[jnp.where(mine, 80 + jnp.bitwise_and(p, 1) * 8 + off[h], 115)] = source

    for a in range(8):
        final(route[a * 8 + z], 8 + a)
        final(route[64 + a * 8 + z], a)
    final(route[128 + jnp.bitwise_and(z + 7, 7) * 8 + z], 28)
    final(route[128 + jnp.bitwise_and(z + 1, 7) * 8 + z], 29)
    for l in range(12):
        final(12 * z + l, 16 + l)


def padded_kernel(
    tab, master, first, second, acts, grads,
    proj_out, hidden_out, step_out,
    strip, blk, mv, gv, fv, sv,
    send1, recv1, aold, wf, gsend, grecv, gown, pk, pown, cp, q, rq,
    hgs, hgr, hb, send3, recv3, send5, hgf, ab, send4, recv4,
    lsem, ss1, rs1, ss2, rs2, xss, xrs, ssq, rsq, ssh, rsh, ss3, rs3, ss5, rs5, ss4, rs4,
):
    ns, nt = 16, 8
    s = lax.axis_index("section")
    t = lax.axis_index("tensor")
    d = lax.axis_index("dp")
    z, c = s // 2, s % 2
    od = 1 - d
    core_peer = (z * 2 + (1 - c), t, d)
    dp_peer = (s, t, od)

    def sec(k):
        return lax.rem(s + k, ns)

    def ten(k):
        return lax.rem(t + k, nt)

    trow = pl.multiple_of(t * 128, 128)
    locals_ = [
        pltpu.make_async_copy(acts.at[pl.ds(trow, 128)], strip, lsem.at[0]),
        pltpu.make_async_copy(master, mv, lsem.at[1]),
        pltpu.make_async_copy(grads, gv, lsem.at[2]),
        pltpu.make_async_copy(first, fv, lsem.at[3]),
        pltpu.make_async_copy(second, sv, lsem.at[4]),
    ]
    for cpy in locals_:
        cpy.start()

    bar = pltpu.get_barrier_semaphore()
    for k in range(1, ns):
        pl.semaphore_signal(bar, inc=1, device_id=(sec(k), t, d), device_id_type=MESH)
    for k in range(1, nt):
        pl.semaphore_signal(bar, inc=1, device_id=(s, ten(k), d), device_id_type=MESH)
    pl.semaphore_signal(bar, inc=1, device_id=dp_peer, device_id_type=MESH)

    slot_of = [tab[o] for o in range(ns)]
    block_for = [tab[16 + p] for p in range(ns)]
    owner_of = [tab[32 + k] for k in range(RCAP)]
    used = [tab[40 + k].astype(F32) for k in range(RCAP)]
    mine = [tab[48 + b] for b in range(BLOCKS)]

    locals_[0].wait()
    for k in range(RCAP):
        blk[k] = strip[:, pl.ds(k * 128, 128)]
    for o in range(ns):
        send1[o] = blk[slot_of[o]]
    locals_[1].wait()
    for b in range(BLOCKS):
        wf[d, pl.ds(b * 128, 128)] = mv[pl.ds(b * 128, 128)].astype(BF)

    pl.semaphore_wait(bar, ns - 1 + nt - 1 + 1)

    def to_sections(src, dst, sends, recvs):
        def copy(p):
            return pltpu.make_async_remote_copy(
                src_ref=src.at[p], dst_ref=dst.at[s],
                send_sem=sends.at[p], recv_sem=recvs.at[s],
                device_id=(p, t, d), device_id_type=MESH)

        def go(k, _):
            copy(sec(k)).start()
            return 0

        def wait_send(k, _):
            copy(sec(k)).wait_send()
            return 0

        def wait_recv(k, _):
            p = sec(k)
            pltpu.make_async_remote_copy(
                src_ref=src.at[p], dst_ref=dst.at[p],
                send_sem=sends.at[p], recv_sem=recvs.at[p],
                device_id=(p, t, d), device_id_type=MESH).wait_recv()
            return 0

        return (
            lambda: lax.fori_loop(1, ns, go, 0),
            lambda: lax.fori_loop(1, ns, wait_send, 0),
            lambda: lax.fori_loop(1, ns, wait_recv, 0),
        )

    go1, ws1, wr1 = to_sections(send1, recv1, ss1, rs1)
    go1()
    wcopy = pltpu.make_async_remote_copy(
        src_ref=wf.at[d], dst_ref=wf.at[d], send_sem=xss.at[0], recv_sem=xrs.at[0],
        device_id=dp_peer, device_id_type=MESH)
    wcopy.start()
    recv1[s] = send1[s]
    wr1()
    for b in range(BLOCKS):
        aold[pl.ds(trow, 128), pl.ds(b * 128, 128)] = recv1[mine[b]]

    def gather(p, q_):
        row = pl.multiple_of(q_ * 128, 128)
        return pltpu.make_async_remote_copy(
            src_ref=aold.at[pl.ds(row, 128)], dst_ref=aold.at[pl.ds(row, 128)],
            send_sem=ss2.at[p], recv_sem=rs2.at[q_],
            device_id=(s, p, d), device_id_type=MESH)

    def go2(k, _):
        gather(ten(k), t).start()
        return 0

    def wr2(k, _):
        p = ten(k)
        gather(p, p).wait_recv()
        return 0

    lax.fori_loop(1, nt, go2, 0)
    locals_[2].wait()
    lax.fori_loop(1, nt, wr2, 0)

    tn = (((0,), (0,)), ((), ()))
    nt_dims = (((1,), (1,)), ((), ()))

    def grad_tile(r, half):
        cols = pl.ds(pl.multiple_of(half * 512, 512), 512)
        return lax.dot_general(
            aold[:, pl.ds(r * 256, 256)], gv[:, cols], tn, preferred_element_type=F32
        ) * (1.0 / 2048.0)

    for r in range(3):
        gsend[pl.ds(r * 256, 256)] = grad_tile(r, od).astype(BF)
    gcopy = pltpu.make_async_remote_copy(
        src_ref=gsend, dst_ref=grecv, send_sem=xss.at[1], recv_sem=xrs.at[1],
        device_id=dp_peer, device_id_type=MESH)
    gcopy.start()

    wcopy.wait_recv()

    def proj_tile(i, _):
        row = pl.multiple_of(i * 128, 128)
        a = aold[pl.ds(row, 128)]
        for h in range(2):
            r = jnp.dot(a, wf[h], preferred_element_type=F32)
            cols = pl.ds(h * 512, 512)
            lo, hi = r[:64], r[64:]
            pk[i, :, cols] = jnp.where(c == 0, hi, lo).astype(BF)
            pown[i, :, cols] = jnp.where(c == 0, lo, hi)
        return 0

    lax.fori_loop(0, nt, proj_tile, 0)
    ccopy = pltpu.make_async_remote_copy(
        src_ref=pk, dst_ref=cp, send_sem=xss.at[2], recv_sem=xrs.at[2],
        device_id=core_peer, device_id_type=MESH)
    ccopy.start()

    def hid(i):
        row = pl.multiple_of(i * 128, 128)
        r = lax.dot_general(gv[pl.ds(row, 128), pl.ds(0, 512)], wf[0], nt_dims, preferred_element_type=F32)
        return r + lax.dot_general(gv[pl.ds(row, 128), pl.ds(512, 512)], wf[1], nt_dims, preferred_element_type=F32)

    def hcopy(p, q_):
        return pltpu.make_async_remote_copy(
            src_ref=hgs.at[p], dst_ref=hgr.at[q_], send_sem=ssh.at[p], recv_sem=rsh.at[q_],
            device_id=(s, p, d), device_id_type=MESH)

    def go_h(k, _):
        p = ten(k)
        hgs[p] = hid(p).astype(BF)
        hcopy(p, t).start()
        return 0

    lax.fori_loop(1, nt, go_h, 0)
    hown = hid(t)
    for b in range(BLOCKS):
        hgr[t, :, pl.ds(b * 128, 128)] = hown[:, b * 128:(b + 1) * 128].astype(BF)

    for r in range(3):
        gown[pl.ds(r * 256, 256)] = grad_tile(r, d)

    ccopy.wait_recv()

    def qcopy(p, q_):
        return pltpu.make_async_remote_copy(
            src_ref=q.at[p], dst_ref=rq.at[q_], send_sem=ssq.at[p], recv_sem=rsq.at[q_],
            device_id=(p * 2 + c, t, d), device_id_type=MESH)

    def go_q(k, _):
        p = lax.rem(z + k, 8)
        q[p] = (pown[p] + cp[p].astype(F32)).astype(BF)
        qcopy(p, z).start()
        return 0

    lax.fori_loop(1, 8, go_q, 0)
    rq[z] = (pown[z] + cp[z].astype(F32)).astype(BF)

    locals_[3].wait()
    locals_[4].wait()
    gcopy.wait_recv()
    for b in range(BLOCKS):
        rows = pl.ds(b * 128, 128)
        g = gown[rows] + grecv[rows].astype(F32)
        f1 = 0.9 * fv[rows] + 0.1 * g
        s1 = 0.999 * sv[rows] + 0.001 * g * g
        ab[b] = (f1 / (jnp.sqrt(s1 / CORR_SECOND) + 1e-08)).astype(BF)
    go4, ws4, wr4 = to_sections(send4, recv4, ss4, rs4)
    for p in range(ns):
        send4[p] = ab[block_for[p]]
    go4()
    recv4[s] = send4[s]

    def wr_h(k, _):
        p = ten(k)
        hcopy(p, p).wait_recv()
        return 0

    lax.fori_loop(1, nt, wr_h, 0)
    for b in range(BLOCKS):
        acc = hgr[0, :, pl.ds(b * 128, 128)].astype(F32)
        for p in range(1, nt):
            acc = acc + hgr[p, :, pl.ds(b * 128, 128)].astype(F32)
        hb[b] = acc.astype(BF)
    for p in range(ns):
        send3[p] = hb[block_for[p]]
    go3, ws3, wr3 = to_sections(send3, recv3, ss3, rs3)
    go3()
    recv3[s] = send3[s]
    wr3()
    for k in range(RCAP):
        send5[k] = (recv3[owner_of[k]].astype(F32) * used[k]).astype(BF)

    def fcopy(p, q_):
        row = pl.multiple_of(q_ * 128, 128)
        return pltpu.make_async_remote_copy(
            src_ref=send5.at[p], dst_ref=hgf.at[pl.ds(row, 128)], send_sem=ss5.at[p], recv_sem=rs5.at[q_],
            device_id=(s, p, d), device_id_type=MESH)

    def go5(k, _):
        fcopy(ten(k), t).start()
        return 0

    def wr5(k, _):
        p = ten(k)
        fcopy(p, p).wait_recv()
        return 0

    lax.fori_loop(1, nt, go5, 0)
    hgf[pl.ds(trow, 128)] = send5[t]

    def wr_q(k, _):
        p = lax.rem(z + k, 8)
        qcopy(p, p).wait_recv()
        return 0

    lax.fori_loop(1, 8, wr_q, 0)
    acc = rq[0].astype(F32)
    for p in range(1, 8):
        acc = acc + rq[p].astype(F32)
    proj_out[...] = acc.astype(BF)

    lax.fori_loop(1, nt, wr5, 0)
    hidden_out[...] = hgf[...]

    wr4()
    for k in range(RCAP):
        step_out[k] = (recv4[owner_of[k]].astype(F32) * used[k]).astype(BF)

    ws1()
    ws3()
    ws4()
    wcopy.wait_send()
    gcopy.wait_send()
    ccopy.wait_send()

    def ws_t(k, _):
        p = ten(k)
        gather(p, t).wait_send()
        hcopy(p, t).wait_send()
        fcopy(p, t).wait_send()
        return 0

    lax.fori_loop(1, nt, ws_t, 0)

    def ws_q(k, _):
        qcopy(lax.rem(z + k, 8), z).wait_send()
        return 0

    lax.fori_loop(1, 8, ws_q, 0)


def routed_kernel(
    tab, master, first, second, acts, grads,
    proj_out, hidden_out, step_out,
    strip, blk, mv, gv, fv, sv, av,
    send1, recv10, recv11, aold, wf, gq, gsend, grecv, gown, gsend0, grecv0, gown0, pk, pown, cp, qs, qr,
    hgs, hgr, hxs, hxr, hown, send5, hgf,
    ab0, pool0, xa0, fa0, sa0, sb0, xs0, xr0,
    ab1, pool1, xa1, fa1, sa1, sb1, xs1, xr1,
    ab2, pool2, xa2, fa2, sa2, sb2, xs2, xr2,
    lsem, ss1, rs1, ss2, rs2, xss, xrs, ssq, rsq, ssh, rsh, ss5, rs5, rss, rsr,
):
    ns, nt = 16, 8
    s = lax.axis_index("section")
    t = lax.axis_index("tensor")
    d = lax.axis_index("dp")
    z, c = s // 2, s % 2
    y, xl = t // 2, t % 2
    od, oc, tx = 1 - d, 1 - c, y * 2 + (1 - xl)
    core_peer = (z * 2 + oc, t, d)
    dp_peer = (s, t, od)
    x_peer = (s, tx, d)

    def sec(k):
        return lax.rem(s + k, ns)

    def ten(k):
        return lax.rem(t + k, nt)

    def ypeer(k):
        return lax.rem(y + k, 4)

    def chip(k):
        return lax.rem(z + k, 8)

    def remote(src, dst, sends, recvs, device):
        return pltpu.make_async_remote_copy(
            src_ref=src, dst_ref=dst, send_sem=sends, recv_sem=recvs,
            device_id=device, device_id_type=MESH)

    trow = pl.multiple_of(t * 128, 128)
    xrow = pl.multiple_of(tx * 128, 128)
    locals_ = [
        pltpu.make_async_copy(acts.at[pl.ds(trow, 128)], strip, lsem.at[0]),
        pltpu.make_async_copy(master, mv, lsem.at[1]),
        pltpu.make_async_copy(first, fv, lsem.at[3]),
        pltpu.make_async_copy(second, sv, lsem.at[4]),
        pltpu.make_async_copy(grads, gv, lsem.at[2]),
        pltpu.make_async_copy(acts, av, lsem.at[5]),
    ]
    for cpy in locals_:
        cpy.start()

    bar = pltpu.get_barrier_semaphore()
    for k in range(1, ns):
        pl.semaphore_signal(bar, inc=1, device_id=(sec(k), t, d), device_id_type=MESH)
    for k in range(1, nt):
        pl.semaphore_signal(bar, inc=1, device_id=(s, ten(k), d), device_id_type=MESH)
    pl.semaphore_signal(bar, inc=1, device_id=dp_peer, device_id_type=MESH)

    locals_[0].wait()
    for k in range(RCAP):
        blk[k] = strip[:, pl.ds(k * 128, 128)]
    for o in range(ns):
        both = blk[tab[o]]
        for h in range(2):
            send1[h, o] = both[h * 64:(h + 1) * 64]
    locals_[1].wait()
    for b in range(BLOCKS):
        wf[d, pl.ds(b * 128, 128)] = mv[pl.ds(b * 128, 128)].astype(BF)

    pl.semaphore_wait(bar, ns - 1 + nt - 1 + 1)

    parts = [
        (ab0, pool0, xa0, fa0, sa0, sb0, xs0, xr0),
        (ab1, pool1, xa1, fa1, sa1, sb1, xs1, xr1),
        (ab2, pool2, xa2, fa2, sa2, sb2, xs2, xr2),
    ]

    def swap_copy(u):
        ab_, pool_ = parts[u][:2]
        return remote(ab_.at[oc], pool_.at[pl.ds(c * BLOCKS, BLOCKS)], rss.at[u, 0], rsr.at[u, 0], core_peer)

    def enter(u):
        ab_, pool_ = parts[u][:2]
        swap_copy(u).start()
        for b in range(BLOCKS):
            pool_[c * BLOCKS + b] = ab_[c, b]

    def copy_a(u, p, o):
        return remote(parts[u][4].at[p], parts[u][2].at[o], rss.at[u, 1 + p], rsr.at[u, 1 + o], (p * 2 + c, t, d))

    def copy_b(u, p, o):
        return remote(parts[u][5].at[p], parts[u][3].at[o], rss.at[u, 9 + p], rsr.at[u, 9 + o], (p * 2 + c, t, d))

    def copy_n(u, j):
        p = chip(1 if j == 0 else 7)
        return remote(parts[u][5].at[8 + j], parts[u][3].at[28 + j], rss.at[u, 17 + j], rsr.at[u, 17 + j], (p * 2 + c, t, d))

    order = (4, 3, 5, 2, 6, 1, 7)

    def round_a(u):
        _, pool_, xa_, _, sa_, _, _, _ = parts[u]
        swap_copy(u).wait_recv()
        for k in order:
            m = chip(k)
            sa_[m] = pool_[tab[56 + m]]
            copy_a(u, m, z).start()
        for l in range(12):
            xa_[8 + l] = pool_[l]
        xa_[z] = jnp.zeros(xa_.shape[1:], BF)

    def round_b(u):
        _, pool_, xa_, fa_, _, sb_, _, _ = parts[u]
        for k in order:
            m = chip(k)
            copy_a(u, m, m).wait_recv()
        for k in order:
            m = chip(k)
            sb_[m] = xa_[tab[64 + m]]
            copy_b(u, m, z).start()
        for j in range(2):
            sb_[8 + j] = xa_[tab[72 + j]]
            copy_n(u, j).start()
        for l in range(20):
            fa_[8 + l] = xa_[l]
        fa_[z] = jnp.zeros(fa_.shape[1:], BF)
        fa_[30] = jnp.zeros(fa_.shape[1:], BF)

    def back_copy(u):
        return remote(parts[u][6], parts[u][7], rss.at[u, 19], rsr.at[u, 19], core_peer)

    def arrive(u):
        _, _, _, fa_, _, _, xs_, _ = parts[u]
        for k in order:
            m = chip(k)
            copy_b(u, m, m).wait_recv()
        for j in range(2):
            copy_n(u, j).wait_recv()
        for k in range(RCAP):
            xs_[k] = fa_[tab[80 + oc * 8 + k]]
        back_copy(u).start()

    def drain(u):
        swap_copy(u).wait_send()
        back_copy(u).wait_send()
        for k in order:
            copy_a(u, chip(k), z).wait_send()
            copy_b(u, chip(k), z).wait_send()
        for j in range(2):
            copy_n(u, j).wait_send()

    def step_of(f0, s0, own, other):
        g = own + other.astype(F32)
        f1 = 0.9 * f0 + 0.1 * g
        s1 = 0.999 * s0 + 0.001 * g * g
        return (f1 / (jnp.sqrt(s1 / CORR_SECOND) + 1e-08)).astype(BF)

    recv1 = (recv10, recv11)

    def acopy(h, p, o):
        return remote(send1.at[h, p], recv1[h].at[o], ss1.at[h, p], rs1.at[h, o], (p, t, d))

    def go1(h):
        for k in (4, 3, 5, 2, 6, 1, 7):
            for e in (c, oc):
                acopy(h, chip(k) * 2 + e, s).start()
        acopy(h, z * 2 + oc, s).start()

    def weights(h):
        rows = wf.at[d, pl.ds(h * 384, 384)]
        return remote(rows, rows, xss.at[5 + h], xrs.at[5 + h], dp_peer)

    go1(0)
    weights(0).start()
    go1(1)
    for h in range(2):
        recv1[h][s] = send1[h, s]

    locals_[2].wait()
    locals_[3].wait()
    for b in range(BLOCKS):
        rows = pl.ds(b * 128, 128)
        for j in range(2):
            ab0[j, b, pl.ds(0, 128)] = fv[rows, pl.ds(j * 256, 128)].astype(BF)
            ab0[j, b, pl.ds(128, 128)] = sv[rows, pl.ds(j * 256, 128)].astype(BF)
    enter(0)

    locals_[4].wait()
    for u in range(2):
        for j in range(2):
            src = j * 256 + u * 128
            for h in range(2):
                gq[h, u, :, pl.ds(j * 128, 128)] = gv[:, pl.ds(h * 512 + src, 128)]

    nt_dims = (((1,), (1,)), ((), ()))
    tn = (((0,), (0,)), ((), ()))
    locals_[5].wait()

    def grad_here(r, h):
        return lax.dot_general(
            av[:, pl.ds(r * 256, 256)], gq[h, 0], tn, preferred_element_type=F32) * (1.0 / 2048.0)

    for r in range(4):
        gsend0[pl.ds(r * 256, 256)] = grad_here(r, od).astype(BF)
        gown0[pl.ds(r * 256, 256)] = grad_here(r, d)
    gcopy0 = remote(gsend0, grecv0, xss.at[1], xrs.at[1], dp_peer)

    def wr1(h):
        def wait(k, _):
            p = sec(k)
            acopy(h, p, p).wait_recv()
            return 0

        lax.fori_loop(1, ns, wait, 0)

    def piece(h, sends, owner, device):
        rows = aold.at[pl.ds(pl.multiple_of(owner * 128 + h * 64, 64), 64)]
        return remote(rows, rows, ss2.at[h, sends], rs2.at[h, owner], device)

    up, down = ypeer(1), ypeer(3)

    def at_y(q):
        return (s, q * 2 + xl, d)

    for h in range(2):
        wr1(h)
        for b in range(BLOCKS):
            aold[pl.ds(pl.multiple_of(t * 128 + h * 64, 64), 64), pl.ds(b * 128, 128)] = recv1[h][tab[48 + b]]
        piece(h, 0, t, x_peer).start()
        piece(h, 1, t, at_y(up)).start()
        piece(h, 2, t, at_y(down)).start()
    round_a(0)
    for h in range(2):
        piece(h, 0, tx, x_peer).wait_recv()
        piece(h, 3, tx, at_y(up)).start()
        piece(h, 4, tx, at_y(down)).start()
        piece(h, 0, up * 2 + xl, x_peer).wait_recv()
        piece(h, 5, up * 2 + xl, at_y(down)).start()
    weights(1).start()
    for h in range(2):
        piece(h, 0, down * 2 + (1 - xl), x_peer).wait_recv()
        piece(h, 6, down * 2 + (1 - xl), at_y(up)).start()

    far = ypeer(2)
    for h in range(2):
        piece(h, 0, down * 2 + xl, x_peer).wait_recv()
        piece(h, 0, up * 2 + (1 - xl), x_peer).wait_recv()
        piece(h, 0, far * 2 + xl, x_peer).wait_recv()
        piece(h, 0, far * 2 + (1 - xl), x_peer).wait_recv()

    def grad_tile(r, h):
        return lax.dot_general(
            aold[:, pl.ds(r * 256, 256)], gq[h, 1], tn, preferred_element_type=F32) * (1.0 / 2048.0)

    for r in range(3):
        gsend[pl.ds(r * 256, 256)] = grad_tile(r, od).astype(BF)
    gcopy = remote(gsend, grecv, xss.at[2], xrs.at[2], dp_peer)
    gcopy.start()
    round_b(0)

    for h in range(2):
        weights(h).wait_recv()

    def proj_tile(i, _):
        a = aold[pl.ds(pl.multiple_of(i * 256, 256), 256)]
        for h in range(2):
            r = jnp.dot(a, wf[h], preferred_element_type=F32)
            cols = pl.ds(h * 512, 512)
            for j in range(2):
                lo, hi = r[j * 128:j * 128 + 64], r[j * 128 + 64:j * 128 + 128]
                pk[i * 2 + j, :, cols] = jnp.where(c == 0, hi, lo).astype(BF)
                pown[i * 2 + j, :, cols] = jnp.where(c == 0, lo, hi)
        return 0

    lax.fori_loop(0, 4, proj_tile, 0)
    ccopy = remote(pk, cp, xss.at[3], xrs.at[3], core_peer)
    ccopy.start()

    def hcopy(i, o):
        return remote(hgs.at[i], hgr.at[o], ssh.at[i], rsh.at[o], (s, i * 2 + xl, d))

    def hid(i):
        row = pl.multiple_of(i * 256, 256)
        r = lax.dot_general(gv[pl.ds(row, 256), pl.ds(0, 512)], wf[0], nt_dims, preferred_element_type=F32)
        return r + lax.dot_general(gv[pl.ds(row, 256), pl.ds(512, 512)], wf[1], nt_dims, preferred_element_type=F32)

    def hid_y(k, _):
        i = ypeer(k)
        r = hid(i).astype(BF)
        for x in range(2):
            hgs[i, x] = r[x * 128:(x + 1) * 128]
        hcopy(i, y).start()
        return 0

    lax.fori_loop(1, 4, hid_y, 0)
    r = hid(y)
    for x in range(2):
        hown[x] = r[x * 128:(x + 1) * 128]


    for r in range(3):
        gown[pl.ds(r * 256, 256)] = grad_tile(r, d)

    ccopy.wait_recv()

    lo, hi = pl.ds(0, 32), pl.ds(32, 32)

    def ring(n, way):
        rows = pl.ds(0, 64) if n > 1 else (lo if way == 0 else hi)
        return remote(
            qs.at[way, n - 1, rows], qr.at[way, n - 1, rows], ssq.at[way, n - 1], rsq.at[way, n - 1],
            (chip(1 if way == 0 else 7) * 2 + c, t, d))

    def partial_(p, rows):
        return pown[p, rows] + cp[p, rows].astype(F32)

    def ring_step(n):
        for way in range(2):
            p = chip(5 - n if way == 0 else n + 3)
            first_rows, other_rows = (lo, hi) if way == 0 else (hi, lo)
            if n > 1:
                ring(n - 1, way).wait_recv()
            if n == 1:
                qs[way, 0, first_rows] = partial_(p, first_rows).astype(BF)
            elif n == 2:
                qs[way, 1, first_rows] = (partial_(p, first_rows) + qr[way, 0, first_rows].astype(F32)).astype(BF)
                qs[way, 1, other_rows] = partial_(p, other_rows).astype(BF)
            else:
                qs[way, n - 1] = (partial_(p, pl.ds(0, 64)) + qr[way, n - 2].astype(F32)).astype(BF)
            ring(n, way).start()

    def adam():
        gcopy.wait_recv()
        for b in range(BLOCKS):
            rows = pl.ds(b * 128, 128)
            for j in range(2):
                cols = pl.ds(j * 256 + 128, 128)
                here = pl.ds(j * 128, 128)
                ab1[j, b] = step_of(fv[rows, cols], sv[rows, cols], gown[rows, here], grecv[rows, here])
        enter(1)

    def place_mine():
        back_copy(0).wait_recv()
        gcopy0.wait_recv()
        for k in range(RCAP):
            used = tab[40 + k].astype(F32)
            rows = pl.ds(k * 128, 128)
            for j in range(2):
                both = fa0[tab[80 + c * 8 + k]] if j == 0 else xr0[k]
                half = c if j == 0 else oc
                here = pl.ds(pl.multiple_of(half * 128, 128), 128)
                st = step_of(both[:128].astype(F32), both[128:].astype(F32), gown0[rows, here], grecv0[rows, here])
                step_out[k, :, pl.ds(pl.multiple_of(half * 256, 128), 128)] = (st.astype(F32) * used).astype(BF)

    def place(u):
        fa_, xr_ = parts[u][3], parts[u][7]
        back_copy(u).wait_recv()
        mine = pl.ds(pl.multiple_of(c * 256 + u * 128, 128), 128)
        theirs = pl.ds(pl.multiple_of(oc * 256 + u * 128, 128), 128)
        for k in range(RCAP):
            step_out[k, :, mine] = fa_[tab[80 + c * 8 + k]]
            step_out[k, :, theirs] = xr_[k]

    ring_step(1)
    adam()
    gcopy0.start()
    ring_step(2)
    round_a(1)
    ring_step(3)

    for k in range(1, 4):
        p = ypeer(k)
        hcopy(p, p).wait_recv()
    for x in range(2):
        total = hown[x]
        for k in range(1, 4):
            total = total + hgr[ypeer(k), x].astype(F32)
        hown[x] = total
    hxs[...] = hown[1 - xl].astype(BF)
    hx = remote(hxs, hxr, xss.at[4], xrs.at[4], x_peer)
    hx.start()
    ring_step(4)
    hx.wait_recv()
    hsum = hown[xl] + hxr[...].astype(F32)
    for b in range(BLOCKS):
        piece_ = hsum[:, b * 128:(b + 1) * 128].astype(BF)
        for j in range(2):
            ab2[j, b] = piece_[j * 64:(j + 1) * 64]
    enter(2)
    round_a(2)
    round_b(2)
    round_b(1)
    arrive(0)
    arrive(2)

    back_copy(2).wait_recv()
    mine = pl.ds(pl.multiple_of(c * 64, 64), 64)
    theirs = pl.ds(pl.multiple_of(oc * 64, 64), 64)
    for k in range(RCAP):
        send5[k, mine] = fa2[tab[80 + c * 8 + k]]
        send5[k, theirs] = xr2[k]

    def fcopy(p, o):
        rows = pl.ds(pl.multiple_of(o * 128, 128), 128)
        return remote(send5.at[p], hgf.at[rows], ss5.at[p], rs5.at[o], (s, p, d))

    def go5(k, _):
        fcopy(ten(k), t).start()
        return 0

    lax.fori_loop(1, nt, go5, 0)
    hgf[pl.ds(trow, 128)] = send5[t]
    place_mine()
    arrive(1)

    for way in range(2):
        ring(4, way).wait_recv()
    proj_out[...] = (partial_(z, pl.ds(0, 64)) + qr[0, 3].astype(F32) + qr[1, 3].astype(F32)).astype(BF)

    place(1)

    def wr5(k, _):
        p = ten(k)
        fcopy(p, p).wait_recv()
        return 0

    lax.fori_loop(1, nt, wr5, 0)
    hidden_out[...] = hgf[...]

    for u in range(3):
        drain(u)
    for cpy in (gcopy0, gcopy, ccopy, hx):
        cpy.wait_send()
    for h in range(2):
        weights(h).wait_send()
        for i in range(7):
            piece(h, i, t, x_peer).wait_send()

        def ws(k, _):
            acopy(h, sec(k), s).wait_send()
            return 0

        lax.fori_loop(1, ns, ws, 0)
    for k in range(1, 4):
        hcopy(ypeer(k), y).wait_send()
    for n in range(1, 5):
        for way in range(2):
            ring(n, way).wait_send()

    def ws5(k, _):
        fcopy(ten(k), t).wait_send()
        return 0

    lax.fori_loop(1, nt, ws5, 0)


def finish(proj, hidden, step, proj_out, hidden_out, step_out):
    proj_out[...] = proj[...]
    hidden_out[...] = hidden[...]
    for k in range(RCAP):
        step_out[pl.ds(k * 128, 128)] = step[k].astype(F32)


def shards(old_master, old_first, old_second, dest_section, dest_offset, hidden_acts, out_grad):
    any_ = pl.BlockSpec(memory_space=pl.ANY)
    smem = pl.BlockSpec(memory_space=pltpu.SMEM)
    vmem = pl.BlockSpec(memory_space=pltpu.VMEM)
    V = pltpu.VMEM
    dma = pltpu.SemaphoreType.DMA
    tab, ok = pl.pallas_call(
        plan,
        out_shape=(jax.ShapeDtypeStruct((128,), jnp.int32), jax.ShapeDtypeStruct((1,), jnp.int32)),
        in_specs=[smem, smem],
        out_specs=(smem, smem),
        scratch_shapes=[pltpu.SMEM((256,), jnp.int32), pltpu.SMEM((128,), jnp.int32)],
        name="plan",
    )(dest_section, dest_offset)
    out_shape = (
        jax.ShapeDtypeStruct((64, 1024), BF),
        jax.ShapeDtypeStruct((1024, 128), BF),
        jax.ShapeDtypeStruct((8, 128, 512), BF),
    )

    def call(body, scratch, number, name):
        return pl.pallas_call(
            body,
            out_shape=out_shape,
            in_specs=[smem, any_, any_, any_, any_, any_],
            out_specs=(vmem, vmem, vmem),
            scratch_shapes=scratch,
            compiler_params=pltpu.CompilerParams(
                collective_id=number, has_side_effects=True, vmem_limit_bytes=58 * 2**20),
            name=name,
        )

    padded = call(padded_kernel, [
        V((128, 1024), BF), V((8, 128, 128), BF), V((768, 512), F32), V((1024, 1024), BF), V((768, 512), F32), V((768, 512), F32),
        V((16, 128, 128), BF), V((16, 128, 128), BF), V((1024, 768), BF), V((2, 768, 512), BF),
        V((768, 512), BF), V((768, 512), BF), V((768, 512), F32),
        V((8, 64, 1024), BF), V((8, 64, 1024), F32), V((8, 64, 1024), BF), V((8, 64, 1024), BF), V((8, 64, 1024), BF),
        V((8, 128, 768), BF), V((8, 128, 768), BF), V((6, 128, 128), BF), V((16, 128, 128), BF), V((16, 128, 128), BF),
        V((8, 128, 128), BF), V((1024, 128), BF), V((6, 128, 512), BF), V((16, 128, 512), BF), V((16, 128, 512), BF),
        dma((5,)), dma((16,)), dma((16,)), dma((8,)), dma((8,)), dma((3,)), dma((3,)), dma((8,)), dma((8,)),
        dma((8,)), dma((8,)), dma((16,)), dma((16,)), dma((8,)), dma((8,)), dma((16,)), dma((16,)),
    ], 0, "padded")


    def buffers(rows):
        shapes = ((2, 6), (12,), (20,), (31,), (8,), (10,), (8,), (8,))
        return [V((*n, rows, 128), BF) for n in shapes]

    routed = call(routed_kernel, [
        V((128, 1024), BF), V((8, 128, 128), BF), V((768, 512), F32), V((1024, 1024), BF), V((768, 512), F32), V((768, 512), F32), V((1024, 1024), BF),
        V((2, 16, 64, 128), BF), V((16, 64, 128), BF), V((16, 64, 128), BF), V((1024, 768), BF), V((2, 768, 512), BF),
        V((2, 2, 1024, 256), BF), V((768, 256), BF), V((768, 256), BF), V((768, 256), F32),
        V((1024, 256), BF), V((1024, 256), BF), V((1024, 256), F32),
        V((8, 64, 1024), BF), V((8, 64, 1024), F32), V((8, 64, 1024), BF), V((2, 4, 64, 1024), BF), V((2, 4, 64, 1024), BF),
        V((4, 2, 128, 768), BF), V((4, 2, 128, 768), BF), V((128, 768), BF), V((128, 768), BF), V((2, 128, 768), F32),
        V((8, 128, 128), BF), V((1024, 128), BF),
        *buffers(256), *buffers(128), *buffers(64),
        dma((6,)), dma((2, 16)), dma((2, 16)), dma((2, 8)), dma((2, 8)), dma((7,)), dma((7,)), dma((2, 4)), dma((2, 4)),
        dma((4,)), dma((4,)), dma((8,)), dma((8,)), dma((3, 20)), dma((3, 20)),
    ], 1, "routed")

    args = (tab, old_master, old_first, old_second, hidden_acts[0], out_grad[0])
    proj, hidden, step = lax.cond(ok[0] == 1, routed, padded, *args)
    proj, hidden, step = pl.pallas_call(
        finish,
        out_shape=(
            jax.ShapeDtypeStruct((64, 1024), BF),
            jax.ShapeDtypeStruct((1024, 128), BF),
            jax.ShapeDtypeStruct((1024, 512), F32),
        ),
        in_specs=[vmem] * 3,
        out_specs=(vmem, vmem, vmem),
        compiler_params=pltpu.CompilerParams(vmem_limit_bytes=32 * 2**20),
        name="finish",
    )(proj, hidden, step)
    return proj[None], hidden[None], step


def solution(mesh):
    placed = (
        P("section", ("tensor", "dp")),
        P("section", ("tensor", "dp")),
        P("section", ("tensor", "dp")),
        P(),
        P(),
        P("dp", None, "section"),
        P("dp", None, "tensor"),
    )
    return jax.shard_map(
        shards,
        mesh=mesh,
        in_specs=placed,
        out_specs=(
            P("dp", "section", "tensor"),
            P("dp", None, ("section", "tensor")),
            P("section", ("tensor", "dp")),
        ),
        check_vma=False,
    )
```
